256 devices in a mesh: gx: 16 (over z, core), gy: 4 (over x), gz: 4 (over y).
Axes of the slice: x: 4, y: 4, z: 8, core: 2. Of those that a mesh axis runs over, the one named last changes fastest.
Arguments:
- velocity: float32 [3, 256, 192, 512], P(None, 'gx', 'gz', 'gy'), may hold values from 0.5 to 1.5
- pressure: float32 [256, 192, 512], P('gx', 'gz', 'gy'), may hold values from -3 to 3
- kernel: float32 [65536, 128], P(('gx', 'gy', 'gz')), may hold values from 0.1 to 1
- owners: int32 [65536, 1], P(('gx', 'gy', 'gz')), may hold values from 0 to 63; in each aligned block of 256 rows (0 to 255, 256 to 511, ...) at most 8 rows name the same one
- lines: int32 [65536], P(('gx', 'gy', 'gz')), may hold values from 0 to 767
- point_turbine: int32 [65536], P(('gx', 'gy', 'gz')), may hold values from 0 to 47
- row_counts: int32 [16, 4, 4], P('gx', 'gy', 'gz'), may hold values from 128 to 256
- thrust: float32 [48], replicated, may hold values from 0.4 to 1
- inflow_x: int32 [48], replicated, may hold values from 0 to 255
- inflow_y: int32 [48], replicated, may hold values from 0 to 480
Outputs:
- velocity_out: float32 [3, 256, 192, 512], P(None, 'gx', 'gz', 'gy')
- pressure_out: float32 [256, 192, 512], P('gx', 'gz', 'gy')
The draws below stay inside these ranges and needn't reach their ends.
Inputs may be any that keep to these rules, and one draw needn't show every extreme that they name: `owners`: among the rows of one device no horizontal block is named by more than 8 rows, and in every draw some device names one block exactly 8 times.
All inputs are finite; a program needn't handle non-finite values.
Results may differ from the reference program's by a relative error of at most 0.00011.
Values sent between devices are 32-bit elements; how exact they have to be, the bound alone decides.
A program may use at most 64 MiB of HBM per device.

```python
import math
import jax
import jax.numpy as jnp
import numpy as np

CX = 16
CZ = 48
KERN = 128
ROWS_DEV = 256
TURB = 48
BAND = 32
STEPS = 2
SWEEPS = 8
CY = 128
NX = 256
NY = 512
NZ = 192
ROWS = 65536
CAP = 8
N_GX = 16
N_GY = 4
N_GZ = 4


def set_ends(drawn, rng, least, largest):
    longest = drawn.shape.index(max(drawn.shape))
    spots = []
    for shift in (0, 1):
        where = [jax.random.randint(jax.random.fold_in(rng, axis), (), 0, length) for axis, length in enumerate(drawn.shape)]
        where[longest] = (where[longest] + shift) % drawn.shape[longest]
        spots.append(tuple(where))
    return drawn.at[spots[0]].set(least).at[spots[1]].set(largest)


def level_of(stream_key, shape, split, low, top_value):
    gain, own = 1.0, jax.random.fold_in(stream_key, 6)
    for dim, parts in split:
        draws = jnp.exp(jax.random.uniform(jax.random.fold_in(own, dim), (parts,), jnp.float32, low / len(split), top_value / len(split)))
        gain = gain * jnp.repeat(draws, shape[dim] // parts).reshape([-1 if axis == dim else 1 for axis in range(len(shape))])
    return gain


def routed_block(rng, own, number, rows, number_of, top, reach, skew):
    sequence = jax.random.permutation(rng, number_of)
    crowded, ordinary = portions_of(number_of, rows * top, reach, skew, True), portions_of(number_of, rows * top, reach, skew, False)
    places = jnp.arange(number_of)

    def named(sizes, rotation):
        used = int((sizes > 0).sum())
        fixed = max(1, used // 4)
        moved = fixed + (places - fixed + rotation * (used - fixed)) % max(1, number_of - fixed)
        return jnp.zeros((number_of,), jnp.int32).at[sequence[jnp.where(places < fixed, places, moved)]].set(jnp.asarray(sizes, jnp.int32))

    sizes = jnp.where(number % 4 == 0, named(crowded, number // 4), named(ordinary, number - number // 4 - 1))
    mixed = jax.random.permutation(jax.random.fold_in(own, 3), number_of)
    giver, receiver = mixed[0:number_of // 2 * 2:2], mixed[1:number_of // 2 * 2:2]
    slack = jnp.minimum(sizes[giver] - 1, reach - sizes[receiver]) // 2
    slack = jnp.where((giver == sequence[0]) | (receiver == sequence[0]) | (sizes[receiver] == 0), 0, jnp.maximum(slack, 0))
    moved = jax.random.randint(jax.random.fold_in(own, 4), (number_of // 2,), 0, 1 << 20) % (slack + 1)
    sizes = sizes.at[giver].add(-moved).at[receiver].add(moved)
    labels = jnp.searchsorted(jnp.cumsum(sizes), jnp.arange(rows * top), side="right").astype(jnp.int32)
    table = labels.reshape(top, rows).T
    table = table[jax.random.permutation(jax.random.fold_in(own, 1), rows)]
    rotation = jax.random.randint(jax.random.fold_in(own, 2), (rows, 1), 0, top)
    return jnp.take_along_axis(table, (jnp.arange(top)[None, :] + rotation) % top, axis=1)


def portions_of(number_of, total, bound, slope, full):
    portions = [(1 << 20) // math.isqrt(grade ** slope) + 1 for grade in range(1, number_of + 1)]
    largest = bound if full else min(bound, max(-(-total // number_of), total * portions[0] // sum(portions)))
    least = 1 if total - largest >= number_of - 1 else 0
    holding, surplus = [largest] + [least] * (number_of - 1), total - largest - least * (number_of - 1)
    while surplus > 0:
        free = [i for i in range(1, number_of) if holding[i] < largest] or [i for i in range(1, number_of) if holding[i] < bound]
        whole, remaining = sum([portions[i] for i in free]), surplus
        for i in free:
            extra = min(bound - holding[i], max(1, remaining * portions[i] // whole), surplus)
            holding[i] = holding[i] + extra
            surplus = surplus - extra
    return np.array(holding)


def noise(own_key, shape, spread, most, split=(), kind=jnp.bfloat16):
    drawn = spread * jax.random.normal(own_key, shape, jnp.float32)
    if split:
        drawn = drawn * level_of(own_key, shape, split, -0.22, 0.18)
    return jnp.clip(drawn, -most, most).astype(kind)


def setup_inputs(seed: int = 0) -> dict:
    splits = jax.random.split(jax.random.key(seed), 11)
    velocity = jnp.clip(0.5 + 1.0 * jax.random.uniform(splits[0], (3, NX, NZ, NY), jnp.float32) ** level_of(splits[0], (3, NX, NZ, NY), ((1, 16), (2, 4), (3, 4)), -0.2, 0.2), 0.5, 1.5)
    pressure = noise(splits[1], (NX, NZ, NY), 0.5, 3.0, ((0, 16), (1, 4), (2, 4)), jnp.float32)
    kernel = jnp.clip(jnp.exp(math.log(1.0) - 2.3025851 * jax.random.uniform(splits[2], (ROWS, KERN), jnp.float32) ** level_of(splits[2], (ROWS, KERN), ((0, 256),), -0.2, 0.2)), 0.1, 1.0)
    owners_keys = jax.random.split(jax.random.fold_in(splits[3], 1), ROWS // ROWS_DEV)
    owners_turns = jax.random.permutation(jax.random.fold_in(splits[3], 3), ROWS // ROWS_DEV)
    owners = jax.vmap(lambda own, number: routed_block(jax.random.fold_in(splits[3], 2), own, number, ROWS_DEV, N_GX * N_GY, 1, CAP, 2))(owners_keys, owners_turns).reshape((ROWS, 1))
    lines = set_ends(jax.random.randint(splits[4], (ROWS,), 0, CX * CZ), jax.random.fold_in(splits[4], 1), 0, (CX * CZ) - 1).astype(jnp.int32)
    point_turbine = set_ends(jax.random.randint(splits[5], (ROWS,), 0, TURB), jax.random.fold_in(splits[5], 1), 0, TURB - 1).astype(jnp.int32)
    row_counts = set_ends(jax.random.randint(splits[6], (N_GX, N_GY, N_GZ), ROWS_DEV // 2, ROWS_DEV + 1), jax.random.fold_in(splits[6], 1), ROWS_DEV // 2, ROWS_DEV).astype(jnp.int32)
    thrust = jnp.clip(jax.random.uniform(splits[7], (TURB,), jnp.float32, 0.4, 1.0), 0.4, 1.0)
    inflow_x = set_ends(jax.random.randint(splits[8], (TURB,), 0, NX), jax.random.fold_in(splits[8], 1), 0, NX - 1).astype(jnp.int32)
    inflow_y = set_ends(jax.random.randint(splits[9], (TURB,), 0, NY - BAND + 1), jax.random.fold_in(splits[9], 1), 0, NY - BAND).astype(jnp.int32)
    return dict(velocity=velocity, pressure=pressure, kernel=kernel, owners=owners, lines=lines, point_turbine=point_turbine, row_counts=row_counts, thrust=thrust, inflow_x=inflow_x, inflow_y=inflow_y)


def neighbours(padded):
    total = padded[..., 2:, 1:-1, 1:-1] + padded[..., :-2, 1:-1, 1:-1]
    total = total + padded[..., 1:-1, 2:, 1:-1] + padded[..., 1:-1, :-2, 1:-1]
    total = total + padded[..., 1:-1, 1:-1, 2:] + padded[..., 1:-1, 1:-1, :-2]
    return total


def pad_cells(field):
    widths = [(0, 0)] * (field.ndim - 3) + [(1, 1), (1, 1), (1, 1)]
    return jnp.pad(field, widths)


def reference(velocity, pressure, kernel, owners, lines, point_turbine, row_counts, thrust, inflow_x, inflow_y):
    time_step = 0.4
    viscosity = 0.05
    row_ids = jnp.arange(ROWS)
    device_ids = row_ids // ROWS_DEV
    counts_flat = row_counts.reshape(-1)
    valid = ((row_ids % ROWS_DEV) < counts_flat[device_ids]).astype(jnp.float32)
    index_z = device_ids % N_GZ
    target = owners[:, 0]
    block_x = target // N_GY
    block_y = target % N_GY
    line_x = lines // CZ
    line_z = lines % CZ
    ypos = jnp.arange(NY)
    band = ((ypos[None, :] >= inflow_y[:, None]) & (ypos[None, :] < inflow_y[:, None] + BAND)).astype(jnp.float32)
    field = velocity
    press = pressure
    for repeat in range(STEPS):
        plane = field[0][inflow_x]
        uref = jnp.sum(plane * band[:, None, :], axis=(1, 2)) / (BAND * NZ)
        magnitude = 0.5 * thrust * uref * jnp.abs(uref)
        rowforce = kernel * (magnitude[point_turbine] * valid)[:, None]
        force = jnp.zeros((N_GX, CX, N_GZ, CZ, N_GY, CY), jnp.float32)
        force = force.at[block_x, line_x, index_z, line_z, block_y].add(rowforce)
        force = force.reshape(NX, NZ, NY)
        forcing = jnp.stack([force, jnp.zeros_like(force), jnp.zeros_like(force)])
        laplace = neighbours(pad_cells(field)) - 6.0 * field
        star = field + time_step * (viscosity * laplace - forcing)
        spad = pad_cells(star)
        source = 0.5 * (spad[0, 2:, 1:-1, 1:-1] - spad[0, :-2, 1:-1, 1:-1])
        source = source + 0.5 * (spad[1, 1:-1, 1:-1, 2:] - spad[1, 1:-1, 1:-1, :-2])
        source = source + 0.5 * (spad[2, 1:-1, 2:, 1:-1] - spad[2, 1:-1, :-2, 1:-1])
        for sweep_index in range(SWEEPS):
            press = (neighbours(pad_cells(press)) - source) / 6.0
        ppad = pad_cells(press)
        grad_x = 0.5 * (ppad[2:, 1:-1, 1:-1] - ppad[:-2, 1:-1, 1:-1])
        grad_y = 0.5 * (ppad[1:-1, 1:-1, 2:] - ppad[1:-1, 1:-1, :-2])
        grad_z = 0.5 * (ppad[1:-1, 2:, 1:-1] - ppad[1:-1, :-2, 1:-1])
        field = star - jnp.stack([grad_x, grad_y, grad_z])
    return field, press
```

```python
import functools

import jax
import jax.numpy as jnp
from jax import lax
from jax.experimental import pallas as pl
from jax.experimental.pallas import tpu as pltpu
from jax.sharding import PartitionSpec as P

BAND = 32
STEPS = 2
SWEEPS = 8
CAP = 8
L = 128
D = 8
MESH = pl.DeviceIdType.MESH
CHUNKS = ((0, 8), (8, 16), (24, 16), (40, 16), (56, 8))
F32 = jnp.float32
BF16 = jnp.bfloat16
DIRS = tuple(
    (dx, dy, dz)
    for dx in (-1, 0, 1)
    for dy in (-1, 0, 1)
    for dz in (-1, 0, 1)
    if (dx, dy, dz) != (0, 0, 0)
)


def lanes(shape):
    return lax.broadcasted_iota(jnp.int32, shape, len(shape) - 1)


def rows_of(shape):
    return lax.broadcasted_iota(jnp.int32, shape, len(shape) - 2)


def pieces(x):
    hi = x.astype(BF16)
    rest = x - hi.astype(F32)
    mid = rest.astype(BF16)
    return hi, mid, (rest - mid.astype(F32)).astype(BF16)


def kernel(
    sizes,
    vel,
    prs,
    kern,
    own_r,
    line_r,
    turb_r,
    cnt,
    thrust,
    infx,
    infy,
    vout,
    pout,
    W,
    wys,
    wyr,
    wzs,
    wzr,
    E,
    ST,
    sys_,
    syr,
    szs,
    szr,
    E2,
    R,
    GS,
    gys,
    gyr,
    BGS,
    F,
    fys,
    fyr,
    BF,
    S,
    PR,
    S1,
    R1,
    S2,
    R2,
    LC,
    TC,
    O,
    KC,
    TB,
    u1s,
    u1r,
    u2s,
    u2r,
    in_sem,
    face_send,
    face_recv,
    star_send,
    star_recv,
    gs_send,
    gs_recv,
    f_send,
    f_recv,
    row_send,
    row_recv,
    u_send,
    u_recv,
):
    NGX, NGY, NGZ, CX, CZ = sizes
    Z = CZ + 2 * D
    X = CX + 2 * D
    NG = CX // 8
    T = thrust.shape[1]
    rows = kern.shape[0]
    peers = NGX * NGY
    slots = peers * CAP
    plane = NGY * NGZ
    gx = lax.axis_index("gx")
    gy = lax.axis_index("gy")
    gz = lax.axis_index("gz")
    own_z = pl.ds(D, CZ)

    def near(dx, dy, dz):
        return (
            lax.rem(gx + dx + NGX, NGX),
            lax.rem(gy + dy + NGY, NGY),
            lax.rem(gz + dz + NGZ, NGZ),
        )

    def plane_peer(r):
        spot = lax.rem(gy * NGZ + gz + r, plane)
        return (gx, spot // NGZ, lax.rem(spot, NGZ))

    def line_peer(r):
        return (lax.rem(gx + r, NGX), gy, gz)

    def remote(src, dst, send, recv, device):
        return pltpu.make_async_remote_copy(
            src_ref=src,
            dst_ref=dst,
            send_sem=send,
            recv_sem=recv,
            device_id=device,
            device_id_type=MESH,
        )

    loads = [
        pltpu.make_async_copy(vel, W.at[pl.ds(0, 3), pl.ds(1, CX), own_z, :], in_sem.at[0]),
        pltpu.make_async_copy(prs, W.at[3, pl.ds(1, CX), own_z, :], in_sem.at[1]),
    ]
    for load in loads:
        load.start()
    barrier = pltpu.get_barrier_semaphore()

    @pl.loop(1, plane)
    def _(r):
        pl.semaphore_signal(barrier, inc=1, device_id=plane_peer(r), device_id_type=MESH)

    @pl.loop(1, NGX)
    def _(r):
        pl.semaphore_signal(barrier, inc=1, device_id=line_peer(r), device_id_type=MESH)

    greeted = plane - 1 + NGX - 1
    for d in DIRS:
        if d[0] and (d[1] or d[2]):
            pl.semaphore_signal(barrier, inc=1, device_id=near(*d), device_id_type=MESH)
            greeted += 1

    owner = own_r[...]
    live = lanes((1, rows)) < cnt[...]
    spot = jnp.where(live, (owner % NGY) * NGX + owner // NGY, -1)
    land = (rows_of((peers, rows)) == spot).astype(F32)
    before = (rows_of((rows, rows)) < lanes((rows, rows))).astype(BF16)
    earlier = jnp.dot(land.astype(BF16), before, preferred_element_type=F32)
    rank = jnp.sum(land * earlier, axis=0, keepdims=True).astype(jnp.int32)
    slot = jnp.where(live, spot * CAP + rank, -1)
    place = (rows_of((slots, rows)) == slot).astype(BF16)
    hi, mid, lo = pieces(kern[...])
    both = jnp.dot(place, jnp.concatenate([hi, mid], axis=1), preferred_element_type=F32)
    sorted_rows = both[:, :L] + both[:, L:]
    sorted_rows = sorted_rows + jnp.dot(place, lo, preferred_element_type=F32)
    kind = rows_of((L, rows))
    line = line_r[...]
    told = jnp.where(kind < 8, line // 32, jnp.where(kind < 16, line % 32, turb_r[...]))
    told = jnp.where((kind % 8 == rank) & (kind < 24), told, 0).astype(F32).astype(BF16)
    meta = lax.dot_general(
        land.astype(BF16), told, (((1,), (1,)), ((), ())), preferred_element_type=F32
    )
    for k in range(NGY):
        S1[k, : NGX * CAP, :] = sorted_rows[k * NGX * CAP : (k + 1) * NGX * CAP]
        S1[k, NGX * CAP :, :] = meta[k * NGX : (k + 1) * NGX]
    TB[...] = jnp.zeros_like(TB)
    TB[0, 0:1, :T] = infx[...].astype(F32)
    TB[1, 0:1, :T] = infy[...].astype(F32)
    TB[2, 0:1, :T] = thrust[...]
    zero_pad = jnp.zeros((8, L), F32)
    for pp in range(2):
        for ab in range(2):

            @pl.loop(0, X)
            def _(x):
                PR[pp, ab, x, 0:8, :] = zero_pad
                PR[pp, ab, x, Z + 8 : Z + 16, :] = zero_pad

    BF[0, :, :] = jnp.zeros((Z, L), F32)
    BF[X + 1, :, :] = jnp.zeros((Z, L), F32)
    for load in loads:
        load.wait()
    pl.semaphore_wait(barrier, greeted)

    def row_first(r):
        peer = lax.rem(gy + r, NGY)
        return remote(
            S1.at[peer], R1.at[r - 1], row_send.at[r - 1], row_recv.at[r - 1], (gx, peer, gz)
        )

    for r in range(1, NGY):
        row_first(r).start()
    R1[NGY - 1] = S1[gy]

    lane = lanes((CZ, L))

    def face_copies(step):
        nc = 4 if step == 0 else 3
        comps = pl.ds(0, nc)
        many = pl.ds(0, nc * CX)
        return [
            remote(
                W.at[comps, pl.ds(CX, 1), own_z, :],
                W.at[comps, pl.ds(0, 1), own_z, :],
                face_send.at[0],
                face_recv.at[0],
                near(1, 0, 0),
            ),
            remote(
                W.at[comps, pl.ds(1, 1), own_z, :],
                W.at[comps, pl.ds(CX + 1, 1), own_z, :],
                face_send.at[1],
                face_recv.at[1],
                near(-1, 0, 0),
            ),
            remote(wys, wyr.at[0], face_send.at[2], face_recv.at[2], near(0, 1, 0)),
            remote(wys, wyr.at[1], face_send.at[3], face_recv.at[3], near(0, -1, 0)),
            remote(
                wzs.at[1, many], wzr.at[0, many], face_send.at[4], face_recv.at[4], near(0, 0, 1)
            ),
            remote(
                wzs.at[0, many], wzr.at[1, many], face_send.at[5], face_recv.at[5], near(0, 0, -1)
            ),
        ]

    def edge_lanes(q):
        return (lane == 2 * q) | (lane == lax.rem(2 * q + L - 1, L))

    def send_faces(step):
        nc = 4 if step == 0 else 3
        copies = face_copies(step)
        copies[0].start()
        copies[1].start()
        for c in range(nc):
            wzs[0, c * CX : (c + 1) * CX, :] = W[c, 1 : CX + 1, D, :]
            wzs[1, c * CX : (c + 1) * CX, :] = W[c, 1 : CX + 1, D + CZ - 1, :]
        copies[4].start()
        copies[5].start()
        packed = jnp.zeros((CZ, L), F32)
        for c in range(nc):

            def pack(x, kept, c=c):
                q = c * CX + x
                turned = pltpu.roll(W[c, 1 + x, own_z, :], 2 * q, 1)
                return jnp.where(edge_lanes(q), turned, kept)

            packed = lax.fori_loop(0, CX, pack, packed)
        wys[...] = packed
        copies[2].start()
        copies[3].start()
        return copies

    def merged(received):
        right = jnp.where(gy < NGY - 1, received[1], 0.0)
        left = jnp.where(gy > 0, received[0], 0.0)
        return jnp.where(lane % 2 == 0, right, pltpu.roll(left, 2, 1))

    def wait_faces(step, copies):
        nc = 4 if step == 0 else 3
        for copy in copies:
            copy.wait()
        E[...] = merged(wyr)
        for c in range(nc):
            W[c, 0, own_z, :] = jnp.where(gx > 0, W[c, 0, own_z, :], 0.0)
            W[c, CX + 1, own_z, :] = jnp.where(gx < NGX - 1, W[c, CX + 1, own_z, :], 0.0)
            above = jnp.where(gz > 0, wzr[0, c * CX : (c + 1) * CX, :], 0.0)
            below = jnp.where(gz < NGZ - 1, wzr[1, c * CX : (c + 1) * CX, :], 0.0)
            W[c, 1 : CX + 1, D - 1, :] = above
            W[c, 1 : CX + 1, D + CZ, :] = below

    def sides(cells, edge):
        left = jnp.where(lane == 0, edge, pltpu.roll(cells, 1, 1))
        right = jnp.where(lane == L - 1, edge, pltpu.roll(cells, L - 1, 1))
        return left, right

    def edge_of(ref, q):
        return pltpu.roll(ref[...], lax.rem(2 * L - 1 - 2 * q, L), 1)

    def star_faces(step):
        nc = 4 if step == 0 else 3
        for c in range(nc):

            @pl.loop(0, CX)
            def _(x):
                cells = W[c, 1 + x, own_z, :]
                left, right = sides(cells, edge_of(E, c * CX + x))
                total = W[c, x, own_z, :] + W[c, x + 2, own_z, :]
                total = total + W[c, 1 + x, pl.ds(D - 1, CZ), :] + W[c, 1 + x, pl.ds(D + 1, CZ), :]
                total = total + left + right
                if c < 3:
                    ST[c, 1 + x, own_z, :] = 0.88 * cells + 0.02 * total
                else:
                    R[x] = total

        copies = [
            remote(
                ST.at[0, CX, own_z, :],
                ST.at[0, 0, own_z, :],
                star_send.at[0],
                star_recv.at[0],
                near(1, 0, 0),
            ),
            remote(
                ST.at[0, 1, own_z, :],
                ST.at[0, CX + 1, own_z, :],
                star_send.at[1],
                star_recv.at[1],
                near(-1, 0, 0),
            ),
            remote(sys_, syr.at[0], star_send.at[2], star_recv.at[2], near(0, 1, 0)),
            remote(sys_, syr.at[1], star_send.at[3], star_recv.at[3], near(0, -1, 0)),
            remote(szs.at[1], szr.at[0], star_send.at[4], star_recv.at[4], near(0, 0, 1)),
            remote(szs.at[0], szr.at[1], star_send.at[5], star_recv.at[5], near(0, 0, -1)),
        ]
        copies[0].start()
        copies[1].start()
        szs[0] = ST[2, 1 : CX + 1, D, :]
        szs[1] = ST[2, 1 : CX + 1, D + CZ - 1, :]
        copies[4].start()
        copies[5].start()

        def pack(x, kept):
            turned = pltpu.roll(ST[1, 1 + x, own_z, :], 2 * x, 1)
            return jnp.where(edge_lanes(x), turned, kept)

        sys_[...] = lax.fori_loop(0, CX, pack, jnp.zeros((CZ, L), F32))
        copies[2].start()
        copies[3].start()
        return copies

    def around(j):
        return lax.rem(lane - 16 * j + 8 + L, L) < 16

    def sources(step, copies):
        for copy in copies:
            copy.wait()
        E2[...] = merged(syr)
        ST[0, 0, own_z, :] = jnp.where(gx > 0, ST[0, 0, own_z, :], 0.0)
        ST[0, CX + 1, own_z, :] = jnp.where(gx < NGX - 1, ST[0, CX + 1, own_z, :], 0.0)
        ST[2, 1 : CX + 1, D - 1, :] = jnp.where(gz > 0, szr[0], 0.0)
        ST[2, 1 : CX + 1, D + CZ, :] = jnp.where(gz < NGZ - 1, szr[1], 0.0)
        for group in range(NG):

            def one(j, kept, group=group):
                x = group * 8 + j
                left, right = sides(ST[1, 1 + x, own_z, :], edge_of(E2, x))
                total = ST[0, x + 2, own_z, :] - ST[0, x, own_z, :] + right - left
                total = total + ST[2, 1 + x, pl.ds(D + 1, CZ), :]
                source = 0.5 * (total - ST[2, 1 + x, pl.ds(D - 1, CZ), :])
                first = R[x] - source
                GS[step, 0, D + x, own_z, :] = first
                GS[step, 1, D + x, own_z, :] = source
                mine = around(j)
                return (
                    jnp.where(mine, pltpu.roll(first, 16 * j, 1), kept[0]),
                    jnp.where(mine, pltpu.roll(source, 16 * j, 1), kept[1]),
                )

            nothing = jnp.zeros((CZ, L), F32)
            kept = lax.fori_loop(0, 8, one, (nothing, nothing))
            gys[0, group] = kept[0]
            gys[1, group] = kept[1]

    def deep_copies(cells, off, packed, received, send, recv):
        fields = pl.ds(0, packed.shape[0])
        copies = []
        for i, (dx, dy, dz) in enumerate(DIRS):
            if dy == 0:
                zs, zd = {
                    0: (own_z, own_z),
                    -1: (pl.ds(D, D), pl.ds(D + CZ, D)),
                    1: (pl.ds(CZ, D), pl.ds(0, D)),
                }[dz]
                deep = off if dz == 0 else D
                xs, xd = {
                    0: (pl.ds(off, CX), pl.ds(off, CX)),
                    -1: (pl.ds(off, deep), pl.ds(off + CX, deep)),
                    1: (pl.ds(off + CX - deep, deep), pl.ds(off - deep, deep)),
                }[dx]
                src = cells.at[fields, xs, zs, :]
                dst = cells.at[fields, xd, zd, :]
            else:
                zs, zd = {
                    0: (pl.ds(0, CZ), own_z),
                    -1: (pl.ds(0, D), pl.ds(D + CZ, D)),
                    1: (pl.ds(CZ - D, D), pl.ds(0, D)),
                }[dz]
                xs, xd = {
                    0: (pl.ds(0, NG), pl.ds(1, NG)),
                    -1: (pl.ds(0, 1), pl.ds(NG + 1, 1)),
                    1: (pl.ds(NG - 1, 1), pl.ds(0, 1)),
                }[dx]
                src = packed.at[fields, xs, zs, :]
                dst = received.at[0 if dy == 1 else 1, fields, xd, zd, :]
            copies.append(remote(src, dst, send.at[i], recv.at[i], near(dx, dy, dz)))
        return copies

    lane_z = lanes((Z, L))

    def unpacked(received, field, x):
        group, j = x // 8, lax.rem(x, 8)
        both_sides = jnp.where(
            lane_z % 16 < 8, received[1, field, group], received[0, field, group]
        )
        return pltpu.roll(both_sides, lax.rem(L - 16 * j, L), 1)

    def one_wait(whole_src, whole_dst, send, recv, device):
        remote(whole_src, whole_dst, send, recv, device).wait()

    def inflow_first(step):
        column = jnp.sum(W[0, 1 : CX + 1, own_z, :], axis=1)
        y = rows_of((L, L)) + gy * L
        begin = TB[1, 0:1, :].astype(jnp.int32)
        band = ((y >= begin) & (y < begin + BAND)).astype(F32)
        sums = jnp.dot(column, band, precision=lax.Precision.HIGHEST, preferred_element_type=F32)
        x = rows_of((CX, L)) + gx * CX
        picked = jnp.where(x == TB[0, 0:1, :].astype(jnp.int32), sums, 0.0)
        u1s[step] = jnp.broadcast_to(jnp.sum(picked, axis=0, keepdims=True), (8, L))

        @pl.loop(1, plane)
        def _(r):
            remote(
                u1s.at[step],
                u1r.at[step, r - 1],
                u_send.at[2 * step],
                u_recv.at[2 * step],
                plane_peer(r),
            ).start()

    def inflow_second(step):
        whole = u1r.at[step]
        one_wait(whole, whole, u_send.at[2 * step], u_recv.at[2 * step], plane_peer(1))
        u2s[step] = u1s[step] + jnp.sum(u1r[step], axis=0)

        @pl.loop(1, NGX)
        def _(r):
            remote(
                u2s.at[step],
                u2r.at[step, r - 1],
                u_send.at[2 * step + 1],
                u_recv.at[2 * step + 1],
                line_peer(r),
            ).start()

    def magnitudes(step):
        whole = u2r.at[step]
        one_wait(whole, whole, u_send.at[2 * step + 1], u_recv.at[2 * step + 1], line_peer(1))
        total = u2s[step] + jnp.sum(u2r[step], axis=0)
        uref = total[0:1] * (1.0 / (BAND * CZ * NGZ))
        return 0.5 * TB[2, 0:1, :] * uref * jnp.abs(uref)

    def forces(step):
        size = magnitudes(step)

        @pl.loop(0, NGX)
        def _(g):
            at = pl.ds(pl.multiple_of(g * CAP * NGY, CAP * NGY), CAP * NGY)
            hot = jnp.where(TC[at, :] == lanes((CAP * NGY, L)).astype(F32), size, 0.0)
            scaled = R2[g, : CAP * NGY, :] * jnp.sum(hot, axis=1, keepdims=True)
            top = scaled.astype(BF16)
            KC[at, :L] = top
            KC[at, L:] = (scaled - top.astype(F32)).astype(BF16)

        part = CX // 4
        for h in range(4):
            both = jnp.dot(
                O[h * part * CZ : (h + 1) * part * CZ, :], KC[...], preferred_element_type=F32
            )
            force = (both[:, :L] + both[:, L:]).reshape(part, CZ, L)
            F[0, D + 1 + h * part : D + 1 + (h + 1) * part, own_z, :] = force
        for group in range(NG):

            def pack(j, kept, group=group):
                turned = pltpu.roll(F[0, D + 1 + group * 8 + j, own_z, :], 16 * j, 1)
                return jnp.where(around(j), turned, kept)

            fys[0, group] = lax.fori_loop(0, 8, pack, jnp.zeros((CZ, L), F32))
        copies = deep_copies(F, D + 1, fys, fyr, f_send, f_recv)
        for copy in copies:
            copy.start()
        return copies

    def inside(x):
        spot_x = gx * CX + x - D
        return (spot_x >= 0) & (spot_x < NGX * CX)

    ringlane = lanes((8, L))[0:1]
    right_ok = jnp.where(gy < NGY - 1, 1.0, 0.0)
    left_ok = jnp.where(gy > 0, 1.0, 0.0)
    ring = jnp.where(ringlane < D, right_ok, jnp.where(ringlane >= L - D, left_ok, 0.0))
    top_ok = jnp.where(gz > 0, 1.0, 0.0)
    bottom_ok = jnp.where(gz < NGZ - 1, 1.0, 0.0)

    def weights(x):
        base = jnp.where(inside(x), 1.0 / 6.0, 0.0)
        out = []
        for start, size in CHUNKS:
            scale = base
            if start == 0:
                scale = base * top_ok
            if start + size == Z:
                scale = base * bottom_ok
            out.append((scale, ring * scale))
        return out

    def ring_sides(a, b):
        lane_c = lanes(a.shape)
        am, bm = pltpu.roll(a, 1, 1), pltpu.roll(b, 1, 1)
        ap, bp = pltpu.roll(a, L - 1, 1), pltpu.roll(b, L - 1, 1)
        first, last = lane_c == 0, lane_c == L - 1
        return (
            (jnp.where(first, bm, am), jnp.where(last, bp, ap)),
            (jnp.where(first, am, bm), jnp.where(last, ap, bp)),
        )

    def sweeps(step, f_copies):
        for copy in f_copies:
            copy.wait()

        @pl.loop(0, X)
        def _(x):
            BF[x + 1] = unpacked(fyr, 0, x)

        @pl.loop(0, X)
        def _(x):
            plus = jnp.where(inside(x + 1), -0.2, 0.0)
            minus = jnp.where(inside(x - 1), -0.2, 0.0)
            scales = weights(x)
            for (start, size), (ca, cb) in zip(CHUNKS, scales):
                at = pl.ds(start, size)
                to = pl.ds(start + 8, size)
                fa = plus * F[0, x + 2, at, :] - minus * F[0, x, at, :]
                fb = plus * BF[x + 2, at, :] - minus * BF[x, at, :]
                S[0, x, at, :] = GS[step, 1, x, at, :] + fa
                S[1, x, at, :] = BGS[1, x, at, :] + fb
                PR[0, 0, x, to, :] = (GS[step, 0, x, at, :] - fa) * ca
                PR[0, 1, x, to, :] = (BGS[0, x, at, :] - fb) * cb

        for k in range(2, SWEEPS + 1):
            src, dst = k % 2, (k + 1) % 2
            deep = SWEEPS + 1 - k

            @pl.loop(D - deep, D + CX + deep)
            def _(x):
                scales = weights(x)
                for (start, size), (ca, cb) in zip(CHUNKS, scales):
                    at = pl.ds(start + 8, size)
                    up = pl.ds(start + 7, size)
                    down = pl.ds(start + 9, size)
                    a_sides, b_sides = ring_sides(PR[src, 0, x, at, :], PR[src, 1, x, at, :])
                    for ab, (left, right), scale in ((0, a_sides, ca), (1, b_sides, cb)):
                        total = PR[src, ab, x - 1, at, :] + PR[src, ab, x + 1, at, :]
                        total = total + PR[src, ab, x, up, :] + PR[src, ab, x, down, :]
                        total = total + (left + right)
                        total = total - S[ab, x, pl.ds(start, size), :]
                        PR[dst, ab, x, at, :] = total * scale

        at = pl.ds(D + 8, CZ)
        last = (SWEEPS + 1) % 2

        @pl.loop(0, CX)
        def _(x):
            deep = D + x
            (left, right), _ = ring_sides(PR[last, 0, deep, at, :], PR[last, 1, deep, at, :])
            back, ahead = PR[last, 0, deep - 1, at, :], PR[last, 0, deep + 1, at, :]
            up = PR[last, 0, deep, pl.ds(D + 7, CZ), :]
            down = PR[last, 0, deep, pl.ds(D + 9, CZ), :]
            force = F[0, D + 1 + x, own_z, :]
            W[0, 1 + x, own_z, :] = ST[0, 1 + x, own_z, :] - 0.4 * force - 0.5 * (ahead - back)
            W[1, 1 + x, own_z, :] = ST[1, 1 + x, own_z, :] - 0.5 * (right - left)
            W[2, 1 + x, own_z, :] = ST[2, 1 + x, own_z, :] - 0.5 * (down - up)
            if step == 0:
                R[x] = back + ahead + up + down + left + right

    def unpack_sources(step, copies):
        for copy in copies:
            copy.wait()
        for field in range(2):

            @pl.loop(0, X)
            def _(x):
                BGS[field, x] = unpacked(gyr.at[step], field, x)

    def row_second():
        for r in range(1, NGY):
            row_first(r).wait()

        @pl.loop(0, NGX)
        def _(d):
            for k in range(NGY):
                at = pl.ds(pl.multiple_of(d * CAP, CAP), CAP)
                S2[d, k * CAP : (k + 1) * CAP, :] = R1[k, at, :]
                S2[d, NGY * CAP + k : NGY * CAP + k + 1, :] = R1[k, pl.ds(NGX * CAP + d, 1), :]

        @pl.loop(1, NGX)
        def _(r):
            peer = lax.rem(gx + r, NGX)
            remote(
                S2.at[peer], R2.at[r - 1], row_send.at[NGY], row_recv.at[NGY], (peer, gy, gz)
            ).start()

        R2[NGX - 1] = S2[gx]

    def row_last():
        whole = R2.at[pl.ds(0, NGX - 1)]
        one_wait(whole, whole, row_send.at[NGY], row_recv.at[NGY], line_peer(1))
        which = lanes((CAP, L)) - rows_of((CAP, L))

        @pl.loop(0, NGX)
        def _(g):
            for k in range(NGY):
                row = R2[g, NGY * CAP + k : NGY * CAP + k + 1, :]
                told_line = jnp.where(which == 0, 32.0 * row, jnp.where(which == 8, row, 0.0))
                told_turbine = jnp.where(which == 16, row, 0.0)
                at = pl.ds(pl.multiple_of((g * NGY + k) * CAP, CAP), CAP)
                LC[at, :] = jnp.broadcast_to(
                    jnp.sum(told_line, axis=1, keepdims=True), (CAP, L)
                )
                TC[at, :] = jnp.broadcast_to(
                    jnp.sum(told_turbine, axis=1, keepdims=True), (CAP, L)
                )

        wide = min(L, slots)
        same = rows_of((wide, wide)) == lanes((wide, wide))
        for c in range(slots // wide):
            turned = jnp.where(same, LC[c * wide : (c + 1) * wide, :wide], 0.0)
            named = jnp.sum(turned, axis=0, keepdims=True).astype(jnp.int32)

            @pl.loop(0, CX)
            def _(x):
                at = pl.ds(pl.multiple_of(x * CZ, CZ), CZ)
                hit = rows_of((CZ, wide)) + x * CZ == named
                O[at, c * wide : (c + 1) * wide] = hit.astype(F32).astype(BF16)

    for step in range(STEPS):
        faces = send_faces(step)
        inflow_first(step)
        wait_faces(step, faces)
        stars = star_faces(step)
        if step == 0:
            row_second()
        inflow_second(step)
        sources(step, stars)
        deep = deep_copies(GS.at[step], D, gys, gyr.at[step], gs_send.at[step], gs_recv.at[step])
        for copy in deep:
            copy.start()
        if step == 0:
            row_last()
        f_copies = forces(step)
        unpack_sources(step, deep)
        sweeps(step, f_copies)

    last = (SWEEPS + 1) % 2
    outs = [
        pltpu.make_async_copy(W.at[pl.ds(0, 3), pl.ds(1, CX), own_z, :], vout, in_sem.at[0]),
        pltpu.make_async_copy(
            PR.at[last, 0, pl.ds(D, CX), pl.ds(D + 8, CZ), :], pout, in_sem.at[1]
        ),
    ]
    for out in outs:
        out.start()
    for out in outs:
        out.wait()


def body(
    shape,
    velocity,
    pressure,
    kern,
    owners,
    lines,
    point_turbine,
    row_counts,
    thrust,
    inflow_x,
    inflow_y,
):
    ngx, ngy, ngz = shape
    cx, cz = velocity.shape[1:3]
    z, x, ng = cz + 2 * D, cx + 2 * D, cx // 8
    rows = kern.shape[0]
    slots = ngx * ngy * CAP
    turbines = thrust.shape[0]
    any_spec = pl.BlockSpec(memory_space=pl.ANY)
    vmem_spec = pl.BlockSpec(memory_space=pltpu.VMEM)
    vm = pltpu.VMEM
    dma = pltpu.SemaphoreType.DMA
    meta = max(8, ngy)
    scratch = [
        vm((4, cx + 2, z, L), F32),
        vm((cz, L), F32),
        vm((2, cz, L), F32),
        vm((2, 4 * cx, L), F32),
        vm((2, 4 * cx, L), F32),
        vm((cz, L), F32),
        vm((3, cx + 2, z, L), F32),
        vm((cz, L), F32),
        vm((2, cz, L), F32),
        vm((2, cx, L), F32),
        vm((2, cx, L), F32),
        vm((cz, L), F32),
        vm((cx, cz, L), F32),
        vm((STEPS, 2, x, z, L), F32),
        vm((2, ng, cz, L), F32),
        vm((STEPS, 2, 2, ng + 2, z, L), F32),
        vm((2, x, z, L), F32),
        vm((1, x + 2, z, L), F32),
        vm((1, ng, cz, L), F32),
        vm((2, 1, ng + 2, z, L), F32),
        vm((x + 2, z, L), F32),
        vm((2, x, z, L), F32),
        vm((2, 2, x, z + 16, L), F32),
        vm((ngy, ngx * CAP + ngx, L), F32),
        vm((ngy, ngx * CAP + ngx, L), F32),
        vm((ngx, ngy * CAP + meta, L), F32),
        vm((ngx, ngy * CAP + meta, L), F32),
        vm((slots, L), F32),
        vm((slots, L), F32),
        vm((cx * cz, slots), BF16),
        vm((slots, 2 * L), BF16),
        vm((3, 8, L), F32),
        vm((STEPS, 8, L), F32),
        vm((STEPS, ngy * ngz - 1, 8, L), F32),
        vm((STEPS, 8, L), F32),
        vm((STEPS, ngx - 1, 8, L), F32),
        dma((2,)),
        dma((6,)),
        dma((6,)),
        dma((6,)),
        dma((6,)),
        dma((STEPS, 26)),
        dma((STEPS, 26)),
        dma((26,)),
        dma((26,)),
        dma((ngy + 1,)),
        dma((ngy + 1,)),
        dma((2 * STEPS,)),
        dma((2 * STEPS,)),
    ]
    return pl.pallas_call(
        functools.partial(kernel, (ngx, ngy, ngz, cx, cz)),
        out_shape=(
            jax.ShapeDtypeStruct(velocity.shape, F32),
            jax.ShapeDtypeStruct(pressure.shape, F32),
        ),
        in_specs=[any_spec] * 2 + [vmem_spec] * 8,
        out_specs=(any_spec, any_spec),
        scratch_shapes=scratch,
        compiler_params=pltpu.CompilerParams(
            collective_id=0, has_side_effects=True, vmem_limit_bytes=56 * 1024 * 1024
        ),
    )(
        velocity,
        pressure,
        kern,
        owners.reshape(1, rows),
        lines.reshape(1, rows),
        point_turbine.reshape(1, rows),
        row_counts.reshape(1, 1),
        thrust.reshape(1, turbines),
        inflow_x.reshape(1, turbines),
        inflow_y.reshape(1, turbines),
    )


def solution(mesh):
    placed = (
        P(None, "gx", "gz", "gy"),
        P("gx", "gz", "gy"),
        P(("gx", "gy", "gz"), None),
        P(("gx", "gy", "gz"), None),
        P(("gx", "gy", "gz")),
        P(("gx", "gy", "gz")),
        P("gx", "gy", "gz"),
        P(),
        P(),
        P(),
    )
    shape = (mesh.shape["gx"], mesh.shape["gy"], mesh.shape["gz"])
    return jax.shard_map(
        functools.partial(body, shape),
        mesh=mesh,
        in_specs=placed,
        out_specs=(P(None, "gx", "gz", "gy"), P("gx", "gz", "gy")),
        check_vma=False,
    )
```

```python
import functools

import jax
import jax.numpy as jnp
from jax import lax
from jax.experimental import pallas as pl
from jax.experimental.pallas import tpu as pltpu
from jax.sharding import PartitionSpec as P

BAND = 32
STEPS = 2
SWEEPS = 8
CAP = 8
L = 128
D = 8
BLOCK = 4
MESH = pl.DeviceIdType.MESH
CHUNKS = ((0, 8), (8, 16), (24, 16), (40, 16), (56, 8))
F32 = jnp.float32
BF16 = jnp.bfloat16
DIRS = tuple(
    (dx, dy, dz)
    for dx in (-1, 0, 1)
    for dy in (-1, 0, 1)
    for dz in (-1, 0, 1)
    if (dx, dy, dz) != (0, 0, 0)
)


def lanes(shape):
    return lax.broadcasted_iota(jnp.int32, shape, len(shape) - 1)


def rows_of(shape):
    return lax.broadcasted_iota(jnp.int32, shape, len(shape) - 2)


def pieces(x):
    hi = x.astype(BF16)
    rest = x - hi.astype(F32)
    mid = rest.astype(BF16)
    return hi, mid, (rest - mid.astype(F32)).astype(BF16)


def kernel(
    sizes,
    vel,
    prs,
    kern,
    own_r,
    line_r,
    turb_r,
    cnt,
    thrust,
    infx,
    infy,
    vout,
    pout,
    W,
    wys,
    wyr,
    wzs,
    wzr,
    E,
    ST,
    sys_,
    syr,
    szs,
    szr,
    E2,
    R,
    GS,
    gys,
    gyr,
    BGS,
    F,
    fys,
    fyr,
    BF,
    S,
    PR,
    S1,
    R1,
    S2,
    R2,
    LC,
    TC,
    O,
    KC,
    TB,
    u1s,
    u1r,
    u2s,
    u2r,
    in_sem,
    face_send,
    face_recv,
    star_send,
    star_recv,
    gs_send,
    gs_recv,
    f_send,
    f_recv,
    row_send,
    row_recv,
    u_send,
    u_recv,
):
    NGX, NGY, NGZ, CX, CZ = sizes
    Z = CZ + 2 * D
    X = CX + 2 * D
    NG = CX // 8
    T = thrust.shape[1]
    rows = kern.shape[0]
    peers = NGX * NGY
    slots = peers * CAP
    plane = NGY * NGZ
    gx = lax.axis_index("gx")
    gy = lax.axis_index("gy")
    gz = lax.axis_index("gz")
    own_z = pl.ds(D, CZ)

    def near(dx, dy, dz):
        return (
            lax.rem(gx + dx + NGX, NGX),
            lax.rem(gy + dy + NGY, NGY),
            lax.rem(gz + dz + NGZ, NGZ),
        )

    def plane_peer(r):
        spot = lax.rem(gy * NGZ + gz + r, plane)
        return (gx, spot // NGZ, lax.rem(spot, NGZ))

    def line_peer(r):
        return (lax.rem(gx + r, NGX), gy, gz)

    def remote(src, dst, send, recv, device):
        return pltpu.make_async_remote_copy(
            src_ref=src,
            dst_ref=dst,
            send_sem=send,
            recv_sem=recv,
            device_id=device,
            device_id_type=MESH,
        )

    loads = [
        pltpu.make_async_copy(vel, W.at[pl.ds(0, 3), pl.ds(1, CX), own_z, :], in_sem.at[0]),
        pltpu.make_async_copy(prs, W.at[3, pl.ds(1, CX), own_z, :], in_sem.at[1]),
    ]
    for load in loads:
        load.start()
    barrier = pltpu.get_barrier_semaphore()

    @pl.loop(1, plane)
    def _(r):
        pl.semaphore_signal(barrier, inc=1, device_id=plane_peer(r), device_id_type=MESH)

    @pl.loop(1, NGX)
    def _(r):
        pl.semaphore_signal(barrier, inc=1, device_id=line_peer(r), device_id_type=MESH)

    greeted = plane - 1 + NGX - 1
    for d in DIRS:
        if d[0] and (d[1] or d[2]):
            pl.semaphore_signal(barrier, inc=1, device_id=near(*d), device_id_type=MESH)
            greeted += 1

    owner = own_r[...]
    live = lanes((1, rows)) < cnt[...]
    spot = jnp.where(live, (owner % NGY) * NGX + owner // NGY, -1)
    land = (rows_of((peers, rows)) == spot).astype(F32)
    before = (rows_of((rows, rows)) < lanes((rows, rows))).astype(BF16)
    earlier = jnp.dot(land.astype(BF16), before, preferred_element_type=F32)
    rank = jnp.sum(land * earlier, axis=0, keepdims=True).astype(jnp.int32)
    slot = jnp.where(live, spot * CAP + rank, -1)
    place = (rows_of((slots, rows)) == slot).astype(BF16)
    hi, mid, lo = pieces(kern[...])
    both = jnp.dot(place, jnp.concatenate([hi, mid], axis=1), preferred_element_type=F32)
    sorted_rows = both[:, :L] + both[:, L:]
    sorted_rows = sorted_rows + jnp.dot(place, lo, preferred_element_type=F32)
    kind = rows_of((L, rows))
    line = line_r[...]
    told = jnp.where(kind < 8, line // 32, jnp.where(kind < 16, line % 32, turb_r[...]))
    told = jnp.where((kind % 8 == rank) & (kind < 24), told, 0).astype(F32).astype(BF16)
    meta = lax.dot_general(
        land.astype(BF16), told, (((1,), (1,)), ((), ())), preferred_element_type=F32
    )
    for k in range(NGY):
        S1[k, : NGX * CAP, :] = sorted_rows[k * NGX * CAP : (k + 1) * NGX * CAP]
        S1[k, NGX * CAP :, :] = meta[k * NGX : (k + 1) * NGX]
    TB[...] = jnp.zeros_like(TB)
    TB[0, 0:1, :T] = infx[...].astype(F32)
    TB[1, 0:1, :T] = infy[...].astype(F32)
    TB[2, 0:1, :T] = thrust[...]
    zero_pad = jnp.zeros((8, L), F32)
    for pp in range(2):
        for ab in range(2):

            @pl.loop(0, X + 2, unroll=X + 2)
            def _(x):
                PR[pp, ab, x, 0:8, :] = zero_pad
                PR[pp, ab, x, Z + 8 : Z + 16, :] = zero_pad

            PR[pp, ab, 0, :, :] = jnp.zeros((Z + 16, L), F32)
            PR[pp, ab, X + 1, :, :] = jnp.zeros((Z + 16, L), F32)

    BF[0, :, :] = jnp.zeros((Z, L), F32)
    BF[X + 1, :, :] = jnp.zeros((Z, L), F32)
    for load in loads:
        load.wait()
    pl.semaphore_wait(barrier, greeted)

    def row_first(r):
        peer = lax.rem(gy + r, NGY)
        return remote(
            S1.at[peer], R1.at[r - 1], row_send.at[r - 1], row_recv.at[r - 1], (gx, peer, gz)
        )

    for r in range(1, NGY):
        row_first(r).start()
    R1[NGY - 1] = S1[gy]

    lane = lanes((CZ, L))

    def face_copies(step):
        nc = 4 if step == 0 else 3
        comps = pl.ds(0, nc)
        many = pl.ds(0, nc * CX)
        return [
            remote(
                W.at[comps, pl.ds(CX, 1), own_z, :],
                W.at[comps, pl.ds(0, 1), own_z, :],
                face_send.at[0],
                face_recv.at[0],
                near(1, 0, 0),
            ),
            remote(
                W.at[comps, pl.ds(1, 1), own_z, :],
                W.at[comps, pl.ds(CX + 1, 1), own_z, :],
                face_send.at[1],
                face_recv.at[1],
                near(-1, 0, 0),
            ),
            remote(wys, wyr.at[0], face_send.at[2], face_recv.at[2], near(0, 1, 0)),
            remote(wys, wyr.at[1], face_send.at[3], face_recv.at[3], near(0, -1, 0)),
            remote(
                wzs.at[1, many], wzr.at[0, many], face_send.at[4], face_recv.at[4], near(0, 0, 1)
            ),
            remote(
                wzs.at[0, many], wzr.at[1, many], face_send.at[5], face_recv.at[5], near(0, 0, -1)
            ),
        ]

    def turn(cells, by):
        return pltpu.roll(cells, by % L, 1) if by % L else cells

    def edge_lanes(q):
        return (lane == 2 * q) | (lane == (2 * q + L - 1) % L)

    def send_faces(step):
        nc = 4 if step == 0 else 3
        copies = face_copies(step)
        copies[0].start()
        copies[1].start()
        for c in range(nc):
            wzs[0, c * CX : (c + 1) * CX, :] = W[c, 1 : CX + 1, D, :]
            wzs[1, c * CX : (c + 1) * CX, :] = W[c, 1 : CX + 1, D + CZ - 1, :]
        copies[4].start()
        copies[5].start()
        packed = jnp.zeros((CZ, L), F32)
        for c in range(nc):

            for x in range(CX):
                q = c * CX + x
                turned = pltpu.roll(W[c, 1 + x, own_z, :], 2 * q, 1) if q else W[c, 1, own_z, :]
                packed = jnp.where(edge_lanes(q), turned, packed)
        wys[...] = packed
        copies[2].start()
        copies[3].start()
        return copies

    def merged(received):
        right = jnp.where(gy < NGY - 1, received[1], 0.0)
        left = jnp.where(gy > 0, received[0], 0.0)
        return jnp.where(lane % 2 == 0, right, pltpu.roll(left, 2, 1))

    def wait_faces(step, copies):
        nc = 4 if step == 0 else 3
        for copy in copies:
            copy.wait()
        E[...] = merged(wyr)
        for c in range(nc):
            W[c, 0, own_z, :] = jnp.where(gx > 0, W[c, 0, own_z, :], 0.0)
            W[c, CX + 1, own_z, :] = jnp.where(gx < NGX - 1, W[c, CX + 1, own_z, :], 0.0)
            above = jnp.where(gz > 0, wzr[0, c * CX : (c + 1) * CX, :], 0.0)
            below = jnp.where(gz < NGZ - 1, wzr[1, c * CX : (c + 1) * CX, :], 0.0)
            W[c, 1 : CX + 1, D - 1, :] = above
            W[c, 1 : CX + 1, D + CZ, :] = below

    def sides(cells, edge):
        left = jnp.where(lane == 0, edge, pltpu.roll(cells, 1, 1))
        right = jnp.where(lane == L - 1, edge, pltpu.roll(cells, L - 1, 1))
        return left, right

    def edge_of(ref, q):
        return pltpu.roll(ref[...], (2 * L - 1 - 2 * q) % L, 1)

    def star_faces(step):
        nc = 4 if step == 0 else 3
        for c in range(nc):

            @pl.loop(0, CX, unroll=8)
            def _(x):
                cells = W[c, 1 + x, own_z, :]
                left, right = sides(cells, edge_of(E, c * CX + x))
                total = W[c, x, own_z, :] + W[c, x + 2, own_z, :]
                total = total + W[c, 1 + x, pl.ds(D - 1, CZ), :] + W[c, 1 + x, pl.ds(D + 1, CZ), :]
                total = total + left + right
                if c < 3:
                    ST[c, 1 + x, own_z, :] = 0.88 * cells + 0.02 * total
                else:
                    R[x] = total

        copies = [
            remote(
                ST.at[0, CX, own_z, :],
                ST.at[0, 0, own_z, :],
                star_send.at[0],
                star_recv.at[0],
                near(1, 0, 0),
            ),
            remote(
                ST.at[0, 1, own_z, :],
                ST.at[0, CX + 1, own_z, :],
                star_send.at[1],
                star_recv.at[1],
                near(-1, 0, 0),
            ),
            remote(sys_, syr.at[0], star_send.at[2], star_recv.at[2], near(0, 1, 0)),
            remote(sys_, syr.at[1], star_send.at[3], star_recv.at[3], near(0, -1, 0)),
            remote(szs.at[1], szr.at[0], star_send.at[4], star_recv.at[4], near(0, 0, 1)),
            remote(szs.at[0], szr.at[1], star_send.at[5], star_recv.at[5], near(0, 0, -1)),
        ]
        copies[0].start()
        copies[1].start()
        szs[0] = ST[2, 1 : CX + 1, D, :]
        szs[1] = ST[2, 1 : CX + 1, D + CZ - 1, :]
        copies[4].start()
        copies[5].start()

        packed = jnp.zeros((CZ, L), F32)
        for x in range(CX):
            turned = pltpu.roll(ST[1, 1 + x, own_z, :], 2 * x, 1) if x else ST[1, 1, own_z, :]
            packed = jnp.where(edge_lanes(x), turned, packed)
        sys_[...] = packed
        copies[2].start()
        copies[3].start()
        return copies

    def around(j):
        return (lane + (8 - 16 * j) % L) % L < 16

    def sources(step, copies):
        for copy in copies:
            copy.wait()
        E2[...] = merged(syr)
        ST[0, 0, own_z, :] = jnp.where(gx > 0, ST[0, 0, own_z, :], 0.0)
        ST[0, CX + 1, own_z, :] = jnp.where(gx < NGX - 1, ST[0, CX + 1, own_z, :], 0.0)
        ST[2, 1 : CX + 1, D - 1, :] = jnp.where(gz > 0, szr[0], 0.0)
        ST[2, 1 : CX + 1, D + CZ, :] = jnp.where(gz < NGZ - 1, szr[1], 0.0)
        for group in range(NG):

            kept = [jnp.zeros((CZ, L), F32), jnp.zeros((CZ, L), F32)]
            for j in range(8):
                x = group * 8 + j
                left, right = sides(ST[1, 1 + x, own_z, :], edge_of(E2, x))
                total = ST[0, x + 2, own_z, :] - ST[0, x, own_z, :] + right - left
                total = total + ST[2, 1 + x, pl.ds(D + 1, CZ), :]
                source = 0.5 * (total - ST[2, 1 + x, pl.ds(D - 1, CZ), :])
                first = R[x] - source
                GS[step, 0, D + x, own_z, :] = first
                GS[step, 1, D + x, own_z, :] = source
                mine = around(j)
                kept[0] = jnp.where(mine, turn(first, 16 * j), kept[0])
                kept[1] = jnp.where(mine, turn(source, 16 * j), kept[1])
            gys[0, group] = kept[0]
            gys[1, group] = kept[1]

    def deep_copies(cells, off, packed, received, send, recv):
        fields = pl.ds(0, packed.shape[0])
        copies = []
        for i, (dx, dy, dz) in enumerate(DIRS):
            if dy == 0:
                zs, zd = {
                    0: (own_z, own_z),
                    -1: (pl.ds(D, D), pl.ds(D + CZ, D)),
                    1: (pl.ds(CZ, D), pl.ds(0, D)),
                }[dz]
                deep = off if dz == 0 else D
                xs, xd = {
                    0: (pl.ds(off, CX), pl.ds(off, CX)),
                    -1: (pl.ds(off, deep), pl.ds(off + CX, deep)),
                    1: (pl.ds(off + CX - deep, deep), pl.ds(off - deep, deep)),
                }[dx]
                src = cells.at[fields, xs, zs, :]
                dst = cells.at[fields, xd, zd, :]
            else:
                zs, zd = {
                    0: (pl.ds(0, CZ), own_z),
                    -1: (pl.ds(0, D), pl.ds(D + CZ, D)),
                    1: (pl.ds(CZ - D, D), pl.ds(0, D)),
                }[dz]
                xs, xd = {
                    0: (pl.ds(0, NG), pl.ds(1, NG)),
                    -1: (pl.ds(0, 1), pl.ds(NG + 1, 1)),
                    1: (pl.ds(NG - 1, 1), pl.ds(0, 1)),
                }[dx]
                src = packed.at[fields, xs, zs, :]
                dst = received.at[0 if dy == 1 else 1, fields, xd, zd, :]
            copies.append(remote(src, dst, send.at[i], recv.at[i], near(dx, dy, dz)))
        return copies

    lane_z = lanes((Z, L))

    def unpack(received, field, target, base):
        @pl.loop(0, NG + 2)
        def _(group):
            both_sides = jnp.where(
                lane_z % 16 < 8, received[1, field, group], received[0, field, group]
            )
            for j in range(8):
                target[base + group * 8 + j] = turn(both_sides, -16 * j)

    def one_wait(whole_src, whole_dst, send, recv, device):
        remote(whole_src, whole_dst, send, recv, device).wait()

    def inflow_first(step):
        column = jnp.sum(W[0, 1 : CX + 1, own_z, :], axis=1)
        y = rows_of((L, L)) + gy * L
        begin = TB[1, 0:1, :].astype(jnp.int32)
        band = ((y >= begin) & (y < begin + BAND)).astype(F32)
        sums = jnp.dot(column, band, precision=lax.Precision.HIGHEST, preferred_element_type=F32)
        x = rows_of((CX, L)) + gx * CX
        picked = jnp.where(x == TB[0, 0:1, :].astype(jnp.int32), sums, 0.0)
        u1s[step] = jnp.broadcast_to(jnp.sum(picked, axis=0, keepdims=True), (8, L))

        @pl.loop(1, plane)
        def _(r):
            remote(
                u1s.at[step],
                u1r.at[step, r - 1],
                u_send.at[2 * step],
                u_recv.at[2 * step],
                plane_peer(r),
            ).start()

    def inflow_second(step):
        whole = u1r.at[step]
        one_wait(whole, whole, u_send.at[2 * step], u_recv.at[2 * step], plane_peer(1))
        u2s[step] = u1s[step] + jnp.sum(u1r[step], axis=0)

        @pl.loop(1, NGX)
        def _(r):
            remote(
                u2s.at[step],
                u2r.at[step, r - 1],
                u_send.at[2 * step + 1],
                u_recv.at[2 * step + 1],
                line_peer(r),
            ).start()

    def magnitudes(step):
        whole = u2r.at[step]
        one_wait(whole, whole, u_send.at[2 * step + 1], u_recv.at[2 * step + 1], line_peer(1))
        total = u2s[step] + jnp.sum(u2r[step], axis=0)
        uref = total[0:1] * (1.0 / (BAND * CZ * NGZ))
        return 0.5 * TB[2, 0:1, :] * uref * jnp.abs(uref)

    def forces(step):
        size = magnitudes(step)

        @pl.loop(0, NGX, unroll=4)
        def _(g):
            at = pl.ds(pl.multiple_of(g * CAP * NGY, CAP * NGY), CAP * NGY)
            hot = jnp.where(TC[at, :] == lanes((CAP * NGY, L)).astype(F32), size, 0.0)
            scaled = R2[g, : CAP * NGY, :] * jnp.sum(hot, axis=1, keepdims=True)
            top = scaled.astype(BF16)
            KC[at, :L] = top
            KC[at, L:] = (scaled - top.astype(F32)).astype(BF16)

        part = CX // 4
        for h in range(4):
            both = jnp.dot(
                O[h * part * CZ : (h + 1) * part * CZ, :], KC[...], preferred_element_type=F32
            )
            force = (both[:, :L] + both[:, L:]).reshape(part, CZ, L)
            F[0, D + 1 + h * part : D + 1 + (h + 1) * part, own_z, :] = force
        for group in range(NG):

            kept = jnp.zeros((CZ, L), F32)
            for j in range(8):
                turned = turn(F[0, D + 1 + group * 8 + j, own_z, :], 16 * j)
                kept = jnp.where(around(j), turned, kept)
            fys[0, group] = kept
        copies = deep_copies(F, D + 1, fys, fyr, f_send, f_recv)
        for copy in copies:
            copy.start()
        return copies

    def inside(x):
        spot_x = gx * CX + x - D
        return (spot_x >= 0) & (spot_x < NGX * CX)

    ringlane = lanes((8, L))[0:1]
    right_ok = jnp.where(gy < NGY - 1, 1.0, 0.0)
    left_ok = jnp.where(gy > 0, 1.0, 0.0)
    ring = jnp.where(ringlane < D, right_ok, jnp.where(ringlane >= L - D, left_ok, 0.0))
    top_ok = jnp.where(gz > 0, 1.0, 0.0)
    bottom_ok = jnp.where(gz < NGZ - 1, 1.0, 0.0)

    def weights():
        out = []
        for start, size in CHUNKS:
            scale = 1.0 / 6.0
            if start == 0:
                scale = scale * top_ok
            if start + size == Z:
                scale = scale * bottom_ok
            out.append((scale, ring * scale))
        return out

    def outside_x(pp):
        for ok, x in ((gx > 0, D), (gx < NGX - 1, D + CX + 1)):

            @pl.when(jnp.logical_not(ok))
            def _():
                for ab in range(2):
                    PR[pp, ab, x, 8 : 8 + Z, :] = jnp.zeros((Z, L), F32)

    def ring_sides(a, b):
        axis, lane_c = a.ndim - 1, lanes(a.shape)
        am, bm = pltpu.roll(a, 1, axis), pltpu.roll(b, 1, axis)
        ap, bp = pltpu.roll(a, L - 1, axis), pltpu.roll(b, L - 1, axis)
        first, last = lane_c == 0, lane_c == L - 1
        return (
            (jnp.where(first, bm, am), jnp.where(last, bp, ap)),
            (jnp.where(first, am, bm), jnp.where(last, ap, bp)),
        )

    def sweeps(step, f_copies):
        for copy in f_copies:
            copy.wait()

        unpack(fyr, 0, BF, 1)
        scales = weights()

        @pl.loop(0, X, unroll=4)
        def _(x):
            plus = jnp.where(inside(x + 1), -0.2, 0.0)
            minus = jnp.where(inside(x - 1), -0.2, 0.0)
            for (start, size), (ca, cb) in zip(CHUNKS, scales):
                at = pl.ds(start, size)
                to = pl.ds(start + 8, size)
                fa = plus * F[0, x + 2, at, :] - minus * F[0, x, at, :]
                fb = plus * BF[x + 2, at, :] - minus * BF[x, at, :]
                S[0, x, at, :] = GS[step, 1, x, at, :] + fa
                S[1, x, at, :] = BGS[1, x, at, :] + fb
                PR[0, 0, x + 1, to, :] = (GS[step, 0, x, at, :] - fa) * ca
                PR[0, 1, x + 1, to, :] = (BGS[0, x, at, :] - fb) * cb

        outside_x(0)
        for k in range(2, SWEEPS + 1):
            src, dst = k % 2, (k + 1) % 2
            wide = -(-(CX + 2 * (SWEEPS + 1 - k)) // BLOCK) * BLOCK
            begin = (X - wide) // 2

            @pl.loop(0, wide // BLOCK)
            def _(block):
                x = begin + block * BLOCK
                mid, back, ahead = pl.ds(x + 1, BLOCK), pl.ds(x, BLOCK), pl.ds(x + 2, BLOCK)
                for (start, size), (ca, cb) in zip(CHUNKS, scales):
                    at = pl.ds(start + 8, size)
                    up = pl.ds(start + 7, size)
                    down = pl.ds(start + 9, size)
                    a_sides, b_sides = ring_sides(PR[src, 0, mid, at, :], PR[src, 1, mid, at, :])
                    for ab, (left, right), scale in ((0, a_sides, ca), (1, b_sides, cb)):
                        total = PR[src, ab, back, at, :] + PR[src, ab, ahead, at, :]
                        total = total + PR[src, ab, mid, up, :] + PR[src, ab, mid, down, :]
                        total = total - S[ab, pl.ds(x, BLOCK), pl.ds(start, size), :]
                        PR[dst, ab, mid, at, :] = (total + (left + right)) * scale

            outside_x(dst)

        at = pl.ds(D + 8, CZ)
        last = (SWEEPS + 1) % 2

        @pl.loop(0, CX, unroll=4)
        def _(x):
            deep = D + x + 1
            (left, right), _ = ring_sides(PR[last, 0, deep, at, :], PR[last, 1, deep, at, :])
            back, ahead = PR[last, 0, deep - 1, at, :], PR[last, 0, deep + 1, at, :]
            up = PR[last, 0, deep, pl.ds(D + 7, CZ), :]
            down = PR[last, 0, deep, pl.ds(D + 9, CZ), :]
            force = F[0, D + 1 + x, own_z, :]
            W[0, 1 + x, own_z, :] = ST[0, 1 + x, own_z, :] - 0.4 * force - 0.5 * (ahead - back)
            W[1, 1 + x, own_z, :] = ST[1, 1 + x, own_z, :] - 0.5 * (right - left)
            W[2, 1 + x, own_z, :] = ST[2, 1 + x, own_z, :] - 0.5 * (down - up)
            if step == 0:
                R[x] = back + ahead + up + down + left + right

    def unpack_sources(step, copies):
        for copy in copies:
            copy.wait()
        for field in range(2):
            unpack(gyr.at[step], field, BGS.at[field], 0)

    def row_second():
        for r in range(1, NGY):
            row_first(r).wait()

        @pl.loop(0, NGX)
        def _(d):
            for k in range(NGY):
                at = pl.ds(pl.multiple_of(d * CAP, CAP), CAP)
                S2[d, k * CAP : (k + 1) * CAP, :] = R1[k, at, :]
                S2[d, NGY * CAP + k : NGY * CAP + k + 1, :] = R1[k, pl.ds(NGX * CAP + d, 1), :]

        @pl.loop(1, NGX)
        def _(r):
            peer = lax.rem(gx + r, NGX)
            remote(
                S2.at[peer], R2.at[r - 1], row_send.at[NGY], row_recv.at[NGY], (peer, gy, gz)
            ).start()

        R2[NGX - 1] = S2[gx]

    def row_last():
        whole = R2.at[pl.ds(0, NGX - 1)]
        one_wait(whole, whole, row_send.at[NGY], row_recv.at[NGY], line_peer(1))
        which = lanes((CAP, L)) - rows_of((CAP, L))

        @pl.loop(0, NGX, unroll=4)
        def _(g):
            for k in range(NGY):
                row = R2[g, NGY * CAP + k : NGY * CAP + k + 1, :]
                told_line = jnp.where(which == 0, 32.0 * row, jnp.where(which == 8, row, 0.0))
                told_turbine = jnp.where(which == 16, row, 0.0)
                at = pl.ds(pl.multiple_of((g * NGY + k) * CAP, CAP), CAP)
                LC[at, :] = jnp.broadcast_to(
                    jnp.sum(told_line, axis=1, keepdims=True), (CAP, L)
                )
                TC[at, :] = jnp.broadcast_to(
                    jnp.sum(told_turbine, axis=1, keepdims=True), (CAP, L)
                )

        wide = min(L, slots)
        same = rows_of((wide, wide)) == lanes((wide, wide))
        for c in range(slots // wide):
            turned = jnp.where(same, LC[c * wide : (c + 1) * wide, :wide], 0.0)
            named = jnp.sum(turned, axis=0, keepdims=True).astype(jnp.int32)

            @pl.loop(0, CX)
            def _(x):
                at = pl.ds(pl.multiple_of(x * CZ, CZ), CZ)
                hit = rows_of((CZ, wide)) + x * CZ == named
                O[at, c * wide : (c + 1) * wide] = hit.astype(F32).astype(BF16)

    for step in range(STEPS):
        faces = send_faces(step)
        inflow_first(step)
        wait_faces(step, faces)
        stars = star_faces(step)
        if step == 0:
            row_second()
        inflow_second(step)
        sources(step, stars)
        deep = deep_copies(GS.at[step], D, gys, gyr.at[step], gs_send.at[step], gs_recv.at[step])
        for copy in deep:
            copy.start()
        if step == 0:
            row_last()
        f_copies = forces(step)
        unpack_sources(step, deep)
        sweeps(step, f_copies)

    last = (SWEEPS + 1) % 2
    outs = [
        pltpu.make_async_copy(W.at[pl.ds(0, 3), pl.ds(1, CX), own_z, :], vout, in_sem.at[0]),
        pltpu.make_async_copy(
            PR.at[last, 0, pl.ds(D + 1, CX), pl.ds(D + 8, CZ), :], pout, in_sem.at[1]
        ),
    ]
    for out in outs:
        out.start()
    for out in outs:
        out.wait()


def body(
    shape,
    velocity,
    pressure,
    kern,
    owners,
    lines,
    point_turbine,
    row_counts,
    thrust,
    inflow_x,
    inflow_y,
):
    ngx, ngy, ngz = shape
    cx, cz = velocity.shape[1:3]
    z, x, ng = cz + 2 * D, cx + 2 * D, cx // 8
    rows = kern.shape[0]
    slots = ngx * ngy * CAP
    turbines = thrust.shape[0]
    any_spec = pl.BlockSpec(memory_space=pl.ANY)
    vmem_spec = pl.BlockSpec(memory_space=pltpu.VMEM)
    vm = pltpu.VMEM
    dma = pltpu.SemaphoreType.DMA
    meta = max(8, ngy)
    scratch = [
        vm((4, cx + 2, z, L), F32),
        vm((cz, L), F32),
        vm((2, cz, L), F32),
        vm((2, 4 * cx, L), F32),
        vm((2, 4 * cx, L), F32),
        vm((cz, L), F32),
        vm((3, cx + 2, z, L), F32),
        vm((cz, L), F32),
        vm((2, cz, L), F32),
        vm((2, cx, L), F32),
        vm((2, cx, L), F32),
        vm((cz, L), F32),
        vm((cx, cz, L), F32),
        vm((STEPS, 2, x, z, L), F32),
        vm((2, ng, cz, L), F32),
        vm((STEPS, 2, 2, ng + 2, z, L), F32),
        vm((2, x, z, L), F32),
        vm((1, x + 2, z, L), F32),
        vm((1, ng, cz, L), F32),
        vm((2, 1, ng + 2, z, L), F32),
        vm((x + 2, z, L), F32),
        vm((2, x, z, L), F32),
        vm((2, 2, x + 2, z + 16, L), F32),
        vm((ngy, ngx * CAP + ngx, L), F32),
        vm((ngy, ngx * CAP + ngx, L), F32),
        vm((ngx, ngy * CAP + meta, L), F32),
        vm((ngx, ngy * CAP + meta, L), F32),
        vm((slots, L), F32),
        vm((slots, L), F32),
        vm((cx * cz, slots), BF16),
        vm((slots, 2 * L), BF16),
        vm((3, 8, L), F32),
        vm((STEPS, 8, L), F32),
        vm((STEPS, ngy * ngz - 1, 8, L), F32),
        vm((STEPS, 8, L), F32),
        vm((STEPS, ngx - 1, 8, L), F32),
        dma((2,)),
        dma((6,)),
        dma((6,)),
        dma((6,)),
        dma((6,)),
        dma((STEPS, 26)),
        dma((STEPS, 26)),
        dma((26,)),
        dma((26,)),
        dma((ngy + 1,)),
        dma((ngy + 1,)),
        dma((2 * STEPS,)),
        dma((2 * STEPS,)),
    ]
    return pl.pallas_call(
        functools.partial(kernel, (ngx, ngy, ngz, cx, cz)),
        out_shape=(
            jax.ShapeDtypeStruct(velocity.shape, F32),
            jax.ShapeDtypeStruct(pressure.shape, F32),
        ),
        in_specs=[any_spec] * 2 + [vmem_spec] * 8,
        out_specs=(any_spec, any_spec),
        scratch_shapes=scratch,
        compiler_params=pltpu.CompilerParams(
            collective_id=0, has_side_effects=True, vmem_limit_bytes=56 * 1024 * 1024
        ),
    )(
        velocity,
        pressure,
        kern,
        owners.reshape(1, rows),
        lines.reshape(1, rows),
        point_turbine.reshape(1, rows),
        row_counts.reshape(1, 1),
        thrust.reshape(1, turbines),
        inflow_x.reshape(1, turbines),
        inflow_y.reshape(1, turbines),
    )


def solution(mesh):
    placed = (
        P(None, "gx", "gz", "gy"),
        P("gx", "gz", "gy"),
        P(("gx", "gy", "gz"), None),
        P(("gx", "gy", "gz"), None),
        P(("gx", "gy", "gz")),
        P(("gx", "gy", "gz")),
        P("gx", "gy", "gz"),
        P(),
        P(),
        P(),
    )
    shape = (mesh.shape["gx"], mesh.shape["gy"], mesh.shape["gz"])
    return jax.shard_map(
        functools.partial(body, shape),
        mesh=mesh,
        in_specs=placed,
        out_specs=(P(None, "gx", "gz", "gy"), P("gx", "gz", "gy")),
        check_vma=False,
    )
```

```python
import functools

import jax
import jax.numpy as jnp
from jax import lax
from jax.experimental import pallas as pl
from jax.experimental.pallas import tpu as pltpu
from jax.sharding import PartitionSpec as P

BAND = 32
STEPS = 2
SWEEPS = 8
CAP = 8
L = 128
D = 8
BLOCK = 4
MESH = pl.DeviceIdType.MESH
CHUNKS = ((0, 8), (8, 16), (24, 16), (40, 16), (56, 8))
F32 = jnp.float32
BF16 = jnp.bfloat16
DIRS = tuple(
    sorted(
        (
            (dx, dy, dz)
            for dx in (-1, 0, 1)
            for dy in (-1, 0, 1)
            for dz in (-1, 0, 1)
            if (dx, dy, dz) != (0, 0, 0)
        ),
        key=lambda d: (abs(d[1]), abs(d[2]), -abs(d[0])),
    )
)


def lanes(shape):
    return lax.broadcasted_iota(jnp.int32, shape, len(shape) - 1)


def rows_of(shape):
    return lax.broadcasted_iota(jnp.int32, shape, len(shape) - 2)


def pieces(x):
    hi = x.astype(BF16)
    rest = x - hi.astype(F32)
    mid = rest.astype(BF16)
    return hi, mid, (rest - mid.astype(F32)).astype(BF16)


def kernel(
    sizes,
    vel,
    prs,
    kern_h,
    own_h,
    line_h,
    turb_h,
    cnt_h,
    thrust_h,
    infx_h,
    infy_h,
    vout,
    pout,
    kern,
    own_r,
    line_r,
    turb_r,
    cnt,
    thrust,
    infx,
    infy,
    W,
    wys,
    wyr,
    wzs,
    wzr,
    E,
    ST,
    sys_,
    syr,
    szs,
    szr,
    E2,
    R,
    GS,
    gys,
    gyr,
    BGS,
    F,
    fys,
    fyr,
    BF,
    S,
    PR,
    S1,
    R1,
    S2,
    R2,
    LC,
    TC,
    O,
    KC,
    TB,
    RING,
    u1s,
    u1r,
    u2s,
    u2r,
    in_sem,
    face_send,
    face_recv,
    star_send,
    star_recv,
    gs_send,
    gs_recv,
    f_send,
    f_recv,
    row_send,
    row_recv,
    u_send,
    u_recv,
):
    NGX, NGY, NGZ, CX, CZ = sizes
    Z = CZ + 2 * D
    X = CX + 2 * D
    NG = CX // 8
    T = thrust.shape[1]
    rows = kern.shape[0]
    peers = NGX * NGY
    slots = peers * CAP
    plane = NGY * NGZ
    gx = lax.axis_index("gx")
    gy = lax.axis_index("gy")
    gz = lax.axis_index("gz")
    own_z = pl.ds(D, CZ)

    def near(dx, dy, dz):
        return (
            lax.rem(gx + dx + NGX, NGX),
            lax.rem(gy + dy + NGY, NGY),
            lax.rem(gz + dz + NGZ, NGZ),
        )

    def plane_peer(r):
        spot = lax.rem(gy * NGZ + gz + r, plane)
        return (gx, spot // NGZ, lax.rem(spot, NGZ))

    def line_peer(r):
        return (lax.rem(gx + r, NGX), gy, gz)

    def remote(src, dst, send, recv, device):
        return pltpu.make_async_remote_copy(
            src_ref=src,
            dst_ref=dst,
            send_sem=send,
            recv_sem=recv,
            device_id=device,
            device_id_type=MESH,
        )

    loads = [
        pltpu.make_async_copy(vel, W.at[pl.ds(0, 3), pl.ds(1, CX), own_z, :], in_sem.at[0]),
        pltpu.make_async_copy(prs, W.at[3, pl.ds(1, CX), own_z, :], in_sem.at[1]),
    ]
    small = [
        pltpu.make_async_copy(source, here, in_sem.at[2 + i])
        for i, (source, here) in enumerate(
            (
                (own_h, own_r),
                (line_h, line_r),
                (turb_h, turb_r),
                (cnt_h, cnt),
                (kern_h, kern),
                (thrust_h, thrust),
                (infx_h, infx),
                (infy_h, infy),
            )
        )
    ]
    for load in small + loads:
        load.start()
    barrier = pltpu.get_barrier_semaphore()

    @pl.loop(1, plane)
    def _(r):
        pl.semaphore_signal(barrier, inc=1, device_id=plane_peer(r), device_id_type=MESH)

    @pl.loop(1, NGX)
    def _(r):
        pl.semaphore_signal(barrier, inc=1, device_id=line_peer(r), device_id_type=MESH)

    greeted = plane - 1 + NGX - 1
    for d in DIRS:
        if d[0] and (d[1] or d[2]):
            pl.semaphore_signal(barrier, inc=1, device_id=near(*d), device_id_type=MESH)
            greeted += 1

    for load in small:
        load.wait()
    owner = own_r[...]
    live = lanes((1, rows)) < cnt[...]
    spot = jnp.where(live, (owner % NGY) * NGX + owner // NGY, -1)
    land = (rows_of((peers, rows)) == spot).astype(F32)
    before = (rows_of((rows, rows)) < lanes((rows, rows))).astype(BF16)
    earlier = jnp.dot(land.astype(BF16), before, preferred_element_type=F32)
    rank = jnp.sum(land * earlier, axis=0, keepdims=True).astype(jnp.int32)
    slot = jnp.where(live, spot * CAP + rank, -1)
    place = (rows_of((slots, rows)) == slot).astype(BF16)
    hi, mid, lo = pieces(kern[...])
    both = jnp.dot(place, jnp.concatenate([hi, mid], axis=1), preferred_element_type=F32)
    sorted_rows = both[:, :L] + both[:, L:]
    sorted_rows = sorted_rows + jnp.dot(place, lo, preferred_element_type=F32)
    kind = rows_of((L, rows))
    line = line_r[...]
    told = jnp.where(kind < 8, line // 32, jnp.where(kind < 16, line % 32, turb_r[...]))
    told = jnp.where((kind % 8 == rank) & (kind < 24), told, 0).astype(F32).astype(BF16)
    meta = lax.dot_general(
        land.astype(BF16), told, (((1,), (1,)), ((), ())), preferred_element_type=F32
    )
    for k in range(NGY):
        S1[k, : NGX * CAP, :] = sorted_rows[k * NGX * CAP : (k + 1) * NGX * CAP]
        S1[k, NGX * CAP :, :] = meta[k * NGX : (k + 1) * NGX]
    TB[...] = jnp.zeros_like(TB)
    TB[0, 0:1, :T] = infx[...].astype(F32)
    TB[1, 0:1, :T] = infy[...].astype(F32)
    TB[2, 0:1, :T] = thrust[...]
    for load in loads:
        load.wait()
    pl.semaphore_wait(barrier, greeted)

    def row_first(r):
        peer = lax.rem(gy + r, NGY)
        return remote(
            S1.at[peer], R1.at[r - 1], row_send.at[r - 1], row_recv.at[r - 1], (gx, peer, gz)
        )

    for r in range(1, NGY):
        row_first(r).start()
    R1[NGY - 1] = S1[gy]

    lane = lanes((CZ, L))

    def face_copies(step):
        nc = 4 if step == 0 else 3
        comps = pl.ds(0, nc)
        many = pl.ds(0, nc * CX)
        return [
            remote(
                W.at[comps, pl.ds(CX, 1), own_z, :],
                W.at[comps, pl.ds(0, 1), own_z, :],
                face_send.at[0],
                face_recv.at[0],
                near(1, 0, 0),
            ),
            remote(
                W.at[comps, pl.ds(1, 1), own_z, :],
                W.at[comps, pl.ds(CX + 1, 1), own_z, :],
                face_send.at[1],
                face_recv.at[1],
                near(-1, 0, 0),
            ),
            remote(wys, wyr.at[0], face_send.at[2], face_recv.at[2], near(0, 1, 0)),
            remote(wys, wyr.at[1], face_send.at[3], face_recv.at[3], near(0, -1, 0)),
            remote(
                wzs.at[1, many], wzr.at[0, many], face_send.at[4], face_recv.at[4], near(0, 0, 1)
            ),
            remote(
                wzs.at[0, many], wzr.at[1, many], face_send.at[5], face_recv.at[5], near(0, 0, -1)
            ),
        ]

    def turn(cells, by):
        return pltpu.roll(cells, by % L, 1) if by % L else cells

    def edge_lanes(q):
        return (lane == 2 * q) | (lane == (2 * q + L - 1) % L)

    def send_faces(step):
        nc = 4 if step == 0 else 3
        copies = face_copies(step)
        copies[0].start()
        copies[1].start()
        for c in range(nc):
            wzs[0, c * CX : (c + 1) * CX, :] = W[c, 1 : CX + 1, D, :]
            wzs[1, c * CX : (c + 1) * CX, :] = W[c, 1 : CX + 1, D + CZ - 1, :]
        copies[4].start()
        copies[5].start()
        packed = jnp.zeros((CZ, L), F32)
        for c in range(nc):

            for x in range(CX):
                q = c * CX + x
                turned = pltpu.roll(W[c, 1 + x, own_z, :], 2 * q, 1) if q else W[c, 1, own_z, :]
                packed = jnp.where(edge_lanes(q), turned, packed)
        wys[...] = packed
        copies[2].start()
        copies[3].start()
        return copies

    def merged(received):
        right = jnp.where(gy < NGY - 1, received[1], 0.0)
        left = jnp.where(gy > 0, received[0], 0.0)
        return jnp.where(lane % 2 == 0, right, pltpu.roll(left, 2, 1))

    def wait_faces(step, copies):
        nc = 4 if step == 0 else 3
        for copy in copies:
            copy.wait()
        E[...] = merged(wyr)
        for c in range(nc):
            W[c, 0, own_z, :] = jnp.where(gx > 0, W[c, 0, own_z, :], 0.0)
            W[c, CX + 1, own_z, :] = jnp.where(gx < NGX - 1, W[c, CX + 1, own_z, :], 0.0)
            above = jnp.where(gz > 0, wzr[0, c * CX : (c + 1) * CX, :], 0.0)
            below = jnp.where(gz < NGZ - 1, wzr[1, c * CX : (c + 1) * CX, :], 0.0)
            W[c, 1 : CX + 1, D - 1, :] = above
            W[c, 1 : CX + 1, D + CZ, :] = below

    def sides(cells, edge):
        left = jnp.where(lane == 0, edge, pltpu.roll(cells, 1, 1))
        right = jnp.where(lane == L - 1, edge, pltpu.roll(cells, L - 1, 1))
        return left, right

    def edge_of(ref, q):
        return pltpu.roll(ref[...], (2 * L - 1 - 2 * q) % L, 1)

    def star_faces(step):
        nc = 4 if step == 0 else 3
        for c in range(nc):

            @pl.loop(0, CX, unroll=8)
            def _(x):
                cells = W[c, 1 + x, own_z, :]
                left, right = sides(cells, edge_of(E, c * CX + x))
                total = W[c, x, own_z, :] + W[c, x + 2, own_z, :]
                total = total + W[c, 1 + x, pl.ds(D - 1, CZ), :] + W[c, 1 + x, pl.ds(D + 1, CZ), :]
                total = total + left + right
                if c < 3:
                    ST[c, 1 + x, own_z, :] = 0.88 * cells + 0.02 * total
                else:
                    R[x] = total

        copies = [
            remote(
                ST.at[0, CX, own_z, :],
                ST.at[0, 0, own_z, :],
                star_send.at[0],
                star_recv.at[0],
                near(1, 0, 0),
            ),
            remote(
                ST.at[0, 1, own_z, :],
                ST.at[0, CX + 1, own_z, :],
                star_send.at[1],
                star_recv.at[1],
                near(-1, 0, 0),
            ),
            remote(sys_, syr.at[0], star_send.at[2], star_recv.at[2], near(0, 1, 0)),
            remote(sys_, syr.at[1], star_send.at[3], star_recv.at[3], near(0, -1, 0)),
            remote(szs.at[1], szr.at[0], star_send.at[4], star_recv.at[4], near(0, 0, 1)),
            remote(szs.at[0], szr.at[1], star_send.at[5], star_recv.at[5], near(0, 0, -1)),
        ]
        copies[0].start()
        copies[1].start()
        szs[0] = ST[2, 1 : CX + 1, D, :]
        szs[1] = ST[2, 1 : CX + 1, D + CZ - 1, :]
        copies[4].start()
        copies[5].start()

        packed = jnp.zeros((CZ, L), F32)
        for x in range(CX):
            turned = pltpu.roll(ST[1, 1 + x, own_z, :], 2 * x, 1) if x else ST[1, 1, own_z, :]
            packed = jnp.where(edge_lanes(x), turned, packed)
        sys_[...] = packed
        copies[2].start()
        copies[3].start()
        return copies

    def around(j):
        return (lane + (8 - 16 * j) % L) % L < 16

    def sources(step, copies):
        for copy in copies:
            copy.wait()
        E2[...] = merged(syr)
        ST[0, 0, own_z, :] = jnp.where(gx > 0, ST[0, 0, own_z, :], 0.0)
        ST[0, CX + 1, own_z, :] = jnp.where(gx < NGX - 1, ST[0, CX + 1, own_z, :], 0.0)
        ST[2, 1 : CX + 1, D - 1, :] = jnp.where(gz > 0, szr[0], 0.0)
        ST[2, 1 : CX + 1, D + CZ, :] = jnp.where(gz < NGZ - 1, szr[1], 0.0)
        for group in range(NG):

            kept = [jnp.zeros((CZ, L), F32), jnp.zeros((CZ, L), F32)]
            for j in range(8):
                x = group * 8 + j
                left, right = sides(ST[1, 1 + x, own_z, :], edge_of(E2, x))
                total = ST[0, x + 2, own_z, :] - ST[0, x, own_z, :] + right - left
                total = total + ST[2, 1 + x, pl.ds(D + 1, CZ), :]
                source = 0.5 * (total - ST[2, 1 + x, pl.ds(D - 1, CZ), :])
                first = R[x] - source
                GS[step, 0, D + x, own_z, :] = first
                GS[step, 1, D + x, own_z, :] = source
                mine = around(j)
                kept[0] = jnp.where(mine, turn(first, 16 * j), kept[0])
                kept[1] = jnp.where(mine, turn(source, 16 * j), kept[1])
            gys[0, group] = kept[0]
            gys[1, group] = kept[1]

    def deep_copies(cells, off, packed, received, send, recv):
        fields = pl.ds(0, packed.shape[0])
        copies = []
        for i, (dx, dy, dz) in enumerate(DIRS):
            if dy == 0:
                zs, zd = {
                    0: (own_z, own_z),
                    -1: (pl.ds(D, D), pl.ds(D + CZ, D)),
                    1: (pl.ds(CZ, D), pl.ds(0, D)),
                }[dz]
                deep = off if dz == 0 else D
                xs, xd = {
                    0: (pl.ds(off, CX), pl.ds(off, CX)),
                    -1: (pl.ds(off, deep), pl.ds(off + CX, deep)),
                    1: (pl.ds(off + CX - deep, deep), pl.ds(off - deep, deep)),
                }[dx]
                src = cells.at[fields, xs, zs, :]
                dst = cells.at[fields, xd, zd, :]
            else:
                zs, zd = {
                    0: (pl.ds(0, CZ), own_z),
                    -1: (pl.ds(0, D), pl.ds(D + CZ, D)),
                    1: (pl.ds(CZ - D, D), pl.ds(0, D)),
                }[dz]
                xs, xd = {
                    0: (pl.ds(0, NG), pl.ds(1, NG)),
                    -1: (pl.ds(0, 1), pl.ds(NG + 1, 1)),
                    1: (pl.ds(NG - 1, 1), pl.ds(0, 1)),
                }[dx]
                src = packed.at[fields, xs, zs, :]
                dst = received.at[0 if dy == 1 else 1, fields, xd, zd, :]
            copies.append(remote(src, dst, send.at[i], recv.at[i], near(dx, dy, dz)))
        return copies

    lane_z = lanes((Z, L))

    def unpack(received, field, target, base):
        @pl.loop(0, NG + 2)
        def _(group):
            both_sides = jnp.where(
                lane_z % 16 < 8, received[1, field, group], received[0, field, group]
            )
            for j in range(8):
                target[base + group * 8 + j] = turn(both_sides, -16 * j)

    def one_wait(whole_src, whole_dst, send, recv, device):
        remote(whole_src, whole_dst, send, recv, device).wait()

    def inflow_first(step):
        column = jnp.sum(W[0, 1 : CX + 1, own_z, :], axis=1)
        y = rows_of((L, L)) + gy * L
        begin = TB[1, 0:1, :].astype(jnp.int32)
        band = ((y >= begin) & (y < begin + BAND)).astype(F32)
        sums = jnp.dot(column, band, precision=lax.Precision.HIGHEST, preferred_element_type=F32)
        x = rows_of((CX, L)) + gx * CX
        picked = jnp.where(x == TB[0, 0:1, :].astype(jnp.int32), sums, 0.0)
        u1s[step] = jnp.broadcast_to(jnp.sum(picked, axis=0, keepdims=True), (8, L))

        @pl.loop(1, plane)
        def _(r):
            remote(
                u1s.at[step],
                u1r.at[step, r - 1],
                u_send.at[2 * step],
                u_recv.at[2 * step],
                plane_peer(r),
            ).start()

    def inflow_second(step):
        whole = u1r.at[step]
        one_wait(whole, whole, u_send.at[2 * step], u_recv.at[2 * step], plane_peer(1))
        u2s[step] = u1s[step] + jnp.sum(u1r[step], axis=0)

        @pl.loop(1, NGX)
        def _(r):
            remote(
                u2s.at[step],
                u2r.at[step, r - 1],
                u_send.at[2 * step + 1],
                u_recv.at[2 * step + 1],
                line_peer(r),
            ).start()

    def magnitudes(step):
        whole = u2r.at[step]
        one_wait(whole, whole, u_send.at[2 * step + 1], u_recv.at[2 * step + 1], line_peer(1))
        total = u2s[step] + jnp.sum(u2r[step], axis=0)
        uref = total[0:1] * (1.0 / (BAND * CZ * NGZ))
        return 0.5 * TB[2, 0:1, :] * uref * jnp.abs(uref)

    def forces(step):
        size = magnitudes(step)

        @pl.loop(0, NGX, unroll=4)
        def _(g):
            at = pl.ds(pl.multiple_of(g * CAP * NGY, CAP * NGY), CAP * NGY)
            hot = jnp.where(TC[at, :] == lanes((CAP * NGY, L)).astype(F32), size, 0.0)
            scaled = R2[g, : CAP * NGY, :] * jnp.sum(hot, axis=1, keepdims=True)
            top = scaled.astype(BF16)
            KC[at, :L] = top
            KC[at, L:] = (scaled - top.astype(F32)).astype(BF16)

        part = CX // 4
        for h in range(4):
            both = jnp.dot(
                O[h * part * CZ : (h + 1) * part * CZ, :], KC[...], preferred_element_type=F32
            )
            force = (both[:, :L] + both[:, L:]).reshape(part, CZ, L)
            F[0, D + 1 + h * part : D + 1 + (h + 1) * part, own_z, :] = force
        for group in range(NG):

            kept = jnp.zeros((CZ, L), F32)
            for j in range(8):
                turned = turn(F[0, D + 1 + group * 8 + j, own_z, :], 16 * j)
                kept = jnp.where(around(j), turned, kept)
            fys[0, group] = kept
        copies = deep_copies(F, D + 1, fys, fyr, f_send, f_recv)
        for copy in copies:
            copy.start()
        return copies

    def inside(x):
        spot_x = gx * CX + x - D
        return (spot_x >= 0) & (spot_x < NGX * CX)

    ringlane = lanes((8, L))[0:1]
    right_ok = jnp.where(gy < NGY - 1, 1.0, 0.0)
    left_ok = jnp.where(gy > 0, 1.0, 0.0)
    ring = jnp.where(ringlane < D, right_ok, jnp.where(ringlane >= L - D, left_ok, 0.0))
    top_ok = jnp.where(gz > 0, 1.0, 0.0)
    bottom_ok = jnp.where(gz < NGZ - 1, 1.0, 0.0)

    def weights():
        out = []
        for start, size in CHUNKS:
            scale = 1.0 / 6.0
            if start == 0:
                scale = scale * top_ok
            if start + size == Z:
                scale = scale * bottom_ok
            out.append((scale, ring * scale))
        return out

    def outside_x(pp):
        for ok, x in ((gx > 0, D), (gx < NGX - 1, D + CX + 1)):

            @pl.when(jnp.logical_not(ok))
            def _():
                for ab in range(2):
                    PR[pp, ab, x, 8 : 8 + Z, :] = jnp.zeros((Z, L), F32)

    def beside(a, b):
        both = jnp.concatenate([a, b], axis=-1).reshape(-1, 2 * L)
        top = both.astype(BF16)
        rest = (both - top.astype(F32)).astype(BF16)
        total = jnp.dot(top, RING[...], preferred_element_type=F32)
        total = total + jnp.dot(rest, RING[...], preferred_element_type=F32)
        return total[:, :L].reshape(a.shape), total[:, L:].reshape(a.shape)

    def ring_sides(a, b):
        axis, lane_c = a.ndim - 1, lanes(a.shape)
        am, bm = pltpu.roll(a, 1, axis), pltpu.roll(b, 1, axis)
        ap, bp = pltpu.roll(a, L - 1, axis), pltpu.roll(b, L - 1, axis)
        first, last = lane_c == 0, lane_c == L - 1
        return (
            (jnp.where(first, bm, am), jnp.where(last, bp, ap)),
            (jnp.where(first, am, bm), jnp.where(last, ap, bp)),
        )

    def sweeps(step, f_copies):
        for copy in f_copies:
            copy.wait()

        unpack(fyr, 0, BF, 1)
        scales = weights()

        @pl.loop(0, X, unroll=4)
        def _(x):
            plus = jnp.where(inside(x + 1), -0.2, 0.0)
            minus = jnp.where(inside(x - 1), -0.2, 0.0)
            for (start, size), (ca, cb) in zip(CHUNKS, scales):
                at = pl.ds(start, size)
                to = pl.ds(start + 8, size)
                fa = plus * F[0, x + 2, at, :] - minus * F[0, x, at, :]
                fb = plus * BF[x + 2, at, :] - minus * BF[x, at, :]
                S[0, x, at, :] = GS[step, 1, x, at, :] + fa
                S[1, x, at, :] = BGS[1, x, at, :] + fb
                PR[0, 0, x + 1, to, :] = (GS[step, 0, x, at, :] - fa) * ca
                PR[0, 1, x + 1, to, :] = (BGS[0, x, at, :] - fb) * cb

        outside_x(0)
        for k in range(2, SWEEPS + 1):
            src, dst = k % 2, (k + 1) % 2
            wide = -(-(CX + 2 * (SWEEPS + 1 - k)) // BLOCK) * BLOCK
            begin = (X - wide) // 2

            @pl.loop(0, wide // BLOCK, unroll=True)
            def _(block):
                x = begin + block * BLOCK
                mid, back, ahead = pl.ds(x + 1, BLOCK), pl.ds(x, BLOCK), pl.ds(x + 2, BLOCK)
                along = beside(PR[src, 0, mid, 8 : 8 + Z, :], PR[src, 1, mid, 8 : 8 + Z, :])
                for (start, size), (ca, cb) in zip(CHUNKS, scales):
                    at = pl.ds(start + 8, size)
                    up = pl.ds(start + 7, size)
                    down = pl.ds(start + 9, size)
                    for ab, scale in ((0, ca), (1, cb)):
                        total = PR[src, ab, back, at, :] + PR[src, ab, ahead, at, :]
                        total = total + PR[src, ab, mid, up, :] + PR[src, ab, mid, down, :]
                        total = total - S[ab, pl.ds(x, BLOCK), pl.ds(start, size), :]
                        total = total + along[ab][:, start : start + size]
                        PR[dst, ab, mid, at, :] = total * scale

            outside_x(dst)

        at = pl.ds(D + 8, CZ)
        last = (SWEEPS + 1) % 2

        @pl.loop(0, CX, unroll=4)
        def _(x):
            deep = D + x + 1
            (left, right), _ = ring_sides(PR[last, 0, deep, at, :], PR[last, 1, deep, at, :])
            back, ahead = PR[last, 0, deep - 1, at, :], PR[last, 0, deep + 1, at, :]
            up = PR[last, 0, deep, pl.ds(D + 7, CZ), :]
            down = PR[last, 0, deep, pl.ds(D + 9, CZ), :]
            force = F[0, D + 1 + x, own_z, :]
            W[0, 1 + x, own_z, :] = ST[0, 1 + x, own_z, :] - 0.4 * force - 0.5 * (ahead - back)
            W[1, 1 + x, own_z, :] = ST[1, 1 + x, own_z, :] - 0.5 * (right - left)
            W[2, 1 + x, own_z, :] = ST[2, 1 + x, own_z, :] - 0.5 * (down - up)
            if step == 0:
                R[x] = back + ahead + up + down + left + right

    def unpack_sources(step, copies):
        for copy in copies:
            copy.wait()
        for field in range(2):
            unpack(gyr.at[step], field, BGS.at[field], 0)

    def row_second():
        for r in range(1, NGY):
            row_first(r).wait()

        @pl.loop(0, NGX)
        def _(d):
            for k in range(NGY):
                at = pl.ds(pl.multiple_of(d * CAP, CAP), CAP)
                S2[d, k * CAP : (k + 1) * CAP, :] = R1[k, at, :]
                S2[d, NGY * CAP + k : NGY * CAP + k + 1, :] = R1[k, pl.ds(NGX * CAP + d, 1), :]

        @pl.loop(1, NGX)
        def _(r):
            peer = lax.rem(gx + r, NGX)
            remote(
                S2.at[peer], R2.at[r - 1], row_send.at[NGY], row_recv.at[NGY], (peer, gy, gz)
            ).start()

        R2[NGX - 1] = S2[gx]

    def row_last():
        whole = R2.at[pl.ds(0, NGX - 1)]
        one_wait(whole, whole, row_send.at[NGY], row_recv.at[NGY], line_peer(1))
        which = lanes((CAP, L)) - rows_of((CAP, L))

        @pl.loop(0, NGX, unroll=4)
        def _(g):
            for k in range(NGY):
                row = R2[g, NGY * CAP + k : NGY * CAP + k + 1, :]
                told_line = jnp.where(which == 0, 32.0 * row, jnp.where(which == 8, row, 0.0))
                told_turbine = jnp.where(which == 16, row, 0.0)
                at = pl.ds(pl.multiple_of((g * NGY + k) * CAP, CAP), CAP)
                LC[at, :] = jnp.broadcast_to(
                    jnp.sum(told_line, axis=1, keepdims=True), (CAP, L)
                )
                TC[at, :] = jnp.broadcast_to(
                    jnp.sum(told_turbine, axis=1, keepdims=True), (CAP, L)
                )

        wide = min(L, slots)
        same = rows_of((wide, wide)) == lanes((wide, wide))
        for c in range(slots // wide):
            turned = jnp.where(same, LC[c * wide : (c + 1) * wide, :wide], 0.0)
            named = jnp.sum(turned, axis=0, keepdims=True).astype(jnp.int32)

            @pl.loop(0, CX)
            def _(x):
                at = pl.ds(pl.multiple_of(x * CZ, CZ), CZ)
                hit = rows_of((CZ, wide)) + x * CZ == named
                O[at, c * wide : (c + 1) * wide] = hit.astype(F32).astype(BF16)

    def constants():
        zero_pad = jnp.zeros((8, L), F32)
        for pp in range(2):
            for ab in range(2):

                @pl.loop(0, X + 2, unroll=X + 2)
                def _(x):
                    PR[pp, ab, x, 0:8, :] = zero_pad
                    PR[pp, ab, x, Z + 8 : Z + 16, :] = zero_pad

                PR[pp, ab, 0, :, :] = jnp.zeros((Z + 16, L), F32)
                PR[pp, ab, X + 1, :, :] = jnp.zeros((Z + 16, L), F32)

        BF[0, :, :] = jnp.zeros((Z, L), F32)
        BF[X + 1, :, :] = jnp.zeros((Z, L), F32)
        step_apart = lax.rem(rows_of((2 * L, 2 * L)) - lanes((2 * L, 2 * L)) + 2 * L, 2 * L)
        RING[...] = ((step_apart == 1) | (step_apart == 2 * L - 1)).astype(F32).astype(BF16)

    for step in range(STEPS):
        faces = send_faces(step)
        inflow_first(step)
        if step == 0:
            constants()
        wait_faces(step, faces)
        stars = star_faces(step)
        if step == 0:
            row_second()
        inflow_second(step)
        sources(step, stars)
        deep = deep_copies(GS.at[step], D, gys, gyr.at[step], gs_send.at[step], gs_recv.at[step])
        for copy in deep:
            copy.start()
        if step == 0:
            row_last()
        f_copies = forces(step)
        unpack_sources(step, deep)
        sweeps(step, f_copies)

    last = (SWEEPS + 1) % 2
    outs = [
        pltpu.make_async_copy(W.at[pl.ds(0, 3), pl.ds(1, CX), own_z, :], vout, in_sem.at[0]),
        pltpu.make_async_copy(
            PR.at[last, 0, pl.ds(D + 1, CX), pl.ds(D + 8, CZ), :], pout, in_sem.at[1]
        ),
    ]
    for out in outs:
        out.start()
    for out in outs:
        out.wait()


def deliver(vel, prs, vout, pout, held, load_sem, store_sem):
    half = prs.shape[0] // 2
    loads, stores = [], []
    for k in range(8):
        at = pl.ds(k % 2 * half, half)
        source, target = (vel.at[k // 2, at], vout.at[k // 2, at])
        if k >= 6:
            source, target = prs.at[at], pout.at[at]
        loads.append(pltpu.make_async_copy(source, held.at[k], load_sem.at[k]))
        stores.append(pltpu.make_async_copy(held.at[k], target, store_sem.at[k]))
    for load in loads:
        load.start()
    for load, store in zip(loads, stores):
        load.wait()
        store.start()
    for store in stores:
        store.wait()


def body(
    shape,
    velocity,
    pressure,
    kern,
    owners,
    lines,
    point_turbine,
    row_counts,
    thrust,
    inflow_x,
    inflow_y,
):
    ngx, ngy, ngz = shape
    cx, cz = velocity.shape[1:3]
    z, x, ng = cz + 2 * D, cx + 2 * D, cx // 8
    rows = kern.shape[0]
    slots = ngx * ngy * CAP
    turbines = thrust.shape[0]
    any_spec = pl.BlockSpec(memory_space=pl.ANY)
    vm = pltpu.VMEM
    dma = pltpu.SemaphoreType.DMA
    meta = max(8, ngy)
    i32 = jnp.int32
    scratch = [
        vm((rows, L), F32),
        vm((1, rows), i32),
        vm((1, rows), i32),
        vm((1, rows), i32),
        vm((1, 1), i32),
        vm((1, turbines), F32),
        vm((1, turbines), i32),
        vm((1, turbines), i32),
        vm((4, cx + 2, z, L), F32),
        vm((cz, L), F32),
        vm((2, cz, L), F32),
        vm((2, 4 * cx, L), F32),
        vm((2, 4 * cx, L), F32),
        vm((cz, L), F32),
        vm((3, cx + 2, z, L), F32),
        vm((cz, L), F32),
        vm((2, cz, L), F32),
        vm((2, cx, L), F32),
        vm((2, cx, L), F32),
        vm((cz, L), F32),
        vm((cx, cz, L), F32),
        vm((STEPS, 2, x, z, L), F32),
        vm((2, ng, cz, L), F32),
        vm((STEPS, 2, 2, ng + 2, z, L), F32),
        vm((2, x, z, L), F32),
        vm((1, x + 2, z, L), F32),
        vm((1, ng, cz, L), F32),
        vm((2, 1, ng + 2, z, L), F32),
        vm((x + 2, z, L), F32),
        vm((2, x, z, L), F32),
        vm((2, 2, x + 2, z + 16, L), F32),
        vm((ngy, ngx * CAP + ngx, L), F32),
        vm((ngy, ngx * CAP + ngx, L), F32),
        vm((ngx, ngy * CAP + meta, L), F32),
        vm((ngx, ngy * CAP + meta, L), F32),
        vm((slots, L), F32),
        vm((slots, L), F32),
        vm((cx * cz, slots), BF16),
        vm((slots, 2 * L), BF16),
        vm((3, 8, L), F32),
        vm((2 * L, 2 * L), BF16),
        vm((STEPS, 8, L), F32),
        vm((STEPS, ngy * ngz - 1, 8, L), F32),
        vm((STEPS, 8, L), F32),
        vm((STEPS, ngx - 1, 8, L), F32),
        dma((10,)),
        dma((6,)),
        dma((6,)),
        dma((6,)),
        dma((6,)),
        dma((STEPS, 26)),
        dma((STEPS, 26)),
        dma((26,)),
        dma((26,)),
        dma((ngy + 1,)),
        dma((ngy + 1,)),
        dma((2 * STEPS,)),
        dma((2 * STEPS,)),
    ]
    ahead = pl.pallas_call(
        functools.partial(kernel, (ngx, ngy, ngz, cx, cz)),
        out_shape=(
            jax.ShapeDtypeStruct(velocity.shape, F32),
            jax.ShapeDtypeStruct(pressure.shape, F32),
        ),
        in_specs=[pl.BlockSpec(memory_space=pltpu.HBM)] * 10,
        out_specs=(any_spec, any_spec),
        scratch_shapes=scratch,
        compiler_params=pltpu.CompilerParams(
            collective_id=0, has_side_effects=True, vmem_limit_bytes=56 * 1024 * 1024
        ),
    )(
        velocity,
        pressure,
        kern,
        owners.reshape(1, rows),
        lines.reshape(1, rows),
        point_turbine.reshape(1, rows),
        row_counts.reshape(1, 1),
        thrust.reshape(1, turbines),
        inflow_x.reshape(1, turbines),
        inflow_y.reshape(1, turbines),
    )
    return pl.pallas_call(
        deliver,
        out_shape=(
            jax.ShapeDtypeStruct(velocity.shape, F32),
            jax.ShapeDtypeStruct(pressure.shape, F32),
        ),
        in_specs=[any_spec] * 2,
        out_specs=(any_spec, any_spec),
        scratch_shapes=[vm((8, cx // 2, cz, L), F32), dma((8,)), dma((8,))],
        compiler_params=pltpu.CompilerParams(vmem_limit_bytes=60 * 1024 * 1024),
    )(*ahead)


def solution(mesh):
    placed = (
        P(None, "gx", "gz", "gy"),
        P("gx", "gz", "gy"),
        P(("gx", "gy", "gz"), None),
        P(("gx", "gy", "gz"), None),
        P(("gx", "gy", "gz")),
        P(("gx", "gy", "gz")),
        P("gx", "gy", "gz"),
        P(),
        P(),
        P(),
    )
    shape = (mesh.shape["gx"], mesh.shape["gy"], mesh.shape["gz"])
    return jax.shard_map(
        functools.partial(body, shape),
        mesh=mesh,
        in_specs=placed,
        out_specs=(P(None, "gx", "gz", "gy"), P("gx", "gz", "gy")),
        check_vma=False,
    )
```

```python
import functools

import jax
import jax.numpy as jnp
from jax import lax
from jax.experimental import pallas as pl
from jax.experimental.pallas import tpu as pltpu
from jax.sharding import PartitionSpec as P

BAND = 32
STEPS = 2
SWEEPS = 8
CAP = 8
L = 128
D = 8
BLOCK = 4
MESH = pl.DeviceIdType.MESH
CHUNKS = ((0, 8), (8, 16), (24, 16), (40, 16), (56, 8))
F32 = jnp.float32
BF16 = jnp.bfloat16
DIRS = tuple(
    sorted(
        (
            (dx, dy, dz)
            for dx in (-1, 0, 1)
            for dy in (-1, 0, 1)
            for dz in (-1, 0, 1)
            if (dx, dy, dz) != (0, 0, 0)
        ),
        key=lambda d: (abs(d[1]), abs(d[2]), -abs(d[0])),
    )
)


def lanes(shape):
    return lax.broadcasted_iota(jnp.int32, shape, len(shape) - 1)


def rows_of(shape):
    return lax.broadcasted_iota(jnp.int32, shape, len(shape) - 2)


def pieces(x):
    hi = x.astype(BF16)
    rest = x - hi.astype(F32)
    mid = rest.astype(BF16)
    return hi, mid, (rest - mid.astype(F32)).astype(BF16)


def kernel(
    sizes,
    vel,
    prs,
    kern_h,
    own_h,
    line_h,
    turb_h,
    cnt_h,
    thrust_h,
    infx_h,
    infy_h,
    vout,
    pout,
    kern,
    own_r,
    line_r,
    turb_r,
    cnt,
    thrust,
    infx,
    infy,
    W,
    wys,
    wyr,
    wzs,
    wzr,
    E,
    ST,
    sys_,
    syr,
    szs,
    szr,
    E2,
    R,
    GS,
    gys,
    gyr,
    BGS,
    F,
    fys,
    fyr,
    BF,
    S,
    PR,
    S1,
    R1,
    S2,
    R2,
    LC,
    TC,
    O,
    KC,
    TB,
    RING,
    u1s,
    u1r,
    u2s,
    u2r,
    in_sem,
    face_send,
    face_recv,
    star_send,
    star_recv,
    gs_send,
    gs_recv,
    f_send,
    f_recv,
    row_send,
    row_recv,
    u_send,
    u_recv,
):
    NGX, NGY, NGZ, CX, CZ = sizes
    Z = CZ + 2 * D
    X = CX + 2 * D
    NG = CX // 8
    T = thrust.shape[1]
    rows = kern.shape[0]
    peers = NGX * NGY
    slots = peers * CAP
    plane = NGY * NGZ
    gx = lax.axis_index("gx")
    gy = lax.axis_index("gy")
    gz = lax.axis_index("gz")
    own_z = pl.ds(D, CZ)

    def near(dx, dy, dz):
        return (
            lax.rem(gx + dx + NGX, NGX),
            lax.rem(gy + dy + NGY, NGY),
            lax.rem(gz + dz + NGZ, NGZ),
        )

    def plane_peer(r):
        spot = lax.rem(gy * NGZ + gz + r, plane)
        return (gx, spot // NGZ, lax.rem(spot, NGZ))

    def line_peer(r):
        return (lax.rem(gx + r, NGX), gy, gz)

    def remote(src, dst, send, recv, device):
        return pltpu.make_async_remote_copy(
            src_ref=src,
            dst_ref=dst,
            send_sem=send,
            recv_sem=recv,
            device_id=device,
            device_id_type=MESH,
        )

    loads = [
        pltpu.make_async_copy(vel, W.at[pl.ds(0, 3), pl.ds(1, CX), own_z, :], in_sem.at[0]),
        pltpu.make_async_copy(prs, W.at[3, pl.ds(1, CX), own_z, :], in_sem.at[1]),
    ]
    small = [
        pltpu.make_async_copy(source, here, in_sem.at[2 + i])
        for i, (source, here) in enumerate(
            (
                (own_h, own_r),
                (line_h, line_r),
                (turb_h, turb_r),
                (cnt_h, cnt),
                (kern_h, kern),
                (thrust_h, thrust),
                (infx_h, infx),
                (infy_h, infy),
            )
        )
    ]
    for load in small + loads:
        load.start()
    barrier = pltpu.get_barrier_semaphore()

    @pl.loop(1, plane)
    def _(r):
        pl.semaphore_signal(barrier, inc=1, device_id=plane_peer(r), device_id_type=MESH)

    @pl.loop(1, NGX)
    def _(r):
        pl.semaphore_signal(barrier, inc=1, device_id=line_peer(r), device_id_type=MESH)

    greeted = plane - 1 + NGX - 1
    for d in DIRS:
        if d[0] and (d[1] or d[2]):
            pl.semaphore_signal(barrier, inc=1, device_id=near(*d), device_id_type=MESH)
            greeted += 1

    for load in small:
        load.wait()
    owner = own_r[...]
    live = lanes((1, rows)) < cnt[...]
    spot = jnp.where(live, (owner % NGY) * NGX + owner // NGY, -1)
    land = (rows_of((peers, rows)) == spot).astype(F32)
    before = (rows_of((rows, rows)) < lanes((rows, rows))).astype(BF16)
    earlier = jnp.dot(land.astype(BF16), before, preferred_element_type=F32)
    rank = jnp.sum(land * earlier, axis=0, keepdims=True).astype(jnp.int32)
    slot = jnp.where(live, spot * CAP + rank, -1)
    place = (rows_of((slots, rows)) == slot).astype(BF16)
    hi, mid, lo = pieces(kern[...])
    both = jnp.dot(place, jnp.concatenate([hi, mid], axis=1), preferred_element_type=F32)
    sorted_rows = both[:, :L] + both[:, L:]
    sorted_rows = sorted_rows + jnp.dot(place, lo, preferred_element_type=F32)
    kind = rows_of((L, rows))
    line = line_r[...]
    told = jnp.where(kind < 8, line // 32, jnp.where(kind < 16, line % 32, turb_r[...]))
    told = jnp.where((kind % 8 == rank) & (kind < 24), told, 0).astype(F32).astype(BF16)
    meta = lax.dot_general(
        land.astype(BF16), told, (((1,), (1,)), ((), ())), preferred_element_type=F32
    )
    hx = NGX // 2
    for k in range(NGY):
        for h in range(2):
            first = k * NGX + h * hx
            S1[k, h, : hx * CAP, :] = sorted_rows[first * CAP : (first + hx) * CAP]
            S1[k, h, hx * CAP :, :] = meta[first : first + hx]
    TB[...] = jnp.zeros_like(TB)
    TB[0, 0:1, :T] = infx[...].astype(F32)
    TB[1, 0:1, :T] = infy[...].astype(F32)
    TB[2, 0:1, :T] = thrust[...]
    for load in loads:
        load.wait()
    pl.semaphore_wait(barrier, greeted)

    def row_first(r, h):
        peer = lax.rem(gy + r, NGY)
        i = 2 * (r - 1) + h
        return remote(
            S1.at[peer, h], R1.at[r - 1, h], row_send.at[i], row_recv.at[i], (gx, peer, gz)
        )

    for h in range(2):
        for r in range(1, NGY):
            row_first(r, h).start()
    R1[NGY - 1] = S1[gy]

    lane = lanes((CZ, L))

    def face_copies(step):
        nc = 4 if step == 0 else 3
        comps = pl.ds(0, nc)
        many = pl.ds(0, nc * CX)
        return [
            remote(
                W.at[comps, pl.ds(CX, 1), own_z, :],
                W.at[comps, pl.ds(0, 1), own_z, :],
                face_send.at[0],
                face_recv.at[0],
                near(1, 0, 0),
            ),
            remote(
                W.at[comps, pl.ds(1, 1), own_z, :],
                W.at[comps, pl.ds(CX + 1, 1), own_z, :],
                face_send.at[1],
                face_recv.at[1],
                near(-1, 0, 0),
            ),
            remote(wys, wyr.at[0], face_send.at[2], face_recv.at[2], near(0, 1, 0)),
            remote(wys, wyr.at[1], face_send.at[3], face_recv.at[3], near(0, -1, 0)),
            remote(
                wzs.at[1, many], wzr.at[0, many], face_send.at[4], face_recv.at[4], near(0, 0, 1)
            ),
            remote(
                wzs.at[0, many], wzr.at[1, many], face_send.at[5], face_recv.at[5], near(0, 0, -1)
            ),
        ]

    def turn(cells, by):
        return pltpu.roll(cells, by % L, 1) if by % L else cells

    def edge_lanes(q):
        return (lane == 2 * q) | (lane == (2 * q + L - 1) % L)

    def send_faces(step):
        nc = 4 if step == 0 else 3
        copies = face_copies(step)
        copies[0].start()
        copies[1].start()
        for c in range(nc):
            wzs[0, c * CX : (c + 1) * CX, :] = W[c, 1 : CX + 1, D, :]
            wzs[1, c * CX : (c + 1) * CX, :] = W[c, 1 : CX + 1, D + CZ - 1, :]
        copies[4].start()
        copies[5].start()
        packed = jnp.zeros((CZ, L), F32)
        for c in range(nc):

            for x in range(CX):
                q = c * CX + x
                turned = pltpu.roll(W[c, 1 + x, own_z, :], 2 * q, 1) if q else W[c, 1, own_z, :]
                packed = jnp.where(edge_lanes(q), turned, packed)
        wys[...] = packed
        copies[2].start()
        copies[3].start()
        return copies

    def merged(received):
        right = jnp.where(gy < NGY - 1, received[1], 0.0)
        left = jnp.where(gy > 0, received[0], 0.0)
        return jnp.where(lane % 2 == 0, right, pltpu.roll(left, 2, 1))

    def wait_faces(step, copies):
        nc = 4 if step == 0 else 3
        for copy in copies:
            copy.wait()
        E[...] = merged(wyr)
        for c in range(nc):
            W[c, 0, own_z, :] = jnp.where(gx > 0, W[c, 0, own_z, :], 0.0)
            W[c, CX + 1, own_z, :] = jnp.where(gx < NGX - 1, W[c, CX + 1, own_z, :], 0.0)
            above = jnp.where(gz > 0, wzr[0, c * CX : (c + 1) * CX, :], 0.0)
            below = jnp.where(gz < NGZ - 1, wzr[1, c * CX : (c + 1) * CX, :], 0.0)
            W[c, 1 : CX + 1, D - 1, :] = above
            W[c, 1 : CX + 1, D + CZ, :] = below

    def sides(cells, edge):
        left = jnp.where(lane == 0, edge, pltpu.roll(cells, 1, 1))
        right = jnp.where(lane == L - 1, edge, pltpu.roll(cells, L - 1, 1))
        return left, right

    def edge_of(ref, q):
        return pltpu.roll(ref[...], (2 * L - 1 - 2 * q) % L, 1)

    def star_faces(step):
        nc = 4 if step == 0 else 3
        for c in range(nc):

            @pl.loop(0, CX, unroll=8)
            def _(x):
                cells = W[c, 1 + x, own_z, :]
                left, right = sides(cells, edge_of(E, c * CX + x))
                total = W[c, x, own_z, :] + W[c, x + 2, own_z, :]
                total = total + W[c, 1 + x, pl.ds(D - 1, CZ), :] + W[c, 1 + x, pl.ds(D + 1, CZ), :]
                total = total + left + right
                if c < 3:
                    ST[c, 1 + x, own_z, :] = 0.88 * cells + 0.02 * total
                else:
                    R[x] = total

        copies = [
            remote(
                ST.at[0, CX, own_z, :],
                ST.at[0, 0, own_z, :],
                star_send.at[0],
                star_recv.at[0],
                near(1, 0, 0),
            ),
            remote(
                ST.at[0, 1, own_z, :],
                ST.at[0, CX + 1, own_z, :],
                star_send.at[1],
                star_recv.at[1],
                near(-1, 0, 0),
            ),
            remote(sys_, syr.at[0], star_send.at[2], star_recv.at[2], near(0, 1, 0)),
            remote(sys_, syr.at[1], star_send.at[3], star_recv.at[3], near(0, -1, 0)),
            remote(szs.at[1], szr.at[0], star_send.at[4], star_recv.at[4], near(0, 0, 1)),
            remote(szs.at[0], szr.at[1], star_send.at[5], star_recv.at[5], near(0, 0, -1)),
        ]
        copies[0].start()
        copies[1].start()
        szs[0] = ST[2, 1 : CX + 1, D, :]
        szs[1] = ST[2, 1 : CX + 1, D + CZ - 1, :]
        copies[4].start()
        copies[5].start()

        packed = jnp.zeros((CZ, L), F32)
        for x in range(CX):
            turned = pltpu.roll(ST[1, 1 + x, own_z, :], 2 * x, 1) if x else ST[1, 1, own_z, :]
            packed = jnp.where(edge_lanes(x), turned, packed)
        sys_[...] = packed
        copies[2].start()
        copies[3].start()
        return copies

    def around(j):
        return (lane + (8 - 16 * j) % L) % L < 16

    def sources(step, copies):
        for copy in copies:
            copy.wait()
        E2[...] = merged(syr)
        ST[0, 0, own_z, :] = jnp.where(gx > 0, ST[0, 0, own_z, :], 0.0)
        ST[0, CX + 1, own_z, :] = jnp.where(gx < NGX - 1, ST[0, CX + 1, own_z, :], 0.0)
        ST[2, 1 : CX + 1, D - 1, :] = jnp.where(gz > 0, szr[0], 0.0)
        ST[2, 1 : CX + 1, D + CZ, :] = jnp.where(gz < NGZ - 1, szr[1], 0.0)
        for group in range(NG):

            kept = [jnp.zeros((CZ, L), F32), jnp.zeros((CZ, L), F32)]
            for j in range(8):
                x = group * 8 + j
                left, right = sides(ST[1, 1 + x, own_z, :], edge_of(E2, x))
                total = ST[0, x + 2, own_z, :] - ST[0, x, own_z, :] + right - left
                total = total + ST[2, 1 + x, pl.ds(D + 1, CZ), :]
                source = 0.5 * (total - ST[2, 1 + x, pl.ds(D - 1, CZ), :])
                first = R[x] - source
                GS[step, 0, D + x, own_z, :] = first
                GS[step, 1, D + x, own_z, :] = source
                mine = around(j)
                kept[0] = jnp.where(mine, turn(first, 16 * j), kept[0])
                kept[1] = jnp.where(mine, turn(source, 16 * j), kept[1])
            gys[0, group] = kept[0]
            gys[1, group] = kept[1]

    def deep_copies(cells, off, packed, received, send, recv):
        fields = pl.ds(0, packed.shape[0])
        copies = []
        for i, (dx, dy, dz) in enumerate(DIRS):
            if dy == 0:
                zs, zd = {
                    0: (own_z, own_z),
                    -1: (pl.ds(D, D), pl.ds(D + CZ, D)),
                    1: (pl.ds(CZ, D), pl.ds(0, D)),
                }[dz]
                deep = off if dz == 0 else D
                xs, xd = {
                    0: (pl.ds(off, CX), pl.ds(off, CX)),
                    -1: (pl.ds(off, deep), pl.ds(off + CX, deep)),
                    1: (pl.ds(off + CX - deep, deep), pl.ds(off - deep, deep)),
                }[dx]
                src = cells.at[fields, xs, zs, :]
                dst = cells.at[fields, xd, zd, :]
            else:
                zs, zd = {
                    0: (pl.ds(0, CZ), own_z),
                    -1: (pl.ds(0, D), pl.ds(D + CZ, D)),
                    1: (pl.ds(CZ - D, D), pl.ds(0, D)),
                }[dz]
                xs, xd = {
                    0: (pl.ds(0, NG), pl.ds(1, NG)),
                    -1: (pl.ds(0, 1), pl.ds(NG + 1, 1)),
                    1: (pl.ds(NG - 1, 1), pl.ds(0, 1)),
                }[dx]
                src = packed.at[fields, xs, zs, :]
                dst = received.at[0 if dy == 1 else 1, fields, xd, zd, :]
            copies.append(remote(src, dst, send.at[i], recv.at[i], near(dx, dy, dz)))
        return copies

    lane_z = lanes((Z, L))

    def unpack(received, field, target, base):
        @pl.loop(0, NG + 2)
        def _(group):
            both_sides = jnp.where(
                lane_z % 16 < 8, received[1, field, group], received[0, field, group]
            )
            for j in range(8):
                target[base + group * 8 + j] = turn(both_sides, -16 * j)

    def one_wait(whole_src, whole_dst, send, recv, device):
        remote(whole_src, whole_dst, send, recv, device).wait()

    def inflow_first(step):
        column = jnp.sum(W[0, 1 : CX + 1, own_z, :], axis=1)
        y = rows_of((L, L)) + gy * L
        begin = TB[1, 0:1, :].astype(jnp.int32)
        band = ((y >= begin) & (y < begin + BAND)).astype(F32)
        sums = jnp.dot(column, band, precision=lax.Precision.HIGHEST, preferred_element_type=F32)
        x = rows_of((CX, L)) + gx * CX
        picked = jnp.where(x == TB[0, 0:1, :].astype(jnp.int32), sums, 0.0)
        u1s[step] = jnp.broadcast_to(jnp.sum(picked, axis=0, keepdims=True), (8, L))

        @pl.loop(1, plane)
        def _(r):
            remote(
                u1s.at[step],
                u1r.at[step, r - 1],
                u_send.at[2 * step],
                u_recv.at[2 * step],
                plane_peer(r),
            ).start()

    def inflow_second(step):
        whole = u1r.at[step]
        one_wait(whole, whole, u_send.at[2 * step], u_recv.at[2 * step], plane_peer(1))
        u2s[step] = u1s[step] + jnp.sum(u1r[step], axis=0)

        @pl.loop(1, NGX)
        def _(r):
            remote(
                u2s.at[step],
                u2r.at[step, r - 1],
                u_send.at[2 * step + 1],
                u_recv.at[2 * step + 1],
                line_peer(r),
            ).start()

    def magnitudes(step):
        whole = u2r.at[step]
        one_wait(whole, whole, u_send.at[2 * step + 1], u_recv.at[2 * step + 1], line_peer(1))
        total = u2s[step] + jnp.sum(u2r[step], axis=0)
        uref = total[0:1] * (1.0 / (BAND * CZ * NGZ))
        return 0.5 * TB[2, 0:1, :] * uref * jnp.abs(uref)

    def forces(step):
        size = magnitudes(step)

        @pl.loop(0, NGX, unroll=4)
        def _(g):
            at = pl.ds(pl.multiple_of(g * CAP * NGY, CAP * NGY), CAP * NGY)
            hot = jnp.where(TC[at, :] == lanes((CAP * NGY, L)).astype(F32), size, 0.0)
            scaled = R2[g, : CAP * NGY, :] * jnp.sum(hot, axis=1, keepdims=True)
            top = scaled.astype(BF16)
            KC[at, :L] = top
            KC[at, L:] = (scaled - top.astype(F32)).astype(BF16)

        part = CX // 4
        for h in range(4):
            both = jnp.dot(
                O[h * part * CZ : (h + 1) * part * CZ, :], KC[...], preferred_element_type=F32
            )
            force = (both[:, :L] + both[:, L:]).reshape(part, CZ, L)
            F[0, D + 1 + h * part : D + 1 + (h + 1) * part, own_z, :] = force
        for group in range(NG):

            kept = jnp.zeros((CZ, L), F32)
            for j in range(8):
                turned = turn(F[0, D + 1 + group * 8 + j, own_z, :], 16 * j)
                kept = jnp.where(around(j), turned, kept)
            fys[0, group] = kept
        copies = deep_copies(F, D + 1, fys, fyr, f_send, f_recv)
        for copy in copies:
            copy.start()
        return copies

    def inside(x):
        spot_x = gx * CX + x - D
        return (spot_x >= 0) & (spot_x < NGX * CX)

    ringlane = lanes((8, L))[0:1]
    right_ok = jnp.where(gy < NGY - 1, 1.0, 0.0)
    left_ok = jnp.where(gy > 0, 1.0, 0.0)
    ring = jnp.where(ringlane < D, right_ok, jnp.where(ringlane >= L - D, left_ok, 0.0))
    top_ok = jnp.where(gz > 0, 1.0, 0.0)
    bottom_ok = jnp.where(gz < NGZ - 1, 1.0, 0.0)

    def weights():
        out = []
        for start, size in CHUNKS:
            scale = 1.0 / 6.0
            if start == 0:
                scale = scale * top_ok
            if start + size == Z:
                scale = scale * bottom_ok
            out.append((scale, ring * scale))
        return out

    def outside_x(pp):
        for ok, x in ((gx > 0, D), (gx < NGX - 1, D + CX + 1)):

            @pl.when(jnp.logical_not(ok))
            def _():
                for ab in range(2):
                    PR[pp, ab, x, 8 : 8 + Z, :] = jnp.zeros((Z, L), F32)

    def beside(a, b):
        both = jnp.concatenate([a, b], axis=-1).reshape(-1, 2 * L)
        top = both.astype(BF16)
        rest = (both - top.astype(F32)).astype(BF16)
        total = jnp.dot(top, RING[...], preferred_element_type=F32)
        total = total + jnp.dot(rest, RING[...], preferred_element_type=F32)
        return total[:, :L].reshape(a.shape), total[:, L:].reshape(a.shape)

    def ring_sides(a, b):
        axis, lane_c = a.ndim - 1, lanes(a.shape)
        am, bm = pltpu.roll(a, 1, axis), pltpu.roll(b, 1, axis)
        ap, bp = pltpu.roll(a, L - 1, axis), pltpu.roll(b, L - 1, axis)
        first, last = lane_c == 0, lane_c == L - 1
        return (
            (jnp.where(first, bm, am), jnp.where(last, bp, ap)),
            (jnp.where(first, am, bm), jnp.where(last, ap, bp)),
        )

    def sweeps(step, f_copies):
        for copy in f_copies:
            copy.wait()

        unpack(fyr, 0, BF, 1)
        scales = weights()

        @pl.loop(0, X, unroll=4)
        def _(x):
            plus = jnp.where(inside(x + 1), -0.2, 0.0)
            minus = jnp.where(inside(x - 1), -0.2, 0.0)
            for (start, size), (ca, cb) in zip(CHUNKS, scales):
                at = pl.ds(start, size)
                to = pl.ds(start + 8, size)
                fa = plus * F[0, x + 2, at, :] - minus * F[0, x, at, :]
                fb = plus * BF[x + 2, at, :] - minus * BF[x, at, :]
                S[0, x, at, :] = GS[step, 1, x, at, :] + fa
                S[1, x, at, :] = BGS[1, x, at, :] + fb
                PR[0, 0, x + 1, to, :] = (GS[step, 0, x, at, :] - fa) * ca
                PR[0, 1, x + 1, to, :] = (BGS[0, x, at, :] - fb) * cb

        outside_x(0)
        for k in range(2, SWEEPS + 1):
            src, dst = k % 2, (k + 1) % 2
            wide = -(-(CX + 2 * (SWEEPS + 1 - k)) // BLOCK) * BLOCK
            begin = (X - wide) // 2

            @pl.loop(0, wide // BLOCK, unroll=True)
            def _(block):
                x = begin + block * BLOCK
                mid, back, ahead = pl.ds(x + 1, BLOCK), pl.ds(x, BLOCK), pl.ds(x + 2, BLOCK)
                along = beside(PR[src, 0, mid, 8 : 8 + Z, :], PR[src, 1, mid, 8 : 8 + Z, :])
                for (start, size), (ca, cb) in zip(CHUNKS, scales):
                    at = pl.ds(start + 8, size)
                    up = pl.ds(start + 7, size)
                    down = pl.ds(start + 9, size)
                    for ab, scale in ((0, ca), (1, cb)):
                        total = PR[src, ab, back, at, :] + PR[src, ab, ahead, at, :]
                        total = total + PR[src, ab, mid, up, :] + PR[src, ab, mid, down, :]
                        total = total - S[ab, pl.ds(x, BLOCK), pl.ds(start, size), :]
                        total = total + along[ab][:, start : start + size]
                        PR[dst, ab, mid, at, :] = total * scale

            outside_x(dst)

        at = pl.ds(D + 8, CZ)
        last = (SWEEPS + 1) % 2

        @pl.loop(0, CX, unroll=4)
        def _(x):
            deep = D + x + 1
            (left, right), _ = ring_sides(PR[last, 0, deep, at, :], PR[last, 1, deep, at, :])
            back, ahead = PR[last, 0, deep - 1, at, :], PR[last, 0, deep + 1, at, :]
            up = PR[last, 0, deep, pl.ds(D + 7, CZ), :]
            down = PR[last, 0, deep, pl.ds(D + 9, CZ), :]
            force = F[0, D + 1 + x, own_z, :]
            W[0, 1 + x, own_z, :] = ST[0, 1 + x, own_z, :] - 0.4 * force - 0.5 * (ahead - back)
            W[1, 1 + x, own_z, :] = ST[1, 1 + x, own_z, :] - 0.5 * (right - left)
            W[2, 1 + x, own_z, :] = ST[2, 1 + x, own_z, :] - 0.5 * (down - up)
            if step == 0:
                R[x] = back + ahead + up + down + left + right

    def unpack_sources(step, copies):
        for copy in copies:
            copy.wait()
        for field in range(2):
            unpack(gyr.at[step], field, BGS.at[field], 0)

    row_all = 2 * (NGY - 1)

    def row_second(h):
        for r in range(1, NGY):
            row_first(r, h).wait()

        @pl.loop(0, hx)
        def _(d):
            notes = R1[0, h, pl.ds(hx * CAP + d, 1), :]
            for k in range(NGY):
                at = pl.ds(pl.multiple_of(d * CAP, CAP), CAP)
                S2[h * hx + d, k * CAP : (k + 1) * CAP, :] = R1[k, h, at, :]
                if k:
                    more = R1[k, h, pl.ds(hx * CAP + d, 1), :]
                    notes = jnp.where(lanes((1, L)) // 32 == k, pltpu.roll(more, 32 * k, 1), notes)
            S2[h * hx + d, NGY * CAP : NGY * CAP + 1, :] = notes

        @pl.loop(h * hx, (h + 1) * hx)
        def _(peer):
            @pl.when(peer != gx)
            def _():
                slot = lax.rem(peer - gx + NGX, NGX) - 1
                remote(
                    S2.at[peer],
                    R2.at[slot],
                    row_send.at[row_all],
                    row_recv.at[row_all],
                    (peer, gy, gz),
                ).start()

        if h == 1:
            R2[NGX - 1] = S2[gx]

    def row_last():
        whole = R2.at[pl.ds(0, NGX - 1)]
        one_wait(whole, whole, row_send.at[row_all], row_recv.at[row_all], line_peer(1))
        which = lanes((CAP, L)) - rows_of((CAP, L))

        @pl.loop(0, NGX, unroll=4)
        def _(g):
            for k in range(NGY):
                row = R2[g, NGY * CAP : NGY * CAP + 1, :]
                base = 32 * k
                coarse = jnp.where(which == base, 32.0 * row, 0.0)
                told_line = jnp.where(which == base + 8, row, coarse)
                told_turbine = jnp.where(which == base + 16, row, 0.0)
                at = pl.ds(pl.multiple_of((g * NGY + k) * CAP, CAP), CAP)
                LC[at, :] = jnp.broadcast_to(
                    jnp.sum(told_line, axis=1, keepdims=True), (CAP, L)
                )
                TC[at, :] = jnp.broadcast_to(
                    jnp.sum(told_turbine, axis=1, keepdims=True), (CAP, L)
                )

        wide = min(L, slots)
        same = rows_of((wide, wide)) == lanes((wide, wide))
        for c in range(slots // wide):
            turned = jnp.where(same, LC[c * wide : (c + 1) * wide, :wide], 0.0)
            named = jnp.sum(turned, axis=0, keepdims=True).astype(jnp.int32)

            @pl.loop(0, CX)
            def _(x):
                at = pl.ds(pl.multiple_of(x * CZ, CZ), CZ)
                hit = rows_of((CZ, wide)) + x * CZ == named
                O[at, c * wide : (c + 1) * wide] = hit.astype(F32).astype(BF16)

    def constants():
        zero_pad = jnp.zeros((8, L), F32)
        for pp in range(2):
            for ab in range(2):

                @pl.loop(0, X + 2, unroll=X + 2)
                def _(x):
                    PR[pp, ab, x, 0:8, :] = zero_pad
                    PR[pp, ab, x, Z + 8 : Z + 16, :] = zero_pad

                PR[pp, ab, 0, :, :] = jnp.zeros((Z + 16, L), F32)
                PR[pp, ab, X + 1, :, :] = jnp.zeros((Z + 16, L), F32)

        BF[0, :, :] = jnp.zeros((Z, L), F32)
        BF[X + 1, :, :] = jnp.zeros((Z, L), F32)
        step_apart = lax.rem(rows_of((2 * L, 2 * L)) - lanes((2 * L, 2 * L)) + 2 * L, 2 * L)
        RING[...] = ((step_apart == 1) | (step_apart == 2 * L - 1)).astype(F32).astype(BF16)

    for step in range(STEPS):
        faces = send_faces(step)
        inflow_first(step)
        if step == 0:
            constants()
            row_second(0)
        wait_faces(step, faces)
        if step == 0:
            row_second(1)
        stars = star_faces(step)
        inflow_second(step)
        sources(step, stars)
        deep = deep_copies(GS.at[step], D, gys, gyr.at[step], gs_send.at[step], gs_recv.at[step])
        for copy in deep:
            copy.start()
        if step == 0:
            row_last()
        f_copies = forces(step)
        unpack_sources(step, deep)
        sweeps(step, f_copies)

    last = (SWEEPS + 1) % 2
    outs = [
        pltpu.make_async_copy(W.at[pl.ds(0, 3), pl.ds(1, CX), own_z, :], vout, in_sem.at[0]),
        pltpu.make_async_copy(
            PR.at[last, 0, pl.ds(D + 1, CX), pl.ds(D + 8, CZ), :], pout, in_sem.at[1]
        ),
    ]
    for out in outs:
        out.start()
    for out in outs:
        out.wait()


def deliver(vel, prs, vout, pout, held, load_sem, store_sem):
    half = prs.shape[0] // 2
    loads, stores = [], []
    for k in range(8):
        at = pl.ds(k % 2 * half, half)
        source, target = (vel.at[k // 2, at], vout.at[k // 2, at])
        if k >= 6:
            source, target = prs.at[at], pout.at[at]
        loads.append(pltpu.make_async_copy(source, held.at[k], load_sem.at[k]))
        stores.append(pltpu.make_async_copy(held.at[k], target, store_sem.at[k]))
    for load in loads:
        load.start()
    for load, store in zip(loads, stores):
        load.wait()
        store.start()
    for store in stores:
        store.wait()


def body(
    shape,
    velocity,
    pressure,
    kern,
    owners,
    lines,
    point_turbine,
    row_counts,
    thrust,
    inflow_x,
    inflow_y,
):
    ngx, ngy, ngz = shape
    cx, cz = velocity.shape[1:3]
    z, x, ng = cz + 2 * D, cx + 2 * D, cx // 8
    rows = kern.shape[0]
    slots = ngx * ngy * CAP
    turbines = thrust.shape[0]
    any_spec = pl.BlockSpec(memory_space=pl.ANY)
    vm = pltpu.VMEM
    dma = pltpu.SemaphoreType.DMA
    i32 = jnp.int32
    scratch = [
        vm((rows, L), F32),
        vm((1, rows), i32),
        vm((1, rows), i32),
        vm((1, rows), i32),
        vm((1, 1), i32),
        vm((1, turbines), F32),
        vm((1, turbines), i32),
        vm((1, turbines), i32),
        vm((4, cx + 2, z, L), F32),
        vm((cz, L), F32),
        vm((2, cz, L), F32),
        vm((2, 4 * cx, L), F32),
        vm((2, 4 * cx, L), F32),
        vm((cz, L), F32),
        vm((3, cx + 2, z, L), F32),
        vm((cz, L), F32),
        vm((2, cz, L), F32),
        vm((2, cx, L), F32),
        vm((2, cx, L), F32),
        vm((cz, L), F32),
        vm((cx, cz, L), F32),
        vm((STEPS, 2, x, z, L), F32),
        vm((2, ng, cz, L), F32),
        vm((STEPS, 2, 2, ng + 2, z, L), F32),
        vm((2, x, z, L), F32),
        vm((1, x + 2, z, L), F32),
        vm((1, ng, cz, L), F32),
        vm((2, 1, ng + 2, z, L), F32),
        vm((x + 2, z, L), F32),
        vm((2, x, z, L), F32),
        vm((2, 2, x + 2, z + 16, L), F32),
        vm((ngy, 2, ngx // 2 * (CAP + 1), L), F32),
        vm((ngy, 2, ngx // 2 * (CAP + 1), L), F32),
        vm((ngx, ngy * CAP + 1, L), F32),
        vm((ngx, ngy * CAP + 1, L), F32),
        vm((slots, L), F32),
        vm((slots, L), F32),
        vm((cx * cz, slots), BF16),
        vm((slots, 2 * L), BF16),
        vm((3, 8, L), F32),
        vm((2 * L, 2 * L), BF16),
        vm((STEPS, 8, L), F32),
        vm((STEPS, ngy * ngz - 1, 8, L), F32),
        vm((STEPS, 8, L), F32),
        vm((STEPS, ngx - 1, 8, L), F32),
        dma((10,)),
        dma((6,)),
        dma((6,)),
        dma((6,)),
        dma((6,)),
        dma((STEPS, 26)),
        dma((STEPS, 26)),
        dma((26,)),
        dma((26,)),
        dma((2 * ngy - 1,)),
        dma((2 * ngy - 1,)),
        dma((2 * STEPS,)),
        dma((2 * STEPS,)),
    ]
    ahead = pl.pallas_call(
        functools.partial(kernel, (ngx, ngy, ngz, cx, cz)),
        out_shape=(
            jax.ShapeDtypeStruct(velocity.shape, F32),
            jax.ShapeDtypeStruct(pressure.shape, F32),
        ),
        in_specs=[pl.BlockSpec(memory_space=pltpu.HBM)] * 10,
        out_specs=(any_spec, any_spec),
        scratch_shapes=scratch,
        compiler_params=pltpu.CompilerParams(
            collective_id=0, has_side_effects=True, vmem_limit_bytes=56 * 1024 * 1024
        ),
    )(
        velocity,
        pressure,
        kern,
        owners.reshape(1, rows),
        lines.reshape(1, rows),
        point_turbine.reshape(1, rows),
        row_counts.reshape(1, 1),
        thrust.reshape(1, turbines),
        inflow_x.reshape(1, turbines),
        inflow_y.reshape(1, turbines),
    )
    return pl.pallas_call(
        deliver,
        out_shape=(
            jax.ShapeDtypeStruct(velocity.shape, F32),
            jax.ShapeDtypeStruct(pressure.shape, F32),
        ),
        in_specs=[any_spec] * 2,
        out_specs=(any_spec, any_spec),
        scratch_shapes=[vm((8, cx // 2, cz, L), F32), dma((8,)), dma((8,))],
        compiler_params=pltpu.CompilerParams(vmem_limit_bytes=60 * 1024 * 1024),
    )(*ahead)


def solution(mesh):
    placed = (
        P(None, "gx", "gz", "gy"),
        P("gx", "gz", "gy"),
        P(("gx", "gy", "gz"), None),
        P(("gx", "gy", "gz"), None),
        P(("gx", "gy", "gz")),
        P(("gx", "gy", "gz")),
        P("gx", "gy", "gz"),
        P(),
        P(),
        P(),
    )
    shape = (mesh.shape["gx"], mesh.shape["gy"], mesh.shape["gz"])
    return jax.shard_map(
        functools.partial(body, shape),
        mesh=mesh,
        in_specs=placed,
        out_specs=(P(None, "gx", "gz", "gy"), P("gx", "gz", "gy")),
        check_vma=False,
    )
```

```python
import functools

import jax
import jax.numpy as jnp
from jax import lax
from jax.experimental import pallas as pl
from jax.experimental.pallas import tpu as pltpu
from jax.sharding import PartitionSpec as P

BAND = 32
STEPS = 2
SWEEPS = 8
CAP = 8
L = 128
D = 8
BLOCK = 4
MESH = pl.DeviceIdType.MESH
CHUNKS = ((0, 8), (8, 16), (24, 16), (40, 16), (56, 8))
F32 = jnp.float32
BF16 = jnp.bfloat16
DIRS = tuple(
    sorted(
        (
            (dx, dy, dz)
            for dx in (-1, 0, 1)
            for dy in (-1, 0, 1)
            for dz in (-1, 0, 1)
            if (dx, dy, dz) != (0, 0, 0)
        ),
        key=lambda d: (abs(d[1]), abs(d[2]), -abs(d[0])),
    )
)


def lanes(shape):
    return lax.broadcasted_iota(jnp.int32, shape, len(shape) - 1)


def rows_of(shape):
    return lax.broadcasted_iota(jnp.int32, shape, len(shape) - 2)


def pieces(x):
    hi = x.astype(BF16)
    rest = x - hi.astype(F32)
    mid = rest.astype(BF16)
    return hi, mid, (rest - mid.astype(F32)).astype(BF16)


def kernel(
    sizes,
    vel,
    prs,
    kern_h,
    own_h,
    line_h,
    turb_h,
    cnt_h,
    thrust_h,
    infx_h,
    infy_h,
    vout,
    pout,
    kern,
    own_r,
    line_r,
    turb_r,
    cnt,
    thrust,
    infx,
    infy,
    W,
    wys,
    wyr,
    wzs,
    wzr,
    E,
    ST,
    sys_,
    syr,
    szs,
    szr,
    E2,
    R,
    GS,
    gys,
    gyr,
    BGS,
    F,
    fys,
    fyr,
    BF,
    S,
    PR,
    S1,
    R1,
    S2,
    R2,
    LC,
    TC,
    O,
    KC,
    TB,
    RING,
    u1s,
    u1r,
    u2s,
    u2r,
    in_sem,
    face_send,
    face_recv,
    star_send,
    star_recv,
    gs_send,
    gs_recv,
    f_send,
    f_recv,
    row_send,
    row_recv,
    u_send,
    u_recv,
):
    NGX, NGY, NGZ, CX, CZ = sizes
    Z = CZ + 2 * D
    X = CX + 2 * D
    NG = CX // 8
    T = thrust.shape[1]
    rows = kern.shape[0]
    peers = NGX * NGY
    slots = peers * CAP
    plane = NGY * NGZ
    gx = lax.axis_index("gx")
    gy = lax.axis_index("gy")
    gz = lax.axis_index("gz")
    own_z = pl.ds(D, CZ)

    def near(dx, dy, dz):
        return (
            lax.rem(gx + dx + NGX, NGX),
            lax.rem(gy + dy + NGY, NGY),
            lax.rem(gz + dz + NGZ, NGZ),
        )

    def plane_peer(r):
        spot = lax.rem(gy * NGZ + gz + r, plane)
        return (gx, spot // NGZ, lax.rem(spot, NGZ))

    def line_peer(r):
        return (lax.rem(gx + r, NGX), gy, gz)

    def remote(src, dst, send, recv, device):
        return pltpu.make_async_remote_copy(
            src_ref=src,
            dst_ref=dst,
            send_sem=send,
            recv_sem=recv,
            device_id=device,
            device_id_type=MESH,
        )

    loads = [
        pltpu.make_async_copy(vel, W.at[pl.ds(0, 3), pl.ds(1, CX), own_z, :], in_sem.at[0]),
        pltpu.make_async_copy(prs, W.at[3, pl.ds(1, CX), own_z, :], in_sem.at[1]),
    ]
    small = [
        pltpu.make_async_copy(source, here, in_sem.at[2 + i])
        for i, (source, here) in enumerate(
            (
                (own_h, own_r),
                (line_h, line_r),
                (turb_h, turb_r),
                (cnt_h, cnt),
                (kern_h, kern),
                (thrust_h, thrust),
                (infx_h, infx),
                (infy_h, infy),
            )
        )
    ]
    for load in small + loads:
        load.start()
    barrier = pltpu.get_barrier_semaphore()

    @pl.loop(1, plane)
    def _(r):
        pl.semaphore_signal(barrier, inc=1, device_id=plane_peer(r), device_id_type=MESH)

    @pl.loop(1, NGX)
    def _(r):
        pl.semaphore_signal(barrier, inc=1, device_id=line_peer(r), device_id_type=MESH)

    greeted = plane - 1 + NGX - 1
    for d in DIRS:
        if d[0] and (d[1] or d[2]):
            pl.semaphore_signal(barrier, inc=1, device_id=near(*d), device_id_type=MESH)
            greeted += 1

    for load in small:
        load.wait()
    owner = own_r[...]
    live = lanes((1, rows)) < cnt[...]
    spot = jnp.where(live, (owner % NGY) * NGX + owner // NGY, -1)
    land = (rows_of((peers, rows)) == spot).astype(F32)
    before = (rows_of((rows, rows)) < lanes((rows, rows))).astype(BF16)
    earlier = jnp.dot(land.astype(BF16), before, preferred_element_type=F32)
    rank = jnp.sum(land * earlier, axis=0, keepdims=True).astype(jnp.int32)
    slot = jnp.where(live, spot * CAP + rank, -1)
    place = (rows_of((slots, rows)) == slot).astype(BF16)
    hi, mid, lo = pieces(kern[...])
    both = jnp.dot(place, jnp.concatenate([hi, mid], axis=1), preferred_element_type=F32)
    sorted_rows = both[:, :L] + both[:, L:]
    sorted_rows = sorted_rows + jnp.dot(place, lo, preferred_element_type=F32)
    kind = rows_of((L, rows))
    line = line_r[...]
    told = jnp.where(kind < 8, line // 32, jnp.where(kind < 16, line % 32, turb_r[...]))
    told = jnp.where((kind % 8 == rank) & (kind < 24), told, 0).astype(F32).astype(BF16)
    meta = lax.dot_general(
        land.astype(BF16), told, (((1,), (1,)), ((), ())), preferred_element_type=F32
    )
    hx = NGX // 2
    for k in range(NGY):
        for h in range(2):
            first = k * NGX + h * hx
            S1[k, h, : hx * CAP, :] = sorted_rows[first * CAP : (first + hx) * CAP]
            S1[k, h, hx * CAP :, :] = meta[first : first + hx]
    TB[...] = jnp.zeros_like(TB)
    TB[0, 0:1, :T] = infx[...].astype(F32)
    TB[1, 0:1, :T] = infy[...].astype(F32)
    TB[2, 0:1, :T] = thrust[...]
    for load in loads:
        load.wait()
    pl.semaphore_wait(barrier, greeted)

    def row_first(r, h):
        peer = lax.rem(gy + r, NGY)
        i = 2 * (r - 1) + h
        return remote(
            S1.at[peer, h], R1.at[r - 1, h], row_send.at[i], row_recv.at[i], (gx, peer, gz)
        )

    for h in range(2):
        for r in range(1, NGY):
            row_first(r, h).start()
    R1[NGY - 1] = S1[gy]

    lane = lanes((CZ, L))

    def face_copies(step):
        nc = 4 if step == 0 else 3
        comps = pl.ds(0, nc)
        many = pl.ds(0, nc * CX)
        return [
            remote(
                W.at[comps, pl.ds(CX, 1), own_z, :],
                W.at[comps, pl.ds(0, 1), own_z, :],
                face_send.at[0],
                face_recv.at[0],
                near(1, 0, 0),
            ),
            remote(
                W.at[comps, pl.ds(1, 1), own_z, :],
                W.at[comps, pl.ds(CX + 1, 1), own_z, :],
                face_send.at[1],
                face_recv.at[1],
                near(-1, 0, 0),
            ),
            remote(wys, wyr.at[0], face_send.at[2], face_recv.at[2], near(0, 1, 0)),
            remote(wys, wyr.at[1], face_send.at[3], face_recv.at[3], near(0, -1, 0)),
            remote(
                wzs.at[1, many], wzr.at[0, many], face_send.at[4], face_recv.at[4], near(0, 0, 1)
            ),
            remote(
                wzs.at[0, many], wzr.at[1, many], face_send.at[5], face_recv.at[5], near(0, 0, -1)
            ),
        ]

    def turn(cells, by):
        return pltpu.roll(cells, by % L, 1) if by % L else cells

    def edge_lanes(q):
        return (lane == 2 * q) | (lane == (2 * q + L - 1) % L)

    def send_faces(step):
        nc = 4 if step == 0 else 3
        copies = face_copies(step)
        copies[0].start()
        copies[1].start()
        for c in range(nc):
            wzs[0, c * CX : (c + 1) * CX, :] = W[c, 1 : CX + 1, D, :]
            wzs[1, c * CX : (c + 1) * CX, :] = W[c, 1 : CX + 1, D + CZ - 1, :]
        copies[4].start()
        copies[5].start()
        packed = jnp.zeros((CZ, L), F32)
        for c in range(nc):

            for x in range(CX):
                q = c * CX + x
                turned = pltpu.roll(W[c, 1 + x, own_z, :], 2 * q, 1) if q else W[c, 1, own_z, :]
                packed = jnp.where(edge_lanes(q), turned, packed)
        wys[...] = packed
        copies[2].start()
        copies[3].start()
        return copies

    def merged(received):
        right = jnp.where(gy < NGY - 1, received[1], 0.0)
        left = jnp.where(gy > 0, received[0], 0.0)
        return jnp.where(lane % 2 == 0, right, pltpu.roll(left, 2, 1))

    def wait_faces(step, copies):
        nc = 4 if step == 0 else 3
        for copy in copies:
            copy.wait()
        E[...] = merged(wyr)
        for c in range(nc):
            W[c, 0, own_z, :] = jnp.where(gx > 0, W[c, 0, own_z, :], 0.0)
            W[c, CX + 1, own_z, :] = jnp.where(gx < NGX - 1, W[c, CX + 1, own_z, :], 0.0)
            above = jnp.where(gz > 0, wzr[0, c * CX : (c + 1) * CX, :], 0.0)
            below = jnp.where(gz < NGZ - 1, wzr[1, c * CX : (c + 1) * CX, :], 0.0)
            W[c, 1 : CX + 1, D - 1, :] = above
            W[c, 1 : CX + 1, D + CZ, :] = below

    def sides(cells, edge):
        left = jnp.where(lane == 0, edge, pltpu.roll(cells, 1, 1))
        right = jnp.where(lane == L - 1, edge, pltpu.roll(cells, L - 1, 1))
        return left, right

    def edge_of(ref, q):
        return pltpu.roll(ref[...], (2 * L - 1 - 2 * q) % L, 1)

    def star_faces(step):
        nc = 4 if step == 0 else 3
        for c in range(nc):

            @pl.loop(0, CX, unroll=8)
            def _(x):
                cells = W[c, 1 + x, own_z, :]
                left, right = sides(cells, edge_of(E, c * CX + x))
                total = W[c, x, own_z, :] + W[c, x + 2, own_z, :]
                total = total + W[c, 1 + x, pl.ds(D - 1, CZ), :] + W[c, 1 + x, pl.ds(D + 1, CZ), :]
                total = total + left + right
                if c < 3:
                    ST[c, 1 + x, own_z, :] = 0.88 * cells + 0.02 * total
                else:
                    R[x] = total

        copies = [
            remote(
                ST.at[0, CX, own_z, :],
                ST.at[0, 0, own_z, :],
                star_send.at[0],
                star_recv.at[0],
                near(1, 0, 0),
            ),
            remote(
                ST.at[0, 1, own_z, :],
                ST.at[0, CX + 1, own_z, :],
                star_send.at[1],
                star_recv.at[1],
                near(-1, 0, 0),
            ),
            remote(sys_, syr.at[0], star_send.at[2], star_recv.at[2], near(0, 1, 0)),
            remote(sys_, syr.at[1], star_send.at[3], star_recv.at[3], near(0, -1, 0)),
            remote(szs.at[1], szr.at[0], star_send.at[4], star_recv.at[4], near(0, 0, 1)),
            remote(szs.at[0], szr.at[1], star_send.at[5], star_recv.at[5], near(0, 0, -1)),
        ]
        copies[0].start()
        copies[1].start()
        szs[0] = ST[2, 1 : CX + 1, D, :]
        szs[1] = ST[2, 1 : CX + 1, D + CZ - 1, :]
        copies[4].start()
        copies[5].start()

        packed = jnp.zeros((CZ, L), F32)
        for x in range(CX):
            turned = pltpu.roll(ST[1, 1 + x, own_z, :], 2 * x, 1) if x else ST[1, 1, own_z, :]
            packed = jnp.where(edge_lanes(x), turned, packed)
        sys_[...] = packed
        copies[2].start()
        copies[3].start()
        return copies

    def around(j):
        return (lane + (8 - 16 * j) % L) % L < 16

    def sources(step, copies):
        for copy in copies:
            copy.wait()
        E2[...] = merged(syr)
        ST[0, 0, own_z, :] = jnp.where(gx > 0, ST[0, 0, own_z, :], 0.0)
        ST[0, CX + 1, own_z, :] = jnp.where(gx < NGX - 1, ST[0, CX + 1, own_z, :], 0.0)
        ST[2, 1 : CX + 1, D - 1, :] = jnp.where(gz > 0, szr[0], 0.0)
        ST[2, 1 : CX + 1, D + CZ, :] = jnp.where(gz < NGZ - 1, szr[1], 0.0)
        for group in range(NG):

            kept = [jnp.zeros((CZ, L), F32), jnp.zeros((CZ, L), F32)]
            for j in range(8):
                x = group * 8 + j
                left, right = sides(ST[1, 1 + x, own_z, :], edge_of(E2, x))
                total = ST[0, x + 2, own_z, :] - ST[0, x, own_z, :] + right - left
                total = total + ST[2, 1 + x, pl.ds(D + 1, CZ), :]
                source = 0.5 * (total - ST[2, 1 + x, pl.ds(D - 1, CZ), :])
                first = R[x] - source
                GS[step, 0, D + x, own_z, :] = first
                GS[step, 1, D + x, own_z, :] = source
                mine = around(j)
                kept[0] = jnp.where(mine, turn(first, 16 * j), kept[0])
                kept[1] = jnp.where(mine, turn(source, 16 * j), kept[1])
            gys[0, group] = kept[0]
            gys[1, group] = kept[1]

    def deep_copies(cells, off, packed, received, send, recv):
        fields = pl.ds(0, packed.shape[0])
        copies = []
        for i, (dx, dy, dz) in enumerate(DIRS):
            if dy == 0:
                zs, zd = {
                    0: (own_z, own_z),
                    -1: (pl.ds(D, D), pl.ds(D + CZ, D)),
                    1: (pl.ds(CZ, D), pl.ds(0, D)),
                }[dz]
                deep = off if dz == 0 else D
                xs, xd = {
                    0: (pl.ds(off, CX), pl.ds(off, CX)),
                    -1: (pl.ds(off, deep), pl.ds(off + CX, deep)),
                    1: (pl.ds(off + CX - deep, deep), pl.ds(off - deep, deep)),
                }[dx]
                src = cells.at[fields, xs, zs, :]
                dst = cells.at[fields, xd, zd, :]
            else:
                zs, zd = {
                    0: (pl.ds(0, CZ), own_z),
                    -1: (pl.ds(0, D), pl.ds(D + CZ, D)),
                    1: (pl.ds(CZ - D, D), pl.ds(0, D)),
                }[dz]
                xs, xd = {
                    0: (pl.ds(0, NG), pl.ds(1, NG)),
                    -1: (pl.ds(0, 1), pl.ds(NG + 1, 1)),
                    1: (pl.ds(NG - 1, 1), pl.ds(0, 1)),
                }[dx]
                src = packed.at[fields, xs, zs, :]
                dst = received.at[0 if dy == 1 else 1, fields, xd, zd, :]
            copies.append(remote(src, dst, send.at[i], recv.at[i], near(dx, dy, dz)))
        return copies

    lane_z = lanes((Z, L))

    def unpack(received, field, target, base):
        @pl.loop(0, NG + 2)
        def _(group):
            both_sides = jnp.where(
                lane_z % 16 < 8, received[1, field, group], received[0, field, group]
            )
            for j in range(8):
                target[base + group * 8 + j] = turn(both_sides, -16 * j)

    def one_wait(whole_src, whole_dst, send, recv, device):
        remote(whole_src, whole_dst, send, recv, device).wait()

    def inflow_first(step):
        column = jnp.sum(W[0, 1 : CX + 1, own_z, :], axis=1)
        y = rows_of((L, L)) + gy * L
        begin = TB[1, 0:1, :].astype(jnp.int32)
        band = ((y >= begin) & (y < begin + BAND)).astype(F32)
        sums = jnp.dot(column, band, precision=lax.Precision.HIGHEST, preferred_element_type=F32)
        x = rows_of((CX, L)) + gx * CX
        picked = jnp.where(x == TB[0, 0:1, :].astype(jnp.int32), sums, 0.0)
        u1s[step] = jnp.broadcast_to(jnp.sum(picked, axis=0, keepdims=True), (8, L))

        @pl.loop(1, plane)
        def _(r):
            remote(
                u1s.at[step],
                u1r.at[step, r - 1],
                u_send.at[2 * step],
                u_recv.at[2 * step],
                plane_peer(r),
            ).start()

    def inflow_second(step):
        whole = u1r.at[step]
        one_wait(whole, whole, u_send.at[2 * step], u_recv.at[2 * step], plane_peer(1))
        u2s[step] = u1s[step] + jnp.sum(u1r[step], axis=0)

        @pl.loop(1, NGX)
        def _(r):
            remote(
                u2s.at[step],
                u2r.at[step, r - 1],
                u_send.at[2 * step + 1],
                u_recv.at[2 * step + 1],
                line_peer(r),
            ).start()

    def magnitudes(step):
        whole = u2r.at[step]
        one_wait(whole, whole, u_send.at[2 * step + 1], u_recv.at[2 * step + 1], line_peer(1))
        total = u2s[step] + jnp.sum(u2r[step], axis=0)
        uref = total[0:1] * (1.0 / (BAND * CZ * NGZ))
        return 0.5 * TB[2, 0:1, :] * uref * jnp.abs(uref)

    def forces(step):
        size = magnitudes(step)

        @pl.loop(0, NGX, unroll=4)
        def _(g):
            at = pl.ds(pl.multiple_of(g * CAP * NGY, CAP * NGY), CAP * NGY)
            hot = jnp.where(TC[at, :] == lanes((CAP * NGY, L)).astype(F32), size, 0.0)
            scaled = R2[g, : CAP * NGY, :] * jnp.sum(hot, axis=1, keepdims=True)
            top = scaled.astype(BF16)
            KC[at, :L] = top
            KC[at, L:] = (scaled - top.astype(F32)).astype(BF16)

        part = CX // 4
        for h in range(4):
            both = jnp.dot(
                O[h * part * CZ : (h + 1) * part * CZ, :], KC[...], preferred_element_type=F32
            )
            force = (both[:, :L] + both[:, L:]).reshape(part, CZ, L)
            F[0, D + 1 + h * part : D + 1 + (h + 1) * part, own_z, :] = force
        for group in range(NG):

            kept = jnp.zeros((CZ, L), F32)
            for j in range(8):
                turned = turn(F[0, D + 1 + group * 8 + j, own_z, :], 16 * j)
                kept = jnp.where(around(j), turned, kept)
            fys[0, group] = kept
        copies = deep_copies(F, D + 1, fys, fyr, f_send, f_recv)
        for copy in copies:
            copy.start()
        return copies

    def inside(x):
        spot_x = gx * CX + x - D
        return (spot_x >= 0) & (spot_x < NGX * CX)

    ringlane = lanes((8, L))[0:1]
    right_ok = jnp.where(gy < NGY - 1, 1.0, 0.0)
    left_ok = jnp.where(gy > 0, 1.0, 0.0)
    ring = jnp.where(ringlane < D, right_ok, jnp.where(ringlane >= L - D, left_ok, 0.0))
    top_ok = jnp.where(gz > 0, 1.0, 0.0)
    bottom_ok = jnp.where(gz < NGZ - 1, 1.0, 0.0)

    def weights():
        out = []
        for start, size in CHUNKS:
            scale = 1.0 / 6.0
            if start == 0:
                scale = scale * top_ok
            if start + size == Z:
                scale = scale * bottom_ok
            out.append((scale, ring * scale))
        return out

    def outside_x(pp):
        for ok, x in ((gx > 0, D), (gx < NGX - 1, D + CX + 1)):

            @pl.when(jnp.logical_not(ok))
            def _():
                for ab in range(2):
                    PR[pp, ab, x, 8 : 8 + Z, :] = jnp.zeros((Z, L), F32)

    def beside(a, b):
        both = jnp.concatenate([a, b], axis=-1).reshape(-1, 2 * L)
        top = both.astype(BF16)
        rest = (both - top.astype(F32)).astype(BF16)
        total = jnp.dot(top, RING[...], preferred_element_type=F32)
        total = total + jnp.dot(rest, RING[...], preferred_element_type=F32)
        return total[:, :L].reshape(a.shape), total[:, L:].reshape(a.shape)

    def ring_sides(a, b):
        axis, lane_c = a.ndim - 1, lanes(a.shape)
        am, bm = pltpu.roll(a, 1, axis), pltpu.roll(b, 1, axis)
        ap, bp = pltpu.roll(a, L - 1, axis), pltpu.roll(b, L - 1, axis)
        first, last = lane_c == 0, lane_c == L - 1
        return (
            (jnp.where(first, bm, am), jnp.where(last, bp, ap)),
            (jnp.where(first, am, bm), jnp.where(last, ap, bp)),
        )

    def sweeps(step, f_copies):
        for copy in f_copies:
            copy.wait()

        unpack(fyr, 0, BF, 1)
        scales = weights()

        @pl.loop(0, X, unroll=4)
        def _(x):
            plus = jnp.where(inside(x + 1), -0.2, 0.0)
            minus = jnp.where(inside(x - 1), -0.2, 0.0)
            for (start, size), (ca, cb) in zip(CHUNKS, scales):
                at = pl.ds(start, size)
                to = pl.ds(start + 8, size)
                fa = plus * F[0, x + 2, at, :] - minus * F[0, x, at, :]
                fb = plus * BF[x + 2, at, :] - minus * BF[x, at, :]
                S[0, x, at, :] = GS[step, 1, x, at, :] + fa
                S[1, x, at, :] = BGS[1, x, at, :] + fb
                PR[0, 0, x + 1, to, :] = (GS[step, 0, x, at, :] - fa) * ca
                PR[0, 1, x + 1, to, :] = (BGS[0, x, at, :] - fb) * cb

        outside_x(0)
        for k in range(2, SWEEPS + 1):
            src, dst = k % 2, (k + 1) % 2
            wide = -(-(CX + 2 * (SWEEPS + 1 - k)) // BLOCK) * BLOCK
            begin = (X - wide) // 2

            @pl.loop(0, wide // BLOCK, unroll=True)
            def _(block):
                x = begin + block * BLOCK
                mid, back, ahead = pl.ds(x + 1, BLOCK), pl.ds(x, BLOCK), pl.ds(x + 2, BLOCK)
                along = beside(PR[src, 0, mid, 8 : 8 + Z, :], PR[src, 1, mid, 8 : 8 + Z, :])
                for (start, size), (ca, cb) in zip(CHUNKS, scales):
                    at = pl.ds(start + 8, size)
                    up = pl.ds(start + 7, size)
                    down = pl.ds(start + 9, size)
                    for ab, scale in ((0, ca), (1, cb)):
                        total = PR[src, ab, back, at, :] + PR[src, ab, ahead, at, :]
                        total = total + PR[src, ab, mid, up, :] + PR[src, ab, mid, down, :]
                        total = total - S[ab, pl.ds(x, BLOCK), pl.ds(start, size), :]
                        total = total + along[ab][:, start : start + size]
                        PR[dst, ab, mid, at, :] = total * scale

            outside_x(dst)

        at = pl.ds(D + 8, CZ)
        last = (SWEEPS + 1) % 2

        @pl.loop(0, CX, unroll=4)
        def _(x):
            deep = D + x + 1
            (left, right), _ = ring_sides(PR[last, 0, deep, at, :], PR[last, 1, deep, at, :])
            back, ahead = PR[last, 0, deep - 1, at, :], PR[last, 0, deep + 1, at, :]
            up = PR[last, 0, deep, pl.ds(D + 7, CZ), :]
            down = PR[last, 0, deep, pl.ds(D + 9, CZ), :]
            force = F[0, D + 1 + x, own_z, :]
            W[0, 1 + x, own_z, :] = ST[0, 1 + x, own_z, :] - 0.4 * force - 0.5 * (ahead - back)
            W[1, 1 + x, own_z, :] = ST[1, 1 + x, own_z, :] - 0.5 * (right - left)
            W[2, 1 + x, own_z, :] = ST[2, 1 + x, own_z, :] - 0.5 * (down - up)
            if step == 0:
                R[x] = back + ahead + up + down + left + right

    def unpack_sources(step, copies):
        for copy in copies:
            copy.wait()
        for field in range(2):
            unpack(gyr.at[step], field, BGS.at[field], 0)

    row_all = 2 * (NGY - 1)

    def row_second(h):
        for r in range(1, NGY):
            row_first(r, h).wait()

        @pl.loop(0, hx)
        def _(d):
            notes = R1[0, h, pl.ds(hx * CAP + d, 1), :]
            for k in range(NGY):
                at = pl.ds(pl.multiple_of(d * CAP, CAP), CAP)
                S2[h * hx + d, k * CAP : (k + 1) * CAP, :] = R1[k, h, at, :]
                if k:
                    more = R1[k, h, pl.ds(hx * CAP + d, 1), :]
                    notes = jnp.where(lanes((1, L)) // 32 == k, pltpu.roll(more, 32 * k, 1), notes)
            S2[h * hx + d, NGY * CAP : NGY * CAP + 1, :] = notes

        @pl.loop(h * hx, (h + 1) * hx)
        def _(peer):
            @pl.when(peer != gx)
            def _():
                slot = lax.rem(peer - gx + NGX, NGX) - 1
                remote(
                    S2.at[peer],
                    R2.at[slot],
                    row_send.at[row_all],
                    row_recv.at[row_all],
                    (peer, gy, gz),
                ).start()

        if h == 1:
            R2[NGX - 1] = S2[gx]

    def row_last():
        whole = R2.at[pl.ds(0, NGX - 1)]
        one_wait(whole, whole, row_send.at[row_all], row_recv.at[row_all], line_peer(1))
        which = lanes((CAP, L)) - rows_of((CAP, L))

        @pl.loop(0, NGX, unroll=4)
        def _(g):
            for k in range(NGY):
                row = R2[g, NGY * CAP : NGY * CAP + 1, :]
                base = 32 * k
                coarse = jnp.where(which == base, 32.0 * row, 0.0)
                told_line = jnp.where(which == base + 8, row, coarse)
                told_turbine = jnp.where(which == base + 16, row, 0.0)
                at = pl.ds(pl.multiple_of((g * NGY + k) * CAP, CAP), CAP)
                LC[at, :] = jnp.broadcast_to(
                    jnp.sum(told_line, axis=1, keepdims=True), (CAP, L)
                )
                TC[at, :] = jnp.broadcast_to(
                    jnp.sum(told_turbine, axis=1, keepdims=True), (CAP, L)
                )

        wide = min(L, slots)
        same = rows_of((wide, wide)) == lanes((wide, wide))
        for c in range(slots // wide):
            turned = jnp.where(same, LC[c * wide : (c + 1) * wide, :wide], 0.0)
            named = jnp.sum(turned, axis=0, keepdims=True).astype(jnp.int32)

            @pl.loop(0, CX)
            def _(x):
                at = pl.ds(pl.multiple_of(x * CZ, CZ), CZ)
                hit = rows_of((CZ, wide)) + x * CZ == named
                O[at, c * wide : (c + 1) * wide] = hit.astype(F32).astype(BF16)

    def constants():
        zero_pad = jnp.zeros((8, L), F32)
        for pp in range(2):
            for ab in range(2):

                @pl.loop(0, X + 2, unroll=X + 2)
                def _(x):
                    PR[pp, ab, x, 0:8, :] = zero_pad
                    PR[pp, ab, x, Z + 8 : Z + 16, :] = zero_pad

                PR[pp, ab, 0, :, :] = jnp.zeros((Z + 16, L), F32)
                PR[pp, ab, X + 1, :, :] = jnp.zeros((Z + 16, L), F32)

        BF[0, :, :] = jnp.zeros((Z, L), F32)
        BF[X + 1, :, :] = jnp.zeros((Z, L), F32)
        step_apart = lax.rem(rows_of((2 * L, 2 * L)) - lanes((2 * L, 2 * L)) + 2 * L, 2 * L)
        RING[...] = ((step_apart == 1) | (step_apart == 2 * L - 1)).astype(F32).astype(BF16)

    for step in range(STEPS):
        faces = send_faces(step)
        inflow_first(step)
        if step == 0:
            constants()
            row_second(0)
        wait_faces(step, faces)
        if step == 0:
            row_second(1)
        inflow_second(step)
        stars = star_faces(step)
        sources(step, stars)
        deep = deep_copies(GS.at[step], D, gys, gyr.at[step], gs_send.at[step], gs_recv.at[step])
        for copy in deep:
            copy.start()
        if step == 0:
            row_last()
        f_copies = forces(step)
        unpack_sources(step, deep)
        sweeps(step, f_copies)

    last = (SWEEPS + 1) % 2
    outs = [
        pltpu.make_async_copy(W.at[pl.ds(0, 3), pl.ds(1, CX), own_z, :], vout, in_sem.at[0]),
        pltpu.make_async_copy(
            PR.at[last, 0, pl.ds(D + 1, CX), pl.ds(D + 8, CZ), :], pout, in_sem.at[1]
        ),
    ]
    for out in outs:
        out.start()
    for out in outs:
        out.wait()


def deliver(vel, prs, vout, pout, held, load_sem, store_sem):
    half = prs.shape[0] // 2
    loads, stores = [], []
    for k in range(8):
        at = pl.ds(k % 2 * half, half)
        source, target = (vel.at[k // 2, at], vout.at[k // 2, at])
        if k >= 6:
            source, target = prs.at[at], pout.at[at]
        loads.append(pltpu.make_async_copy(source, held.at[k], load_sem.at[k]))
        stores.append(pltpu.make_async_copy(held.at[k], target, store_sem.at[k]))
    for load in loads:
        load.start()
    for load, store in zip(loads, stores):
        load.wait()
        store.start()
    for store in stores:
        store.wait()


def body(
    shape,
    velocity,
    pressure,
    kern,
    owners,
    lines,
    point_turbine,
    row_counts,
    thrust,
    inflow_x,
    inflow_y,
):
    ngx, ngy, ngz = shape
    cx, cz = velocity.shape[1:3]
    z, x, ng = cz + 2 * D, cx + 2 * D, cx // 8
    rows = kern.shape[0]
    slots = ngx * ngy * CAP
    turbines = thrust.shape[0]
    any_spec = pl.BlockSpec(memory_space=pl.ANY)
    vm = pltpu.VMEM
    dma = pltpu.SemaphoreType.DMA
    i32 = jnp.int32
    scratch = [
        vm((rows, L), F32),
        vm((1, rows), i32),
        vm((1, rows), i32),
        vm((1, rows), i32),
        vm((1, 1), i32),
        vm((1, turbines), F32),
        vm((1, turbines), i32),
        vm((1, turbines), i32),
        vm((4, cx + 2, z, L), F32),
        vm((cz, L), F32),
        vm((2, cz, L), F32),
        vm((2, 4 * cx, L), F32),
        vm((2, 4 * cx, L), F32),
        vm((cz, L), F32),
        vm((3, cx + 2, z, L), F32),
        vm((cz, L), F32),
        vm((2, cz, L), F32),
        vm((2, cx, L), F32),
        vm((2, cx, L), F32),
        vm((cz, L), F32),
        vm((cx, cz, L), F32),
        vm((STEPS, 2, x, z, L), F32),
        vm((2, ng, cz, L), F32),
        vm((STEPS, 2, 2, ng + 2, z, L), F32),
        vm((2, x, z, L), F32),
        vm((1, x + 2, z, L), F32),
        vm((1, ng, cz, L), F32),
        vm((2, 1, ng + 2, z, L), F32),
        vm((x + 2, z, L), F32),
        vm((2, x, z, L), F32),
        vm((2, 2, x + 2, z + 16, L), F32),
        vm((ngy, 2, ngx // 2 * (CAP + 1), L), F32),
        vm((ngy, 2, ngx // 2 * (CAP + 1), L), F32),
        vm((ngx, ngy * CAP + 1, L), F32),
        vm((ngx, ngy * CAP + 1, L), F32),
        vm((slots, L), F32),
        vm((slots, L), F32),
        vm((cx * cz, slots), BF16),
        vm((slots, 2 * L), BF16),
        vm((3, 8, L), F32),
        vm((2 * L, 2 * L), BF16),
        vm((STEPS, 8, L), F32),
        vm((STEPS, ngy * ngz - 1, 8, L), F32),
        vm((STEPS, 8, L), F32),
        vm((STEPS, ngx - 1, 8, L), F32),
        dma((10,)),
        dma((6,)),
        dma((6,)),
        dma((6,)),
        dma((6,)),
        dma((STEPS, 26)),
        dma((STEPS, 26)),
        dma((26,)),
        dma((26,)),
        dma((2 * ngy - 1,)),
        dma((2 * ngy - 1,)),
        dma((2 * STEPS,)),
        dma((2 * STEPS,)),
    ]
    ahead = pl.pallas_call(
        functools.partial(kernel, (ngx, ngy, ngz, cx, cz)),
        out_shape=(
            jax.ShapeDtypeStruct(velocity.shape, F32),
            jax.ShapeDtypeStruct(pressure.shape, F32),
        ),
        in_specs=[pl.BlockSpec(memory_space=pltpu.HBM)] * 10,
        out_specs=(any_spec, any_spec),
        scratch_shapes=scratch,
        compiler_params=pltpu.CompilerParams(
            collective_id=0, has_side_effects=True, vmem_limit_bytes=56 * 1024 * 1024
        ),
    )(
        velocity,
        pressure,
        kern,
        owners.reshape(1, rows),
        lines.reshape(1, rows),
        point_turbine.reshape(1, rows),
        row_counts.reshape(1, 1),
        thrust.reshape(1, turbines),
        inflow_x.reshape(1, turbines),
        inflow_y.reshape(1, turbines),
    )
    return pl.pallas_call(
        deliver,
        out_shape=(
            jax.ShapeDtypeStruct(velocity.shape, F32),
            jax.ShapeDtypeStruct(pressure.shape, F32),
        ),
        in_specs=[any_spec] * 2,
        out_specs=(any_spec, any_spec),
        scratch_shapes=[vm((8, cx // 2, cz, L), F32), dma((8,)), dma((8,))],
        compiler_params=pltpu.CompilerParams(vmem_limit_bytes=60 * 1024 * 1024),
    )(*ahead)


def solution(mesh):
    placed = (
        P(None, "gx", "gz", "gy"),
        P("gx", "gz", "gy"),
        P(("gx", "gy", "gz"), None),
        P(("gx", "gy", "gz"), None),
        P(("gx", "gy", "gz")),
        P(("gx", "gy", "gz")),
        P("gx", "gy", "gz"),
        P(),
        P(),
        P(),
    )
    shape = (mesh.shape["gx"], mesh.shape["gy"], mesh.shape["gz"])
    return jax.shard_map(
        functools.partial(body, shape),
        mesh=mesh,
        in_specs=placed,
        out_specs=(P(None, "gx", "gz", "gy"), P("gx", "gz", "gy")),
        check_vma=False,
    )
```

```python
import functools

import jax
import jax.numpy as jnp
from jax import lax
from jax.experimental import pallas as pl
from jax.experimental.pallas import tpu as pltpu
from jax.sharding import PartitionSpec as P

BAND = 32
STEPS = 2
SWEEPS = 8
CAP = 8
L = 128
D = 8
BLOCK = 4
MESH = pl.DeviceIdType.MESH
CHUNKS = ((0, 8), (8, 16), (24, 16), (40, 16), (56, 8))
F32 = jnp.float32
BF16 = jnp.bfloat16
DIRS = tuple(
    sorted(
        (
            (dx, dy, dz)
            for dx in (-1, 0, 1)
            for dy in (-1, 0, 1)
            for dz in (-1, 0, 1)
            if (dx, dy, dz) != (0, 0, 0)
        ),
        key=lambda d: (abs(d[1]), abs(d[2]), -abs(d[0])),
    )
)


def lanes(shape):
    return lax.broadcasted_iota(jnp.int32, shape, len(shape) - 1)


def rows_of(shape):
    return lax.broadcasted_iota(jnp.int32, shape, len(shape) - 2)


def pieces(x):
    hi = x.astype(BF16)
    rest = x - hi.astype(F32)
    mid = rest.astype(BF16)
    return hi, mid, (rest - mid.astype(F32)).astype(BF16)


def kernel(
    sizes,
    vel,
    prs,
    kern_h,
    own_h,
    line_h,
    turb_h,
    cnt_h,
    thrust_h,
    infx_h,
    infy_h,
    vout,
    pout,
    kern,
    own_r,
    line_r,
    turb_r,
    cnt,
    thrust,
    infx,
    infy,
    W,
    wys,
    wyr,
    wzs,
    wzr,
    E,
    ST,
    sys_,
    syr,
    szs,
    szr,
    E2,
    R,
    GS,
    gys,
    gyr,
    BGS,
    F,
    fys,
    fyr,
    BF,
    S,
    PR,
    S1,
    R1,
    S2,
    R2,
    LC,
    TC,
    O,
    KC,
    TB,
    RING,
    u1s,
    u1r,
    u2s,
    u2r,
    in_sem,
    face_send,
    face_recv,
    star_send,
    star_recv,
    gs_send,
    gs_recv,
    f_send,
    f_recv,
    row_send,
    row_recv,
    u_send,
    u_recv,
):
    NGX, NGY, NGZ, CX, CZ = sizes
    Z = CZ + 2 * D
    X = CX + 2 * D
    NG = CX // 8
    T = thrust.shape[1]
    rows = kern.shape[0]
    peers = NGX * NGY
    slots = peers * CAP
    plane = NGY * NGZ
    gx = lax.axis_index("gx")
    gy = lax.axis_index("gy")
    gz = lax.axis_index("gz")
    own_z = pl.ds(D, CZ)

    def near(dx, dy, dz):
        return (
            lax.rem(gx + dx + NGX, NGX),
            lax.rem(gy + dy + NGY, NGY),
            lax.rem(gz + dz + NGZ, NGZ),
        )

    def plane_peer(r):
        spot = lax.rem(gy * NGZ + gz + r, plane)
        return (gx, spot // NGZ, lax.rem(spot, NGZ))

    def line_peer(r):
        return (lax.rem(gx + r, NGX), gy, gz)

    def remote(src, dst, send, recv, device):
        return pltpu.make_async_remote_copy(
            src_ref=src,
            dst_ref=dst,
            send_sem=send,
            recv_sem=recv,
            device_id=device,
            device_id_type=MESH,
        )

    loads = [
        pltpu.make_async_copy(vel, W.at[pl.ds(0, 3), pl.ds(1, CX), own_z, :], in_sem.at[0]),
        pltpu.make_async_copy(prs, W.at[3, pl.ds(1, CX), own_z, :], in_sem.at[1]),
    ]
    small = [
        pltpu.make_async_copy(source, here, in_sem.at[2 + i])
        for i, (source, here) in enumerate(
            (
                (own_h, own_r),
                (line_h, line_r),
                (turb_h, turb_r),
                (cnt_h, cnt),
                (kern_h, kern),
                (thrust_h, thrust),
                (infx_h, infx),
                (infy_h, infy),
            )
        )
    ]
    for load in small + loads:
        load.start()
    barrier = pltpu.get_barrier_semaphore()

    @pl.loop(1, plane)
    def _(r):
        pl.semaphore_signal(barrier, inc=1, device_id=plane_peer(r), device_id_type=MESH)

    @pl.loop(1, NGX)
    def _(r):
        pl.semaphore_signal(barrier, inc=1, device_id=line_peer(r), device_id_type=MESH)

    greeted = plane - 1 + NGX - 1
    for d in DIRS:
        if d[0] and (d[1] or d[2]):
            pl.semaphore_signal(barrier, inc=1, device_id=near(*d), device_id_type=MESH)
            greeted += 1

    for load in small:
        load.wait()
    owner = own_r[...]
    live = lanes((1, rows)) < cnt[...]
    spot = jnp.where(live, (owner % NGY) * NGX + owner // NGY, -1)
    land = (rows_of((peers, rows)) == spot).astype(F32)
    before = (rows_of((rows, rows)) < lanes((rows, rows))).astype(BF16)
    earlier = jnp.dot(land.astype(BF16), before, preferred_element_type=F32)
    rank = jnp.sum(land * earlier, axis=0, keepdims=True).astype(jnp.int32)
    slot = jnp.where(live, spot * CAP + rank, -1)
    place = (rows_of((slots, rows)) == slot).astype(BF16)
    hi, mid, lo = pieces(kern[...])
    both = jnp.dot(place, jnp.concatenate([hi, mid], axis=1), preferred_element_type=F32)
    sorted_rows = both[:, :L] + both[:, L:]
    sorted_rows = sorted_rows + jnp.dot(place, lo, preferred_element_type=F32)
    kind = rows_of((L, rows))
    line = line_r[...]
    told = jnp.where(kind < 8, line // 32, jnp.where(kind < 16, line % 32, turb_r[...]))
    told = jnp.where((kind % 8 == rank) & (kind < 24), told, 0).astype(F32).astype(BF16)
    meta = lax.dot_general(
        land.astype(BF16), told, (((1,), (1,)), ((), ())), preferred_element_type=F32
    )
    hx = NGX // 2
    for k in range(NGY):
        for h in range(2):
            first = k * NGX + h * hx
            S1[k, h, : hx * CAP, :] = sorted_rows[first * CAP : (first + hx) * CAP]
            S1[k, h, hx * CAP :, :] = meta[first : first + hx]
    TB[...] = jnp.zeros_like(TB)
    TB[0, 0:1, :T] = infx[...].astype(F32)
    TB[1, 0:1, :T] = infy[...].astype(F32)
    TB[2, 0:1, :T] = thrust[...]
    for load in loads:
        load.wait()
    pl.semaphore_wait(barrier, greeted)

    def row_first(r, h):
        peer = lax.rem(gy + r, NGY)
        i = 2 * (r - 1) + h
        return remote(
            S1.at[peer, h], R1.at[r - 1, h], row_send.at[i], row_recv.at[i], (gx, peer, gz)
        )

    for h in range(2):
        for r in range(1, NGY):
            row_first(r, h).start()
    R1[NGY - 1] = S1[gy]

    lane = lanes((CZ, L))

    def face_copies(step):
        nc = 4 if step == 0 else 3
        comps = pl.ds(0, nc)
        many = pl.ds(0, nc * CX)
        return [
            remote(
                W.at[comps, pl.ds(CX, 1), own_z, :],
                W.at[comps, pl.ds(0, 1), own_z, :],
                face_send.at[0],
                face_recv.at[0],
                near(1, 0, 0),
            ),
            remote(
                W.at[comps, pl.ds(1, 1), own_z, :],
                W.at[comps, pl.ds(CX + 1, 1), own_z, :],
                face_send.at[1],
                face_recv.at[1],
                near(-1, 0, 0),
            ),
            remote(wys, wyr.at[0], face_send.at[2], face_recv.at[2], near(0, 1, 0)),
            remote(wys, wyr.at[1], face_send.at[3], face_recv.at[3], near(0, -1, 0)),
            remote(
                wzs.at[1, many], wzr.at[0, many], face_send.at[4], face_recv.at[4], near(0, 0, 1)
            ),
            remote(
                wzs.at[0, many], wzr.at[1, many], face_send.at[5], face_recv.at[5], near(0, 0, -1)
            ),
        ]

    def turn(cells, by):
        return pltpu.roll(cells, by % L, 1) if by % L else cells

    def edge_lanes(q):
        return (lane == 2 * q) | (lane == (2 * q + L - 1) % L)

    def send_faces(step):
        nc = 4 if step == 0 else 3
        copies = face_copies(step)
        copies[0].start()
        copies[1].start()
        for c in range(nc):
            wzs[0, c * CX : (c + 1) * CX, :] = W[c, 1 : CX + 1, D, :]
            wzs[1, c * CX : (c + 1) * CX, :] = W[c, 1 : CX + 1, D + CZ - 1, :]
        copies[4].start()
        copies[5].start()
        packed = jnp.zeros((CZ, L), F32)
        for c in range(nc):

            for x in range(CX):
                q = c * CX + x
                turned = pltpu.roll(W[c, 1 + x, own_z, :], 2 * q, 1) if q else W[c, 1, own_z, :]
                packed = jnp.where(edge_lanes(q), turned, packed)
        wys[...] = packed
        copies[2].start()
        copies[3].start()
        return copies

    def merged(received):
        right = jnp.where(gy < NGY - 1, received[1], 0.0)
        left = jnp.where(gy > 0, received[0], 0.0)
        return jnp.where(lane % 2 == 0, right, pltpu.roll(left, 2, 1))

    def wait_faces(step, copies):
        nc = 4 if step == 0 else 3
        for copy in copies:
            copy.wait()
        E[...] = merged(wyr)
        for c in range(nc):
            W[c, 0, own_z, :] = jnp.where(gx > 0, W[c, 0, own_z, :], 0.0)
            W[c, CX + 1, own_z, :] = jnp.where(gx < NGX - 1, W[c, CX + 1, own_z, :], 0.0)
            above = jnp.where(gz > 0, wzr[0, c * CX : (c + 1) * CX, :], 0.0)
            below = jnp.where(gz < NGZ - 1, wzr[1, c * CX : (c + 1) * CX, :], 0.0)
            W[c, 1 : CX + 1, D - 1, :] = above
            W[c, 1 : CX + 1, D + CZ, :] = below

    def sides(cells, edge):
        left = jnp.where(lane == 0, edge, pltpu.roll(cells, 1, 1))
        right = jnp.where(lane == L - 1, edge, pltpu.roll(cells, L - 1, 1))
        return left, right

    def edge_of(ref, q):
        return pltpu.roll(ref[...], (2 * L - 1 - 2 * q) % L, 1)

    def star_faces(step):
        nc = 4 if step == 0 else 3
        for c in range(nc):

            @pl.loop(0, CX, unroll=8)
            def _(x):
                cells = W[c, 1 + x, own_z, :]
                left, right = sides(cells, edge_of(E, c * CX + x))
                total = W[c, x, own_z, :] + W[c, x + 2, own_z, :]
                total = total + W[c, 1 + x, pl.ds(D - 1, CZ), :] + W[c, 1 + x, pl.ds(D + 1, CZ), :]
                total = total + left + right
                if c < 3:
                    ST[c, 1 + x, own_z, :] = 0.88 * cells + 0.02 * total
                else:
                    R[x] = total

        copies = [
            remote(
                ST.at[0, CX, own_z, :],
                ST.at[0, 0, own_z, :],
                star_send.at[0],
                star_recv.at[0],
                near(1, 0, 0),
            ),
            remote(
                ST.at[0, 1, own_z, :],
                ST.at[0, CX + 1, own_z, :],
                star_send.at[1],
                star_recv.at[1],
                near(-1, 0, 0),
            ),
            remote(sys_, syr.at[0], star_send.at[2], star_recv.at[2], near(0, 1, 0)),
            remote(sys_, syr.at[1], star_send.at[3], star_recv.at[3], near(0, -1, 0)),
            remote(szs.at[1], szr.at[0], star_send.at[4], star_recv.at[4], near(0, 0, 1)),
            remote(szs.at[0], szr.at[1], star_send.at[5], star_recv.at[5], near(0, 0, -1)),
        ]
        copies[0].start()
        copies[1].start()
        szs[0] = ST[2, 1 : CX + 1, D, :]
        szs[1] = ST[2, 1 : CX + 1, D + CZ - 1, :]
        copies[4].start()
        copies[5].start()

        packed = jnp.zeros((CZ, L), F32)
        for x in range(CX):
            turned = pltpu.roll(ST[1, 1 + x, own_z, :], 2 * x, 1) if x else ST[1, 1, own_z, :]
            packed = jnp.where(edge_lanes(x), turned, packed)
        sys_[...] = packed
        copies[2].start()
        copies[3].start()
        return copies

    def around(j):
        return (lane + (8 - 16 * j) % L) % L < 16

    def sources(step, copies):
        for copy in copies:
            copy.wait()
        E2[...] = merged(syr)
        ST[0, 0, own_z, :] = jnp.where(gx > 0, ST[0, 0, own_z, :], 0.0)
        ST[0, CX + 1, own_z, :] = jnp.where(gx < NGX - 1, ST[0, CX + 1, own_z, :], 0.0)
        ST[2, 1 : CX + 1, D - 1, :] = jnp.where(gz > 0, szr[0], 0.0)
        ST[2, 1 : CX + 1, D + CZ, :] = jnp.where(gz < NGZ - 1, szr[1], 0.0)
        for group in range(NG):

            kept = [jnp.zeros((CZ, L), F32), jnp.zeros((CZ, L), F32)]
            for j in range(8):
                x = group * 8 + j
                left, right = sides(ST[1, 1 + x, own_z, :], edge_of(E2, x))
                total = ST[0, x + 2, own_z, :] - ST[0, x, own_z, :] + right - left
                total = total + ST[2, 1 + x, pl.ds(D + 1, CZ), :]
                source = 0.5 * (total - ST[2, 1 + x, pl.ds(D - 1, CZ), :])
                first = R[x] - source
                GS[step, 0, D + x, own_z, :] = first
                GS[step, 1, D + x, own_z, :] = source
                mine = around(j)
                kept[0] = jnp.where(mine, turn(first, 16 * j), kept[0])
                kept[1] = jnp.where(mine, turn(source, 16 * j), kept[1])
            gys[0, group] = kept[0]
            gys[1, group] = kept[1]

    def deep_copies(cells, off, packed, received, send, recv):
        fields = pl.ds(0, packed.shape[0])
        copies = []
        for i, (dx, dy, dz) in enumerate(DIRS):
            if dy == 0:
                zs, zd = {
                    0: (own_z, own_z),
                    -1: (pl.ds(D, D), pl.ds(D + CZ, D)),
                    1: (pl.ds(CZ, D), pl.ds(0, D)),
                }[dz]
                deep = off if dz == 0 else D
                xs, xd = {
                    0: (pl.ds(off, CX), pl.ds(off, CX)),
                    -1: (pl.ds(off, deep), pl.ds(off + CX, deep)),
                    1: (pl.ds(off + CX - deep, deep), pl.ds(off - deep, deep)),
                }[dx]
                src = cells.at[fields, xs, zs, :]
                dst = cells.at[fields, xd, zd, :]
            else:
                zs, zd = {
                    0: (pl.ds(0, CZ), own_z),
                    -1: (pl.ds(0, D), pl.ds(D + CZ, D)),
                    1: (pl.ds(CZ - D, D), pl.ds(0, D)),
                }[dz]
                xs, xd = {
                    0: (pl.ds(0, NG), pl.ds(1, NG)),
                    -1: (pl.ds(0, 1), pl.ds(NG + 1, 1)),
                    1: (pl.ds(NG - 1, 1), pl.ds(0, 1)),
                }[dx]
                src = packed.at[fields, xs, zs, :]
                dst = received.at[0 if dy == 1 else 1, fields, xd, zd, :]
            copies.append(remote(src, dst, send.at[i], recv.at[i], near(dx, dy, dz)))
        return copies

    lane_z = lanes((Z, L))

    def unpack(received, field, target, base):
        @pl.loop(0, NG + 2)
        def _(group):
            both_sides = jnp.where(
                lane_z % 16 < 8, received[1, field, group], received[0, field, group]
            )
            for j in range(8):
                target[base + group * 8 + j] = turn(both_sides, -16 * j)

    def one_wait(whole_src, whole_dst, send, recv, device):
        remote(whole_src, whole_dst, send, recv, device).wait()

    def inflow_first(step):
        column = jnp.sum(W[0, 1 : CX + 1, own_z, :], axis=1)
        y = rows_of((L, L)) + gy * L
        begin = TB[1, 0:1, :].astype(jnp.int32)
        band = ((y >= begin) & (y < begin + BAND)).astype(F32)
        sums = jnp.dot(column, band, precision=lax.Precision.HIGHEST, preferred_element_type=F32)
        x = rows_of((CX, L)) + gx * CX
        picked = jnp.where(x == TB[0, 0:1, :].astype(jnp.int32), sums, 0.0)
        u1s[step] = jnp.broadcast_to(jnp.sum(picked, axis=0, keepdims=True), (8, L))

        @pl.loop(1, plane)
        def _(r):
            remote(
                u1s.at[step],
                u1r.at[step, r - 1],
                u_send.at[2 * step],
                u_recv.at[2 * step],
                plane_peer(r),
            ).start()

    def inflow_second(step):
        whole = u1r.at[step]
        one_wait(whole, whole, u_send.at[2 * step], u_recv.at[2 * step], plane_peer(1))
        u2s[step] = u1s[step] + jnp.sum(u1r[step], axis=0)

        @pl.loop(1, NGX)
        def _(r):
            remote(
                u2s.at[step],
                u2r.at[step, r - 1],
                u_send.at[2 * step + 1],
                u_recv.at[2 * step + 1],
                line_peer(r),
            ).start()

    def magnitudes(step):
        whole = u2r.at[step]
        one_wait(whole, whole, u_send.at[2 * step + 1], u_recv.at[2 * step + 1], line_peer(1))
        total = u2s[step] + jnp.sum(u2r[step], axis=0)
        uref = total[0:1] * (1.0 / (BAND * CZ * NGZ))
        return 0.5 * TB[2, 0:1, :] * uref * jnp.abs(uref)

    def forces(step):
        size = magnitudes(step)

        @pl.loop(0, NGX, unroll=8)
        def _(g):
            at = pl.ds(pl.multiple_of(g * CAP * NGY, CAP * NGY), CAP * NGY)
            hot = jnp.where(TC[at, :] == lanes((CAP * NGY, L)).astype(F32), size, 0.0)
            scaled = R2[g, : CAP * NGY, :] * jnp.sum(hot, axis=1, keepdims=True)
            top = scaled.astype(BF16)
            KC[at, :L] = top
            KC[at, L:] = (scaled - top.astype(F32)).astype(BF16)

        part = CX // 4
        for h in range(4):
            both = jnp.dot(
                O[h * part * CZ : (h + 1) * part * CZ, :], KC[...], preferred_element_type=F32
            )
            force = (both[:, :L] + both[:, L:]).reshape(part, CZ, L)
            F[0, D + 1 + h * part : D + 1 + (h + 1) * part, own_z, :] = force
        for group in range(NG):

            kept = jnp.zeros((CZ, L), F32)
            for j in range(8):
                turned = turn(F[0, D + 1 + group * 8 + j, own_z, :], 16 * j)
                kept = jnp.where(around(j), turned, kept)
            fys[0, group] = kept
        copies = deep_copies(F, D + 1, fys, fyr, f_send, f_recv)
        for copy in copies:
            copy.start()
        return copies

    def inside(x):
        spot_x = gx * CX + x - D
        return (spot_x >= 0) & (spot_x < NGX * CX)

    ringlane = lanes((8, L))[0:1]
    right_ok = jnp.where(gy < NGY - 1, 1.0, 0.0)
    left_ok = jnp.where(gy > 0, 1.0, 0.0)
    ring = jnp.where(ringlane < D, right_ok, jnp.where(ringlane >= L - D, left_ok, 0.0))
    top_ok = jnp.where(gz > 0, 1.0, 0.0)
    bottom_ok = jnp.where(gz < NGZ - 1, 1.0, 0.0)

    def weights():
        out = []
        for start, size in CHUNKS:
            scale = 1.0 / 6.0
            if start == 0:
                scale = scale * top_ok
            if start + size == Z:
                scale = scale * bottom_ok
            out.append((scale, ring * scale))
        return out

    def outside_x(pp):
        for ok, x in ((gx > 0, D), (gx < NGX - 1, D + CX + 1)):

            @pl.when(jnp.logical_not(ok))
            def _():
                for ab in range(2):
                    PR[pp, ab, x, 8 : 8 + Z, :] = jnp.zeros((Z, L), F32)

    def beside(a, b):
        both = jnp.concatenate([a, b], axis=-1).reshape(-1, 2 * L)
        top = both.astype(BF16)
        rest = (both - top.astype(F32)).astype(BF16)
        total = jnp.dot(top, RING[...], preferred_element_type=F32)
        total = total + jnp.dot(rest, RING[...], preferred_element_type=F32)
        return total[:, :L].reshape(a.shape), total[:, L:].reshape(a.shape)

    def ring_sides(a, b):
        axis, lane_c = a.ndim - 1, lanes(a.shape)
        am, bm = pltpu.roll(a, 1, axis), pltpu.roll(b, 1, axis)
        ap, bp = pltpu.roll(a, L - 1, axis), pltpu.roll(b, L - 1, axis)
        first, last = lane_c == 0, lane_c == L - 1
        return (
            (jnp.where(first, bm, am), jnp.where(last, bp, ap)),
            (jnp.where(first, am, bm), jnp.where(last, ap, bp)),
        )

    def sweeps(step, f_copies):
        for copy in f_copies:
            copy.wait()

        unpack(fyr, 0, BF, 1)
        scales = weights()

        @pl.loop(0, X, unroll=8)
        def _(x):
            plus = jnp.where(inside(x + 1), -0.2, 0.0)
            minus = jnp.where(inside(x - 1), -0.2, 0.0)
            for (start, size), (ca, cb) in zip(CHUNKS, scales):
                at = pl.ds(start, size)
                to = pl.ds(start + 8, size)
                fa = plus * F[0, x + 2, at, :] - minus * F[0, x, at, :]
                fb = plus * BF[x + 2, at, :] - minus * BF[x, at, :]
                S[0, x, at, :] = GS[step, 1, x, at, :] + fa
                S[1, x, at, :] = BGS[1, x, at, :] + fb
                PR[0, 0, x + 1, to, :] = (GS[step, 0, x, at, :] - fa) * ca
                PR[0, 1, x + 1, to, :] = (BGS[0, x, at, :] - fb) * cb

        outside_x(0)
        for k in range(2, SWEEPS + 1):
            src, dst = k % 2, (k + 1) % 2
            wide = -(-(CX + 2 * (SWEEPS + 1 - k)) // BLOCK) * BLOCK
            begin = (X - wide) // 2

            @pl.loop(0, wide // BLOCK, unroll=True)
            def _(block):
                x = begin + block * BLOCK
                mid, back, ahead = pl.ds(x + 1, BLOCK), pl.ds(x, BLOCK), pl.ds(x + 2, BLOCK)
                along = beside(PR[src, 0, mid, 8 : 8 + Z, :], PR[src, 1, mid, 8 : 8 + Z, :])
                for (start, size), (ca, cb) in zip(CHUNKS, scales):
                    at = pl.ds(start + 8, size)
                    up = pl.ds(start + 7, size)
                    down = pl.ds(start + 9, size)
                    for ab, scale in ((0, ca), (1, cb)):
                        total = PR[src, ab, back, at, :] + PR[src, ab, ahead, at, :]
                        total = total + PR[src, ab, mid, up, :] + PR[src, ab, mid, down, :]
                        total = total - S[ab, pl.ds(x, BLOCK), pl.ds(start, size), :]
                        total = total + along[ab][:, start : start + size]
                        PR[dst, ab, mid, at, :] = total * scale

            outside_x(dst)

        at = pl.ds(D + 8, CZ)
        last = (SWEEPS + 1) % 2

        @pl.loop(0, CX, unroll=8)
        def _(x):
            deep = D + x + 1
            (left, right), _ = ring_sides(PR[last, 0, deep, at, :], PR[last, 1, deep, at, :])
            back, ahead = PR[last, 0, deep - 1, at, :], PR[last, 0, deep + 1, at, :]
            up = PR[last, 0, deep, pl.ds(D + 7, CZ), :]
            down = PR[last, 0, deep, pl.ds(D + 9, CZ), :]
            force = F[0, D + 1 + x, own_z, :]
            W[0, 1 + x, own_z, :] = ST[0, 1 + x, own_z, :] - 0.4 * force - 0.5 * (ahead - back)
            W[1, 1 + x, own_z, :] = ST[1, 1 + x, own_z, :] - 0.5 * (right - left)
            W[2, 1 + x, own_z, :] = ST[2, 1 + x, own_z, :] - 0.5 * (down - up)
            if step == 0:
                R[x] = back + ahead + up + down + left + right

    def unpack_sources(step, copies):
        for copy in copies:
            copy.wait()
        for field in range(2):
            unpack(gyr.at[step], field, BGS.at[field], 0)

    row_all = 2 * (NGY - 1)

    def row_second(h):
        for r in range(1, NGY):
            row_first(r, h).wait()

        @pl.loop(0, hx)
        def _(d):
            notes = R1[0, h, pl.ds(hx * CAP + d, 1), :]
            for k in range(NGY):
                at = pl.ds(pl.multiple_of(d * CAP, CAP), CAP)
                S2[h * hx + d, k * CAP : (k + 1) * CAP, :] = R1[k, h, at, :]
                if k:
                    more = R1[k, h, pl.ds(hx * CAP + d, 1), :]
                    notes = jnp.where(lanes((1, L)) // 32 == k, pltpu.roll(more, 32 * k, 1), notes)
            S2[h * hx + d, NGY * CAP : NGY * CAP + 1, :] = notes

        @pl.loop(h * hx, (h + 1) * hx)
        def _(peer):
            @pl.when(peer != gx)
            def _():
                slot = lax.rem(peer - gx + NGX, NGX) - 1
                remote(
                    S2.at[peer],
                    R2.at[slot],
                    row_send.at[row_all],
                    row_recv.at[row_all],
                    (peer, gy, gz),
                ).start()

        if h == 1:
            R2[NGX - 1] = S2[gx]

    def row_last():
        whole = R2.at[pl.ds(0, NGX - 1)]
        one_wait(whole, whole, row_send.at[row_all], row_recv.at[row_all], line_peer(1))
        which = lanes((CAP, L)) - rows_of((CAP, L))

        @pl.loop(0, NGX, unroll=8)
        def _(g):
            for k in range(NGY):
                row = R2[g, NGY * CAP : NGY * CAP + 1, :]
                base = 32 * k
                coarse = jnp.where(which == base, 32.0 * row, 0.0)
                told_line = jnp.where(which == base + 8, row, coarse)
                told_turbine = jnp.where(which == base + 16, row, 0.0)
                at = pl.ds(pl.multiple_of((g * NGY + k) * CAP, CAP), CAP)
                LC[at, :] = jnp.broadcast_to(
                    jnp.sum(told_line, axis=1, keepdims=True), (CAP, L)
                )
                TC[at, :] = jnp.broadcast_to(
                    jnp.sum(told_turbine, axis=1, keepdims=True), (CAP, L)
                )

        wide = min(L, slots)
        same = rows_of((wide, wide)) == lanes((wide, wide))
        for c in range(slots // wide):
            turned = jnp.where(same, LC[c * wide : (c + 1) * wide, :wide], 0.0)
            named = jnp.sum(turned, axis=0, keepdims=True).astype(jnp.int32)

            @pl.loop(0, CX)
            def _(x):
                at = pl.ds(pl.multiple_of(x * CZ, CZ), CZ)
                hit = rows_of((CZ, wide)) + x * CZ == named
                O[at, c * wide : (c + 1) * wide] = hit.astype(F32).astype(BF16)

    def constants():
        zero_pad = jnp.zeros((8, L), F32)
        for pp in range(2):
            for ab in range(2):

                @pl.loop(0, X + 2, unroll=X + 2)
                def _(x):
                    PR[pp, ab, x, 0:8, :] = zero_pad
                    PR[pp, ab, x, Z + 8 : Z + 16, :] = zero_pad

                PR[pp, ab, 0, :, :] = jnp.zeros((Z + 16, L), F32)
                PR[pp, ab, X + 1, :, :] = jnp.zeros((Z + 16, L), F32)

        BF[0, :, :] = jnp.zeros((Z, L), F32)
        BF[X + 1, :, :] = jnp.zeros((Z, L), F32)
        step_apart = lax.rem(rows_of((2 * L, 2 * L)) - lanes((2 * L, 2 * L)) + 2 * L, 2 * L)
        RING[...] = ((step_apart == 1) | (step_apart == 2 * L - 1)).astype(F32).astype(BF16)

    for step in range(STEPS):
        faces = send_faces(step)
        inflow_first(step)
        if step == 0:
            constants()
            row_second(0)
        wait_faces(step, faces)
        if step == 0:
            row_second(1)
        stars = star_faces(step)
        inflow_second(step)
        sources(step, stars)
        deep = deep_copies(GS.at[step], D, gys, gyr.at[step], gs_send.at[step], gs_recv.at[step])
        for copy in deep:
            copy.start()
        if step == 0:
            row_last()
        f_copies = forces(step)
        unpack_sources(step, deep)
        sweeps(step, f_copies)

    last = (SWEEPS + 1) % 2
    outs = [
        pltpu.make_async_copy(W.at[pl.ds(0, 3), pl.ds(1, CX), own_z, :], vout, in_sem.at[0]),
        pltpu.make_async_copy(
            PR.at[last, 0, pl.ds(D + 1, CX), pl.ds(D + 8, CZ), :], pout, in_sem.at[1]
        ),
    ]
    for out in outs:
        out.start()
    for out in outs:
        out.wait()


def deliver(vel, prs, vout, pout, held, load_sem, store_sem):
    half = prs.shape[0] // 2
    loads, stores = [], []
    for k in range(8):
        at = pl.ds(k % 2 * half, half)
        source, target = (vel.at[k // 2, at], vout.at[k // 2, at])
        if k >= 6:
            source, target = prs.at[at], pout.at[at]
        loads.append(pltpu.make_async_copy(source, held.at[k], load_sem.at[k]))
        stores.append(pltpu.make_async_copy(held.at[k], target, store_sem.at[k]))
    for load in loads:
        load.start()
    for load, store in zip(loads, stores):
        load.wait()
        store.start()
    for store in stores:
        store.wait()


def body(
    shape,
    velocity,
    pressure,
    kern,
    owners,
    lines,
    point_turbine,
    row_counts,
    thrust,
    inflow_x,
    inflow_y,
):
    ngx, ngy, ngz = shape
    cx, cz = velocity.shape[1:3]
    z, x, ng = cz + 2 * D, cx + 2 * D, cx // 8
    rows = kern.shape[0]
    slots = ngx * ngy * CAP
    turbines = thrust.shape[0]
    any_spec = pl.BlockSpec(memory_space=pl.ANY)
    vm = pltpu.VMEM
    dma = pltpu.SemaphoreType.DMA
    i32 = jnp.int32
    scratch = [
        vm((rows, L), F32),
        vm((1, rows), i32),
        vm((1, rows), i32),
        vm((1, rows), i32),
        vm((1, 1), i32),
        vm((1, turbines), F32),
        vm((1, turbines), i32),
        vm((1, turbines), i32),
        vm((4, cx + 2, z, L), F32),
        vm((cz, L), F32),
        vm((2, cz, L), F32),
        vm((2, 4 * cx, L), F32),
        vm((2, 4 * cx, L), F32),
        vm((cz, L), F32),
        vm((3, cx + 2, z, L), F32),
        vm((cz, L), F32),
        vm((2, cz, L), F32),
        vm((2, cx, L), F32),
        vm((2, cx, L), F32),
        vm((cz, L), F32),
        vm((cx, cz, L), F32),
        vm((STEPS, 2, x, z, L), F32),
        vm((2, ng, cz, L), F32),
        vm((STEPS, 2, 2, ng + 2, z, L), F32),
        vm((2, x, z, L), F32),
        vm((1, x + 2, z, L), F32),
        vm((1, ng, cz, L), F32),
        vm((2, 1, ng + 2, z, L), F32),
        vm((x + 2, z, L), F32),
        vm((2, x, z, L), F32),
        vm((2, 2, x + 2, z + 16, L), F32),
        vm((ngy, 2, ngx // 2 * (CAP + 1), L), F32),
        vm((ngy, 2, ngx // 2 * (CAP + 1), L), F32),
        vm((ngx, ngy * CAP + 1, L), F32),
        vm((ngx, ngy * CAP + 1, L), F32),
        vm((slots, L), F32),
        vm((slots, L), F32),
        vm((cx * cz, slots), BF16),
        vm((slots, 2 * L), BF16),
        vm((3, 8, L), F32),
        vm((2 * L, 2 * L), BF16),
        vm((STEPS, 8, L), F32),
        vm((STEPS, ngy * ngz - 1, 8, L), F32),
        vm((STEPS, 8, L), F32),
        vm((STEPS, ngx - 1, 8, L), F32),
        dma((10,)),
        dma((6,)),
        dma((6,)),
        dma((6,)),
        dma((6,)),
        dma((STEPS, 26)),
        dma((STEPS, 26)),
        dma((26,)),
        dma((26,)),
        dma((2 * ngy - 1,)),
        dma((2 * ngy - 1,)),
        dma((2 * STEPS,)),
        dma((2 * STEPS,)),
    ]
    ahead = pl.pallas_call(
        functools.partial(kernel, (ngx, ngy, ngz, cx, cz)),
        out_shape=(
            jax.ShapeDtypeStruct(velocity.shape, F32),
            jax.ShapeDtypeStruct(pressure.shape, F32),
        ),
        in_specs=[pl.BlockSpec(memory_space=pltpu.HBM)] * 10,
        out_specs=(any_spec, any_spec),
        scratch_shapes=scratch,
        compiler_params=pltpu.CompilerParams(
            collective_id=0, has_side_effects=True, vmem_limit_bytes=56 * 1024 * 1024
        ),
    )(
        velocity,
        pressure,
        kern,
        owners.reshape(1, rows),
        lines.reshape(1, rows),
        point_turbine.reshape(1, rows),
        row_counts.reshape(1, 1),
        thrust.reshape(1, turbines),
        inflow_x.reshape(1, turbines),
        inflow_y.reshape(1, turbines),
    )
    return pl.pallas_call(
        deliver,
        out_shape=(
            jax.ShapeDtypeStruct(velocity.shape, F32),
            jax.ShapeDtypeStruct(pressure.shape, F32),
        ),
        in_specs=[any_spec] * 2,
        out_specs=(any_spec, any_spec),
        scratch_shapes=[vm((8, cx // 2, cz, L), F32), dma((8,)), dma((8,))],
        compiler_params=pltpu.CompilerParams(vmem_limit_bytes=60 * 1024 * 1024),
    )(*ahead)


def solution(mesh):
    placed = (
        P(None, "gx", "gz", "gy"),
        P("gx", "gz", "gy"),
        P(("gx", "gy", "gz"), None),
        P(("gx", "gy", "gz"), None),
        P(("gx", "gy", "gz")),
        P(("gx", "gy", "gz")),
        P("gx", "gy", "gz"),
        P(),
        P(),
        P(),
    )
    shape = (mesh.shape["gx"], mesh.shape["gy"], mesh.shape["gz"])
    return jax.shard_map(
        functools.partial(body, shape),
        mesh=mesh,
        in_specs=placed,
        out_specs=(P(None, "gx", "gz", "gy"), P("gx", "gz", "gy")),
        check_vma=False,
    )
```
